256 devices in a mesh: sx: 8 (over y, core), sy: 32 (over x, z).
Axes of the slice: x: 4, y: 4, z: 8, core: 2. Of those that a mesh axis runs over, the one named last changes fastest.
Arguments:
- residual: float32 [96, 331776], P(None, ('sx', 'sy')), may hold values from -52 to 52
- ritz_block: float32 [96, 331776], P(None, ('sx', 'sy')), may hold values from -52 to 52
- search_block: float32 [96, 331776], P(None, ('sx', 'sy')), may hold values from -52 to 52
- inverse_factor: float32 [8, 32, 1600, 1600], P('sx', 'sy'), may hold values from -2.5 to 2.5, as said below
- send_rows: int32 [8, 32, 8, 128], P('sx', 'sy'), may hold values from 0 to 1295
- send_count: int32 [8, 32, 8], P('sx', 'sy'), may hold values from 0 to 72, as said below
Outputs:
- precond: float32 [96, 331776], P(None, ('sx', 'sy'))
- gram: float32 [288, 288], replicated
The draws below stay inside these ranges and needn't reach their ends.
Inputs may be any that keep to these rules, and one draw needn't show every extreme that they name: `send_rows`: entries from send_count on are padding, read by nothing. `send_count`: directions 0 to 3 carry 36 to 72 vertices, directions 4 to 7 one to 4; both bounds are reached in every draw; zero exactly where the neighbour lies outside the grid. `inverse_factor`: lower triangular, diagonal from 0.5 to 2.
All inputs are finite; a program needn't handle non-finite values.
Results may differ from the reference program's by a relative error of at most 0.00055.
Values sent between devices are 32-bit elements; how exact they have to be, the bound alone decides.
No kernel may reach another device: no remote copies, remote signals or barrier semaphores. Data moves between devices by JAX's collectives and lax.ppermute only.
A program may use at most 64 MiB of HBM per device.

```python
import math
import jax
import jax.numpy as jnp
from jax import lax

K = 96
SIDE = 36
CORNER = 4
NEIGHBOURS = 8
SLOT = 128
OWNED = 1296
EDGE = 72
EXT = 1600
GRID_X = 8
GRID_Y = 32


def scaled_field(key, base):
    col_key, row_key = jax.random.split(key, 2)
    vertex_total = OWNED * GRID_X * GRID_Y
    col_scale = jnp.exp(jax.random.uniform(col_key, (K, 1), minval=math.log(0.2), maxval=math.log(2.0)))
    row_scale = jnp.exp(jax.random.uniform(row_key, (1, vertex_total), minval=math.log(0.3), maxval=math.log(3.0)))
    device_pos = (jnp.arange(vertex_total) // OWNED).astype(jnp.float32) / max(GRID_X * GRID_Y - 1, 1)
    rising = 0.5 * jnp.exp(math.log(3.0) * device_pos)
    values = base * col_scale * row_scale * rising[None, :]
    return values.astype(jnp.float32)


def draw_residual(key, part):
    key = jax.random.fold_in(key, 11)
    base_key, rest_key = jax.random.split(key)
    shape = (K, OWNED * GRID_X * GRID_Y)
    base = jax.random.truncated_normal(base_key, -5.0, 5.0, shape)
    return scaled_field(rest_key, base)


def draw_ritz_block(key, part):
    key = jax.random.fold_in(key, 17)
    base_key, rest_key = jax.random.split(key)
    shape = (K, OWNED * GRID_X * GRID_Y)
    base = jax.random.truncated_normal(base_key, -5.0, 5.0, shape)
    return scaled_field(rest_key, base)


def draw_search_block(key, part):
    key = jax.random.fold_in(key, 23)
    base_key, rest_key = jax.random.split(key)
    shape = (K, OWNED * GRID_X * GRID_Y)
    base = jax.random.truncated_normal(base_key, -5.0, 5.0, shape)
    return scaled_field(rest_key, base)


def draw_inverse_factor(key, part):
    key = jax.random.fold_in(key, 29)
    diag_key, off_key = jax.random.split(key)
    shape = (GRID_X, GRID_Y, EXT, EXT)
    off_entries = jax.random.truncated_normal(off_key, -5.0, 5.0, shape)
    row_ids = jnp.arange(EXT)[:, None]
    col_ids = jnp.arange(EXT)[None, :]
    below = (col_ids < row_ids).astype(jnp.float32)
    row_scale = 0.5 / jnp.sqrt(jnp.maximum(row_ids, 1).astype(jnp.float32))
    diagonal = jnp.exp(jax.random.uniform(diag_key, (GRID_X, GRID_Y, EXT), minval=math.log(0.5), maxval=math.log(2.0)))
    identity = (col_ids == row_ids).astype(jnp.float32)
    return (off_entries * row_scale * below + diagonal[..., None] * identity).astype(jnp.float32)


def draw_send_count(key, part):
    key = jax.random.fold_in(key, 41)
    edge_key, corner_key, pick_key, other_key = jax.random.split(key, 4)
    edges = jax.random.randint(edge_key, (GRID_X, GRID_Y, 4), SIDE, EDGE + 1)
    corners = jax.random.randint(corner_key, (GRID_X, GRID_Y, 4), 1, CORNER + 1)
    counts = jnp.concatenate([edges, corners], axis=2)
    row_steps = jnp.array([1, -1, 0, 0, 1, 1, -1, -1], dtype=jnp.int32)
    col_steps = jnp.array([0, 0, 1, -1, 1, -1, 1, -1], dtype=jnp.int32)
    target_row = jnp.arange(GRID_X, dtype=jnp.int32)[:, None, None] + row_steps[None, None, :]
    target_col = jnp.arange(GRID_Y, dtype=jnp.int32)[None, :, None] + col_steps[None, None, :]
    inside = (target_row >= 0) & (target_row < GRID_X) & (target_col >= 0) & (target_col < GRID_Y)
    edge_col = jax.random.randint(pick_key, (), 0, GRID_Y)
    corner_col = jax.random.randint(other_key, (), 0, GRID_Y - 1)
    counts = counts.at[0, edge_col, 0].set(EDGE)
    counts = counts.at[0, corner_col, 4].set(CORNER)
    return jnp.where(inside, counts, 0).astype(jnp.int32)


def touch_ends(values, key, smallest, largest):
    index_at = [jax.random.randint(jax.random.fold_in(key, axis), (), 0, length) for axis, length in enumerate(values.shape)]
    longest = values.shape.index(max(values.shape))
    beside = index_at[:longest] + [(index_at[longest] + 1) % values.shape[longest]] + index_at[longest + 1:]
    return values.at[tuple(index_at)].set(smallest).at[tuple(beside)].set(largest)


def setup_inputs(seed: int = 0) -> dict:
    splits = jax.random.split(jax.random.key(seed), 7)
    return {
        "residual": draw_residual(jax.random.fold_in(splits[6], 71), 0),
        "ritz_block": draw_ritz_block(jax.random.fold_in(splits[6], 71), 0),
        "search_block": draw_search_block(jax.random.fold_in(splits[6], 71), 0),
        "inverse_factor": draw_inverse_factor(jax.random.fold_in(splits[6], 71), 0),
        "send_rows": touch_ends(jax.random.randint(splits[4], (GRID_X, GRID_Y, NEIGHBOURS, SLOT), 0, OWNED), jax.random.fold_in(splits[4], 1), 0, OWNED - 1).astype(jnp.int32),
        "send_count": draw_send_count(jax.random.fold_in(splits[6], 71), 0),
    }


direction_table = ((1, 0), (-1, 0), (0, 1), (0, -1), (1, 1), (1, -1), (-1, 1), (-1, -1))


def slab_size(slot_index):
    if slot_index < 4:
        return EDGE
    return CORNER


def slab_start(slot_index):
    if slot_index < 4:
        return OWNED + slot_index * EDGE
    return OWNED + 4 * EDGE + (slot_index - 4) * CORNER


def shift_grid(values, row_step, col_step):
    grid_rows, grid_cols = values.shape[0], values.shape[1]
    padded = jnp.pad(values, ((1, 1), (1, 1)) + ((0, 0),) * (values.ndim - 2))
    return padded[1 - row_step:1 - row_step + grid_rows, 1 - col_step:1 - col_step + grid_cols]


def product(left, right):
    return jnp.dot(left, right, precision=lax.Precision.HIGHEST, preferred_element_type=jnp.float32)


def take_columns(field_block, row_ids):
    return jnp.take(field_block, row_ids, axis=1)


def add_columns(running, row_ids, values):
    return running.at[:, row_ids].add(values)


def reference(residual, ritz_block, search_block, inverse_factor, send_rows, send_count):
    grid_rows, grid_cols = send_count.shape[0], send_count.shape[1]
    owned_block = residual.reshape(K, grid_rows, grid_cols, OWNED).transpose(1, 2, 0, 3)
    slot_ids = jnp.arange(SLOT)
    live_mask = (slot_ids[None, None, None, :] < send_count[..., None]).astype(jnp.float32)
    flat_rows = send_rows.reshape(grid_rows, grid_cols, NEIGHBOURS * SLOT)
    packed = jax.vmap(jax.vmap(take_columns))(owned_block, flat_rows)
    packed = packed.reshape(grid_rows, grid_cols, K, NEIGHBOURS, SLOT) * live_mask[:, :, None, :, :]
    pieces = [owned_block]
    for slot_index in range(NEIGHBOURS):
        row_step, col_step = direction_table[slot_index]
        moved_block = shift_grid(packed[:, :, :, slot_index, :], row_step, col_step)
        pieces.append(moved_block[..., :slab_size(slot_index)])
    extended = jnp.concatenate(pieces, axis=-1)

    def local_solve(pair):
        field_block, factor = pair
        half_solve = product(field_block, factor.T)
        return product(half_solve, factor)

    local_solution = lax.map(local_solve, (extended.reshape(-1, K, EXT), inverse_factor.reshape(-1, EXT, EXT)))
    local_solution = local_solution.reshape(grid_rows, grid_cols, K, EXT)
    update = local_solution[..., :OWNED]
    for slot_index in range(NEIGHBOURS):
        row_step, col_step = direction_table[slot_index]
        start = slab_start(slot_index)
        size_here = slab_size(slot_index)
        returned = shift_grid(local_solution[..., start:start + size_here], -row_step, -col_step)
        returned = jnp.pad(returned, ((0, 0), (0, 0), (0, 0), (0, SLOT - size_here)))
        returned = returned * live_mask[:, :, None, slot_index, :]
        update = jax.vmap(jax.vmap(add_columns))(update, send_rows[:, :, slot_index, :], returned)
    precond = update.transpose(2, 0, 1, 3).reshape(K, -1)
    stacked = jnp.concatenate([ritz_block, precond, search_block], axis=0)
    gram = product(stacked, stacked.T) / stacked.shape[1]
    return precond, gram
```

```python
import jax
import jax.numpy as jnp
from jax import lax
from jax.experimental import pallas as pl
from jax.experimental.pallas import tpu as pltpu
from jax.sharding import PartitionSpec as P

EDGE = 72
LANES = 128
TAIL = 1280
F32 = jnp.float32
BF16 = jnp.bfloat16
VMEM = pl.BlockSpec(memory_space=pltpu.VMEM)
SMEM = pl.BlockSpec(memory_space=pltpu.SMEM)
HBM = pl.BlockSpec(memory_space=pl.ANY)
NN = (((1,), (0,)), ((), ()))
NT = (((1,), (1,)), ((), ()))


def split(value):
    high = value.astype(BF16)
    low = (value - high.astype(F32)).astype(BF16)
    return high, low


def dot(left, right, dims):
    return lax.dot_general(left, right, dims, preferred_element_type=F32)


def dot_pairs(left, right, dims):
    rows = left[0].shape[0]
    both = dot(jnp.concatenate(left, axis=0), right[0], dims)
    return both[:rows] + both[rows:] + dot(left[0], right[1], dims)


def dot_exact(left, right, dims):
    rows = left[0].shape[0]
    both = dot(jnp.concatenate(left, axis=0), right, dims)
    return both[:rows] + both[rows:]


def pick(odd, when_even, when_odd):
    return jnp.where(jnp.full(when_even.shape, odd, jnp.int32) == 0, when_even, when_odd)


def call(kernel, out, in_specs, scratch=(), flops=0, moved=0, name=None):
    return pl.pallas_call(
        kernel,
        out_shape=out,
        in_specs=in_specs,
        out_specs=jax.tree.map(lambda _: VMEM, out),
        scratch_shapes=list(scratch),
        compiler_params=pltpu.CompilerParams(vmem_limit_bytes=40 * 1024 * 1024),
        cost_estimate=pl.CostEstimate(flops=flops, bytes_accessed=moved, transcendentals=0),
        name=name,
    )


def shaped(*shape, dtype=F32):
    return jax.ShapeDtypeStruct(shape, dtype)


def gather_kernel(odd, count, rows, residual, sxa, sxb, sya, syb, hot):
    lane = lax.broadcasted_iota(jnp.int32, (1, LANES), 1)
    table = rows[0, 0]

    def edge(n):
        return jnp.where(lane < count[n], table[n : n + 1], -1)

    def corner(base, n, at):
        moved = pltpu.roll(table, at, 1)[n : n + 1]
        return jnp.where((lane >= at) & (lane < at + count[n]), moved, base)

    down = corner(corner(edge(0), 4, 72), 5, 80)
    up = corner(corner(edge(1), 6, 76), 7, 84)
    right, left = edge(2), edge(3)
    lists = [
        pick(odd[0], down, up),
        pick(odd[0], up, down),
        pick(odd[1], right, left),
        pick(odd[1], left, right),
    ]
    own = residual.shape[1]
    row = lax.broadcasted_iota(jnp.int32, (own, LANES), 0)
    ones = [jnp.where(row == ids, 1.0, 0.0).astype(BF16) for ids in lists]
    onehot = jnp.concatenate(ones, axis=1)
    hot[...] = onehot
    packed = dot_exact(split(residual[...]), onehot, NN)
    for k, out in enumerate((sxa, sxb, sya, syb)):
        out[...] = packed[:, k * LANES : (k + 1) * LANES]


def halo_place():
    col = lax.broadcasted_iota(jnp.int32, (320, 4 * LANES), 0) - 16
    spot = lax.broadcasted_iota(jnp.int32, (320, 4 * LANES), 1)
    lane = spot % LANES
    block = spot // LANES
    source = jnp.where(lane < EDGE, block * EDGE + lane, -99)
    for n, b, at in ((4, 2, 72), (6, 2, 76), (5, 3, 80), (7, 3, 84)):
        inside = (block == b) & (lane >= at) & (lane < at + 4)
        source = jnp.where(inside, 4 * EDGE + (n - 4) * 4 + lane - at, source)
    return jnp.where(col == source, 1.0, 0.0).astype(BF16)


def tail_kernel(residual, factor, part, ph, plo, oh, olo, slab, sem):
    copy = pltpu.make_async_copy(factor.at[0, 0, pl.ds(TAIL, 320), :], slab, sem)
    copy.start()
    place = halo_place()
    field = split(residual[...])
    copy.wait()
    own = residual.shape[1]
    oh[...], olo[...] = split(slab[:, :own])
    part[...] = dot_pairs(field, (oh[...], olo[...]), NT)
    high, low = split(slab[:, TAIL:])
    ph[...] = dot(high, place, NN).astype(BF16)
    plo[...] = dot(low, place, NN).astype(BF16)


def halo_kernel(odd, sxa, sxb, sya, syb, part, ph, plo, half, bxa, bxb, bya, byb):
    xa, xb, ya, yb = sxa[...], sxb[...], sya[...], syb[...]
    arrived = jnp.concatenate(
        [pick(odd[0], xb, xa), pick(odd[0], xa, xb), pick(odd[1], yb, ya), pick(odd[1], ya, yb)], axis=1
    )
    factor = (ph[...], plo[...])
    solved = part[...] + dot_pairs(split(arrived), factor, NT)
    half[...] = solved
    back = dot_pairs(split(solved), factor, NN)
    b = [back[:, k * LANES : (k + 1) * LANES] for k in range(4)]
    bxa[...] = pick(odd[0], b[1], b[0])
    bxb[...] = pick(odd[0], b[0], b[1])
    bya[...] = pick(odd[1], b[3], b[2])
    byb[...] = pick(odd[1], b[2], b[3])


def body_kernel(residual, factor, out, *scratch):
    slabs, sem = scratch[:-1], scratch[-1]
    copies = []
    for k, slab in enumerate(slabs):
        copies.append(
            pltpu.make_async_copy(
                factor.at[0, 0, pl.ds(256 * k, 256), pl.ds(0, 256 * (k + 1))], slab, sem.at[k]
            )
        )
        copies[-1].start()
    high, low = split(residual[:, :TAIL])
    for k, slab in enumerate(slabs):
        width = 256 * (k + 1)
        copies[k].wait()
        block = split(slab[...])
        solved = dot_pairs((high[:, :width], low[:, :width]), block, NT)
        piece = dot_pairs(split(solved), block, NN)
        if k:
            out[:, : width - 256] = out[:, : width - 256] + piece[:, : width - 256]
        out[:, width - 256 : width] = piece[:, width - 256 :]


def local_kernel(base, half, oh, olo, ritz, search, local, early):
    add = dot_pairs(split(half[...]), (oh[...], olo[...]), NN)
    local[:, :TAIL] = base[...] + add[:, :TAIL]
    local[:, TAIL:] = add[:, TAIL:]
    r, s = split(ritz[...]), split(search[...])
    both = (jnp.concatenate([r[0], s[0]], axis=0), jnp.concatenate([r[1], s[1]], axis=0))
    early[:192] = dot_pairs(both, r, NT)
    early[192:] = dot_pairs(s, s, NT)


def gram_kernel(rxa, rxb, rya, ryb, hot, local, ritz, search, precond, late):
    back = jnp.concatenate([rxa[...], rxb[...], rya[...], ryb[...]], axis=1)
    update = local[...] + dot_exact(split(back), hot[...], NT)
    precond[...] = update
    r, p, s = split(ritz[...]), split(update), split(search[...])
    stacked = tuple(jnp.concatenate([r[k], p[k], s[k]], axis=0) for k in range(2))
    late[...] = dot_pairs(stacked, p, NT)


def final_kernel(scale, place, own, one, two, three, out, whole):
    for m, piece in enumerate((own, one, two, three)):
        at = place[0] ^ m
        whole[at] = piece[...] * scale
    def block(core, n):
        rows = [whole[y, core] for y in range(4)]
        return jnp.concatenate(rows, axis=0)[n * 96 : (n + 1) * 96]

    rp, pp, sp = (block(0, n) for n in range(3))
    rr, sr, ss = (block(1, n) for n in range(3))
    out[0:96, :] = jnp.concatenate([rr, rp, sr.T], axis=1)
    out[96:192, :] = jnp.concatenate([rp.T, pp, sp.T], axis=1)
    out[192:288, :] = jnp.concatenate([sr, sp, ss], axis=1)


def swap(block, axis, step):
    return lax.ppermute(block, axis, [(i, i ^ step) for i in range(lax.axis_size(axis))])


def swap_odd(block, axis):
    size = lax.axis_size(axis)
    route = [(i, i + 1) for i in range(1, size - 1, 2)]
    return lax.ppermute(block, axis, route + [(b, a) for a, b in route])


def body(residual, ritz_block, search_block, inverse_factor, send_rows, send_count):
    own = residual.shape[1]
    p, q = lax.axis_index("sx"), lax.axis_index("sy")
    odd = jnp.stack([p % 2, q % 2]).astype(jnp.int32)
    lane = jnp.arange(LANES)[None, :]
    msg = shaped(96, LANES)

    sxa, sxb, sya, syb, hot = call(
        gather_kernel,
        (msg, msg, msg, msg, shaped(own, 4 * LANES, dtype=BF16)),
        [SMEM, SMEM, VMEM, VMEM],
        flops=2 * 192 * 1296 * 512,
        moved=2000000,
        name="gather",
    )(odd, send_count[0, 0], send_rows, residual)

    part, ph, plo, oh, olo = call(
        tail_kernel,
        (
            shaped(96, 320),
            shaped(320, 512, dtype=BF16),
            shaped(320, 512, dtype=BF16),
            shaped(320, own, dtype=BF16),
            shaped(320, own, dtype=BF16),
        ),
        [VMEM, HBM],
        [pltpu.VMEM((320, 1600), F32), pltpu.SemaphoreType.DMA],
        flops=2 * 96 * 1296 * 320 * 3,
        moved=4000000,
        name="tail",
    )(residual, inverse_factor)

    base = call(
        body_kernel,
        shaped(96, TAIL),
        [VMEM, HBM],
        [pltpu.VMEM((256, 256 * (k + 1)), F32) for k in range(5)] + [pltpu.SemaphoreType.DMA((5,))],
        flops=2 * 2 * 96 * 256 * 256 * 15 * 3,
        moved=5000000,
        name="body",
    )(residual, inverse_factor)

    gxa, gxb = swap(sxa, "sx", 1), swap_odd(sxb, "sx")
    relay = jnp.where(lane >= EDGE, gxa + gxb, 0.0)
    gya, gyb = swap(sya + relay, "sy", 1), swap_odd(syb + relay, "sy")

    half, bxa, bxb, bya, byb = call(
        halo_kernel,
        (shaped(96, 320), msg, msg, msg, msg),
        [SMEM] + [VMEM] * 7,
        flops=2 * 2 * 96 * 320 * 512 * 3,
        moved=1000000,
        name="halo",
    )(odd, gxa, gxb, gya, gyb, part, ph, plo)

    rya, ryb = swap(bya, "sy", 1), swap_odd(byb, "sy")
    relay = jnp.where(lane >= EDGE, rya + ryb, 0.0)
    rxa, rxb = swap(bxa + relay, "sx", 1), swap_odd(bxb + relay, "sx")

    local, early = call(
        local_kernel,
        (shaped(96, own), shaped(288, 96)),
        [VMEM] * 6,
        flops=2 * 96 * 1296 * 320 * 3 + 2 * 96 * 288 * 1296 * 3,
        moved=4000000,
        name="local",
    )(base, half, oh, olo, ritz_block, search_block)

    precond, late = call(
        gram_kernel,
        (shaped(96, own), shaped(288, 96)),
        [VMEM] * 8,
        flops=2 * 192 * 1296 * 512 + 2 * 96 * 288 * 1296 * 3,
        moved=4000000,
        name="gram",
    )(rxa, rxb, rya, ryb, hot, local, ritz_block, search_block)

    core, y = p % 2, p // 2
    kept = jnp.where(core == 0, late, early) + swap(jnp.where(core == 0, early, late), "sx", 1)
    quarters = kept.reshape(4, 72, 96)

    def quarter(m):
        return lax.dynamic_index_in_dim(quarters, y ^ m, 0, keepdims=False)

    def summed(value, axis, steps):
        total = value
        for step in steps:
            total = total + swap(value, axis, step)
        return total

    total = quarter(0)
    for m in (2, 1, 3):
        total = total + swap(quarter(m), "sx", 2 * m)
    total = summed(total, "sy", (16, 8, 24))
    total = summed(total, "sy", (3, 2, 1))
    total = summed(total, "sy", (6,))
    other = swap(total, "sx", 1)
    mine = jnp.where(core == 0, jnp.stack([total, other]), jnp.stack([other, total]))
    two, one, three = (swap(mine, "sx", 2 * m) for m in (2, 1, 3))

    vertex_total = own * lax.axis_size("sx") * lax.axis_size("sy")

    def finish(place, *refs):
        final_kernel(1.0 / vertex_total, place, *refs)

    gram = call(
        finish,
        shaped(288, 288),
        [SMEM] + [VMEM] * 4,
        [pltpu.VMEM((4, 2, 72, 96), F32)],
        flops=1000000,
        moved=700000,
        name="final",
    )(y.astype(jnp.int32).reshape(1), mine, one, two, three)
    return precond, gram


def solution(mesh):
    placed = (
        P(None, ("sx", "sy")),
        P(None, ("sx", "sy")),
        P(None, ("sx", "sy")),
        P("sx", "sy", None, None),
        P("sx", "sy", None, None),
        P("sx", "sy", None),
    )
    return jax.shard_map(
        body, mesh=mesh, in_specs=placed, out_specs=(P(None, ("sx", "sy")), P()), check_vma=False
    )
```

```python
import jax
import jax.numpy as jnp
from jax import lax
from jax.experimental import pallas as pl
from jax.experimental.pallas import tpu as pltpu
from jax.sharding import PartitionSpec as P

EDGE = 72
LANES = 128
TAIL = 1280
F32 = jnp.float32
BF16 = jnp.bfloat16
VMEM = pl.BlockSpec(memory_space=pltpu.VMEM)
SMEM = pl.BlockSpec(memory_space=pltpu.SMEM)
HBM = pl.BlockSpec(memory_space=pl.ANY)
NN = (((1,), (0,)), ((), ()))
NT = (((1,), (1,)), ((), ()))


def split(value):
    high = value.astype(BF16)
    low = (value - high.astype(F32)).astype(BF16)
    return high, low


def dot(left, right, dims):
    return lax.dot_general(left, right, dims, preferred_element_type=F32)


def dot_pairs(left, right, dims):
    rows = left[0].shape[0]
    both = dot(jnp.concatenate(left, axis=0), right[0], dims)
    return both[:rows] + both[rows:] + dot(left[0], right[1], dims)


def dot_exact(left, right, dims):
    rows = left[0].shape[0]
    both = dot(jnp.concatenate(left, axis=0), right, dims)
    return both[:rows] + both[rows:]


def pick(odd, when_even, when_odd):
    return jnp.where(jnp.full(when_even.shape, odd, jnp.int32) == 0, when_even, when_odd)


def call(kernel, out, in_specs, scratch=(), flops=0, moved=0, name=None, out_specs=None, limit=20):
    return pl.pallas_call(
        kernel,
        out_shape=out,
        in_specs=in_specs,
        out_specs=jax.tree.map(lambda _: VMEM, out) if out_specs is None else out_specs,
        scratch_shapes=list(scratch),
        compiler_params=pltpu.CompilerParams(vmem_limit_bytes=limit * 1024 * 1024),
        cost_estimate=pl.CostEstimate(flops=flops, bytes_accessed=moved, transcendentals=0),
        name=name,
    )


def shaped(*shape, dtype=F32):
    return jax.ShapeDtypeStruct(shape, dtype)


def in_hbm(value):
    return pltpu.with_memory_space_constraint(value, pltpu.HBM)


def gather_kernel(odd, count_hbm, rows_hbm, res_hbm, sxa, sxb, sya, syb, field, ids, count, rows, res, sem):
    fetch_count = pltpu.make_async_copy(count_hbm, count, sem.at[0])
    fetch_rows = pltpu.make_async_copy(rows_hbm, rows, sem.at[1])
    fetch_res = pltpu.make_async_copy(res_hbm, res, sem.at[2])
    fetch_count.start()
    fetch_rows.start()
    fetch_res.start()
    lane = lax.broadcasted_iota(jnp.int32, (1, LANES), 1)
    fetch_count.wait()
    fetch_rows.wait()
    table = rows[0, 0]

    def live(n):
        return count[0, 0, n]

    def edge(n):
        return jnp.where(lane < live(n), table[n : n + 1], -1)

    def corner(base, n, at):
        moved = pltpu.roll(table, at, 1)[n : n + 1]
        return jnp.where((lane >= at) & (lane < at + live(n)), moved, base)

    down = corner(corner(edge(0), 4, 72), 5, 80)
    up = corner(corner(edge(1), 6, 76), 7, 84)
    right, left = edge(2), edge(3)
    lists = [
        pick(odd[0], down, up),
        pick(odd[0], up, down),
        pick(odd[1], right, left),
        pick(odd[1], left, right),
    ]
    for k, values in enumerate(lists + lists):
        ids[k : k + 1] = values
    own = res.shape[1]
    row = lax.broadcasted_iota(jnp.int32, (own, LANES), 0)
    ones = [jnp.where(row == values, 1.0, 0.0).astype(BF16) for values in lists]
    onehot = jnp.concatenate(ones, axis=1)
    fetch_res.wait()
    high, low = split(res[...])
    field[:96] = high
    field[96:] = low
    packed = dot(field[...], onehot, NN)
    packed = packed[:96] + packed[96:]
    for k, out in enumerate((sxa, sxb, sya, syb)):
        out[...] = packed[:, k * LANES : (k + 1) * LANES]


def halo_place():
    col = lax.broadcasted_iota(jnp.int32, (320, 4 * LANES), 0) - 16
    spot = lax.broadcasted_iota(jnp.int32, (320, 4 * LANES), 1)
    lane = spot % LANES
    block = spot // LANES
    source = jnp.where(lane < EDGE, block * EDGE + lane, -99)
    for n, b, at in ((4, 2, 72), (6, 2, 76), (5, 3, 80), (7, 3, 84)):
        inside = (block == b) & (lane >= at) & (lane < at + 4)
        source = jnp.where(inside, 4 * EDGE + (n - 4) * 4 + lane - at, source)
    return jnp.where(col == source, 1.0, 0.0).astype(BF16)


def tail_kernel(field, factor, part, ph, plo, th, tlo, oh, olo, slab, sem):
    copy = pltpu.make_async_copy(factor.at[0, 0, pl.ds(TAIL, 320), :], slab, sem)
    copy.start()
    place = halo_place()
    copy.wait()
    own = field.shape[1]
    oh[...], olo[...] = split(slab[:, :own])
    part[...] = dot_pairs((field[:96], field[96:]), (oh[...], olo[...]), NT)
    for value, out, turned in zip(split(slab[:, TAIL:]), (ph, plo), (th, tlo)):
        placed = dot(value, place, NN)
        out[...] = placed.astype(BF16)
        turned[...] = placed.T.astype(BF16)


def halo_kernel(odd, sxa, sxb, sya, syb, part, ph, plo, th, tlo, half, bxa, bxb, bya, byb):
    xa, xb, ya, yb = sxa[...], sxb[...], sya[...], syb[...]
    arrived = jnp.concatenate(
        [pick(odd[0], xb, xa), pick(odd[0], xa, xb), pick(odd[1], yb, ya), pick(odd[1], ya, yb)], axis=1
    )
    solved = part[...] + dot_pairs(split(arrived), (th[...], tlo[...]), NN)
    half[...] = solved
    back = dot_pairs(split(solved), (ph[...], plo[...]), NN)
    b = [back[:, k * LANES : (k + 1) * LANES] for k in range(4)]
    bxa[...] = pick(odd[0], b[1], b[0])
    bxb[...] = pick(odd[0], b[0], b[1])
    bya[...] = pick(odd[1], b[3], b[2])
    byb[...] = pick(odd[1], b[2], b[3])


def body_kernel(field, factor, out, *scratch):
    slabs, sem = scratch[:-1], scratch[-1]
    copies = []
    for k, slab in enumerate(slabs):
        copies.append(
            pltpu.make_async_copy(
                factor.at[0, 0, pl.ds(256 * k, 256), pl.ds(0, 256 * (k + 1))], slab, sem.at[k]
            )
        )
        copies[-1].start()
    for k, slab in enumerate(slabs):
        width = 256 * (k + 1)
        copies[k].wait()
        block = split(slab[...])
        solved = dot_pairs((field[:96, :width], field[96:, :width]), block, NT)
        piece = dot_pairs(split(solved), block, NN)
        if k:
            out[:, : width - 256] = out[:, : width - 256] + piece[:, : width - 256]
        out[:, width - 256 : width] = piece[:, width - 256 :]


def local_kernel(base, half, oh, olo, ids, ritz_hbm, search_hbm, local, early, hot, rsh, rsl, ritz, search, sem):
    fetch_ritz = pltpu.make_async_copy(ritz_hbm, ritz, sem.at[0])
    fetch_search = pltpu.make_async_copy(search_hbm, search, sem.at[1])
    fetch_ritz.start()
    fetch_search.start()
    add = dot_pairs(split(half[...]), (oh[...], olo[...]), NN)
    local[:, :TAIL] = base[...] + add[:, :TAIL]
    local[:, TAIL:] = add[:, TAIL:]
    own = ritz.shape[1]
    columns = ids[...].astype(F32).T
    place = lax.broadcasted_iota(jnp.int32, (LANES, own), 1).astype(F32)
    for k in range(4):
        hot[k * LANES : (k + 1) * LANES] = jnp.where(columns[:, k : k + 1] == place, 1.0, 0.0).astype(BF16)
    fetch_ritz.wait()
    fetch_search.wait()
    r, s = split(ritz[...]), split(search[...])
    rt, st = split(ritz[...].T), split(search[...].T)
    blank = jnp.zeros((own, 32), BF16)
    rsh[...] = jnp.concatenate([rt[0], blank, st[0], blank], axis=1)
    rsl[...] = jnp.concatenate([rt[1], blank, st[1], blank], axis=1)
    both = (jnp.concatenate([r[0], s[0]], axis=0), jnp.concatenate([r[1], s[1]], axis=0))
    early[:192] = dot_pairs(both, rt, NN)
    early[192:] = dot_pairs(s, st, NN)


def gram_kernel(rxa, rxb, rya, ryb, hot, local, rsh, rsl, precond, late, update, sem):
    back = split(jnp.concatenate([rxa[...], rxb[...], rya[...], ryb[...]], axis=1))
    update[...] = local[...] + dot_exact(back, hot[...], NN)
    store = pltpu.make_async_copy(update, precond, sem)
    store.start()
    p = split(update[...])
    late[:96] = dot_pairs(p, p, NT)
    cross = dot_pairs(p, (rsh[...], rsl[...]), NN)
    late[96:192] = cross[:, :96]
    late[192:] = cross[:, LANES : LANES + 96]
    store.wait()


def final_kernel(scale, place, own, one, two, three, out, whole):
    for m, piece in enumerate((own, one, two, three)):
        at = place[0] ^ m
        whole[at] = piece[...] * scale
    def block(core, n):
        rows = [whole[y, core] for y in range(4)]
        return jnp.concatenate(rows, axis=0)[n * 96 : (n + 1) * 96]

    pp, pr, ps = (block(0, n) for n in range(3))
    rr, sr, ss = (block(1, n) for n in range(3))
    out[0:96, :] = jnp.concatenate([rr, pr.T, sr.T], axis=1)
    out[96:192, :] = jnp.concatenate([pr, pp, ps], axis=1)
    out[192:288, :] = jnp.concatenate([sr, ps.T, ss], axis=1)


def swap(block, axis, step):
    return lax.ppermute(block, axis, [(i, i ^ step) for i in range(lax.axis_size(axis))])


def swap_odd(block, axis):
    size = lax.axis_size(axis)
    route = [(i, i + 1) for i in range(1, size - 1, 2)]
    return lax.ppermute(block, axis, route + [(b, a) for a, b in route])


def body(residual, ritz_block, search_block, inverse_factor, send_rows, send_count):
    own = residual.shape[1]
    p, q = lax.axis_index("sx"), lax.axis_index("sy")
    odd = jnp.stack([p % 2, q % 2]).astype(jnp.int32)
    lane = jnp.arange(LANES)[None, :]
    msg = shaped(96, LANES)

    factor = in_hbm(inverse_factor)
    sxa, sxb, sya, syb, field, ids = call(
        gather_kernel,
        (msg, msg, msg, msg, shaped(192, own, dtype=BF16), shaped(8, LANES, dtype=jnp.int32)),
        [SMEM, HBM, HBM, HBM],
        [
            pltpu.SMEM((1, 1, 8), jnp.int32),
            pltpu.VMEM((1, 1, 8, LANES), jnp.int32),
            pltpu.VMEM((96, own), F32),
            pltpu.SemaphoreType.DMA((3,)),
        ],
        flops=2 * 192 * 1296 * 512,
        moved=2000000,
        name="gather",
    )(odd, in_hbm(send_count), in_hbm(send_rows), in_hbm(residual))

    placed, turned = shaped(320, 512, dtype=BF16), shaped(512, 320, dtype=BF16)
    wide = shaped(320, own, dtype=BF16)
    part, ph, plo, th, tlo, oh, olo = call(
        tail_kernel,
        (shaped(96, 320), placed, placed, turned, turned, wide, wide),
        [VMEM, HBM],
        [pltpu.VMEM((320, 1600), F32), pltpu.SemaphoreType.DMA],
        flops=2 * 96 * 1296 * 320 * 3,
        moved=4000000,
        name="tail",
    )(field, factor)

    base = call(
        body_kernel,
        shaped(96, TAIL),
        [VMEM, HBM],
        [pltpu.VMEM((256, 256 * (k + 1)), F32) for k in range(5)] + [pltpu.SemaphoreType.DMA((5,))],
        flops=2 * 2 * 96 * 256 * 256 * 15 * 3,
        moved=5000000,
        name="body",
    )(field, factor)

    gxa, gxb = swap(sxa, "sx", 1), swap_odd(sxb, "sx")
    relay = jnp.where(lane >= EDGE, gxa + gxb, 0.0)
    gya, gyb = swap(sya + relay, "sy", 1), swap_odd(syb + relay, "sy")

    half, bxa, bxb, bya, byb = call(
        halo_kernel,
        (shaped(96, 320), msg, msg, msg, msg),
        [SMEM] + [VMEM] * 9,
        flops=2 * 2 * 96 * 320 * 512 * 3,
        moved=1000000,
        name="halo",
    )(odd, gxa, gxb, gya, gyb, part, ph, plo, th, tlo)

    rya, ryb = swap(bya, "sy", 1), swap_odd(byb, "sy")
    relay = jnp.where(lane >= EDGE, rya + ryb, 0.0)
    rxa, rxb = swap(bxa + relay, "sx", 1), swap_odd(bxb + relay, "sx")

    sides = shaped(own, 2 * LANES, dtype=BF16)
    local, early, hot, rsh, rsl = call(
        local_kernel,
        (shaped(96, own), shaped(288, 96), shaped(512, own, dtype=BF16), sides, sides),
        [VMEM] * 5 + [HBM] * 2,
        [pltpu.VMEM((96, own), F32), pltpu.VMEM((96, own), F32), pltpu.SemaphoreType.DMA((2,))],
        flops=2 * 96 * 1296 * 320 * 3 + 2 * 96 * 288 * 1296 * 3,
        moved=4000000,
        name="local",
    )(base, half, oh, olo, ids, in_hbm(ritz_block), in_hbm(search_block))

    precond, late = call(
        gram_kernel,
        (shaped(96, own), shaped(288, 96)),
        [VMEM] * 8,
        [pltpu.VMEM((96, own), F32), pltpu.SemaphoreType.DMA],
        flops=2 * 192 * 1296 * 512 + 2 * 96 * 288 * 1296 * 3,
        moved=4000000,
        name="gram",
        out_specs=(HBM, VMEM),
    )(rxa, rxb, rya, ryb, hot, local, rsh, rsl)

    core, y = p % 2, p // 2
    kept = jnp.where(core == 0, late, early) + swap(jnp.where(core == 0, early, late), "sx", 1)
    quarters = kept.reshape(4, 72, 96)

    def quarter(m):
        return lax.dynamic_index_in_dim(quarters, y ^ m, 0, keepdims=False)

    def summed(value, axis, steps):
        total = value
        for step in steps:
            total = total + swap(value, axis, step)
        return total

    total = quarter(0)
    for m in (2, 1, 3):
        total = total + swap(quarter(m), "sx", 2 * m)
    total = summed(total, "sy", (16, 8, 24))
    total = summed(total, "sy", (3, 2, 1))
    total = summed(total, "sy", (6,))
    other = swap(total, "sx", 1)
    mine = jnp.where(core == 0, jnp.stack([total, other]), jnp.stack([other, total]))
    two, one, three = (swap(mine, "sx", 2 * m) for m in (2, 1, 3))

    vertex_total = own * lax.axis_size("sx") * lax.axis_size("sy")

    def finish(place, *refs):
        final_kernel(1.0 / vertex_total, place, *refs)

    gram = call(
        finish,
        shaped(288, 288),
        [SMEM] + [VMEM] * 4,
        [pltpu.VMEM((4, 2, 72, 96), F32)],
        flops=1000000,
        moved=700000,
        name="final",
    )(y.astype(jnp.int32).reshape(1), mine, one, two, three)
    return precond, gram


def solution(mesh):
    placed = (
        P(None, ("sx", "sy")),
        P(None, ("sx", "sy")),
        P(None, ("sx", "sy")),
        P("sx", "sy", None, None),
        P("sx", "sy", None, None),
        P("sx", "sy", None),
    )
    return jax.shard_map(
        body, mesh=mesh, in_specs=placed, out_specs=(P(None, ("sx", "sy")), P()), check_vma=False
    )
```

```python
import jax
import jax.numpy as jnp
from jax import lax
from jax.experimental import pallas as pl
from jax.experimental.pallas import tpu as pltpu
from jax.sharding import PartitionSpec as P

EDGE = 72
LANES = 128
TAIL = 1280
F32 = jnp.float32
BF16 = jnp.bfloat16
VMEM = pl.BlockSpec(memory_space=pltpu.VMEM)
SMEM = pl.BlockSpec(memory_space=pltpu.SMEM)
HBM = pl.BlockSpec(memory_space=pl.ANY)
NN = (((1,), (0,)), ((), ()))
NT = (((1,), (1,)), ((), ()))


def split(value):
    high = value.astype(BF16)
    low = (value - high.astype(F32)).astype(BF16)
    return high, low


def dot(left, right, dims):
    return lax.dot_general(left, right, dims, preferred_element_type=F32)


def dot_pairs(left, right, dims):
    rows = left[0].shape[0]
    both = dot(jnp.concatenate(left, axis=0), right[0], dims)
    return both[:rows] + both[rows:] + dot(left[0], right[1], dims)


def dot_exact(left, right, dims):
    rows = left[0].shape[0]
    both = dot(jnp.concatenate(left, axis=0), right, dims)
    return both[:rows] + both[rows:]


def pick(odd, when_even, when_odd):
    return jnp.where(jnp.full(when_even.shape, odd, jnp.int32) == 0, when_even, when_odd)


def call(kernel, out, in_specs, scratch=(), flops=0, moved=0, name=None, out_specs=None, limit=20):
    return pl.pallas_call(
        kernel,
        out_shape=out,
        in_specs=in_specs,
        out_specs=jax.tree.map(lambda _: VMEM, out) if out_specs is None else out_specs,
        scratch_shapes=list(scratch),
        compiler_params=pltpu.CompilerParams(vmem_limit_bytes=limit * 1024 * 1024),
        cost_estimate=pl.CostEstimate(flops=flops, bytes_accessed=moved, transcendentals=0),
        name=name,
    )


def shaped(*shape, dtype=F32):
    return jax.ShapeDtypeStruct(shape, dtype)


def in_hbm(value):
    return pltpu.with_memory_space_constraint(value, pltpu.HBM)


def gather_kernel(
    odd, count_hbm, rows_hbm, res_hbm, factor, sxa, sxb, sya, syb, field, ids, slab, count, rows, res, sem
):
    fetch_count = pltpu.make_async_copy(count_hbm, count, sem.at[0])
    fetch_rows = pltpu.make_async_copy(rows_hbm, rows, sem.at[1])
    fetch_res = pltpu.make_async_copy(res_hbm, res, sem.at[2])
    fetch_count.start()
    fetch_rows.start()
    fetch_res.start()
    fetch_slab = pltpu.make_async_copy(factor.at[0, 0, pl.ds(TAIL, 320), :], slab, sem.at[3])
    fetch_slab.start()
    lane = lax.broadcasted_iota(jnp.int32, (1, LANES), 1)
    fetch_count.wait()
    fetch_rows.wait()
    table = rows[0, 0]

    def live(n):
        return count[0, 0, n]

    def edge(n):
        return jnp.where(lane < live(n), table[n : n + 1], -1)

    def corner(base, n, at):
        moved = pltpu.roll(table, at, 1)[n : n + 1]
        return jnp.where((lane >= at) & (lane < at + live(n)), moved, base)

    down = corner(corner(edge(0), 4, 72), 5, 80)
    up = corner(corner(edge(1), 6, 76), 7, 84)
    right, left = edge(2), edge(3)
    lists = [
        pick(odd[0], down, up),
        pick(odd[0], up, down),
        pick(odd[1], right, left),
        pick(odd[1], left, right),
    ]
    for k, values in enumerate(lists + lists):
        ids[k : k + 1] = values
    own = res.shape[1]
    row = lax.broadcasted_iota(jnp.int32, (own, LANES), 0)
    ones = [jnp.where(row == values, 1.0, 0.0).astype(BF16) for values in lists]
    onehot = jnp.concatenate(ones, axis=1)
    fetch_res.wait()
    high, low = split(res[...])
    field[:96] = high
    field[96:] = low
    packed = dot(field[...], onehot, NN)
    packed = packed[:96] + packed[96:]
    for k, out in enumerate((sxa, sxb, sya, syb)):
        out[...] = packed[:, k * LANES : (k + 1) * LANES]
    fetch_slab.wait()


def halo_place():
    col = lax.broadcasted_iota(jnp.int32, (320, 4 * LANES), 0) - 16
    spot = lax.broadcasted_iota(jnp.int32, (320, 4 * LANES), 1)
    lane = spot % LANES
    block = spot // LANES
    source = jnp.where(lane < EDGE, block * EDGE + lane, -99)
    for n, b, at in ((4, 2, 72), (6, 2, 76), (5, 3, 80), (7, 3, 84)):
        inside = (block == b) & (lane >= at) & (lane < at + 4)
        source = jnp.where(inside, 4 * EDGE + (n - 4) * 4 + lane - at, source)
    return jnp.where(col == source, 1.0, 0.0).astype(BF16)


def tail_kernel(field, slab, factor, part, ph, plo, th, tlo, oh, olo, *rest):
    slabs, sem = rest[:-1], rest[-1]
    copies = []
    for k, dest in enumerate(slabs):
        block = factor.at[0, 0, pl.ds(256 * k, 256), pl.ds(0, 256 * (k + 1))]
        copies.append(pltpu.make_async_copy(block, dest, sem.at[k]))
        copies[-1].start()
    place = halo_place()
    own = field.shape[1]
    oh[...], olo[...] = split(slab[:, :own])
    part[...] = dot_pairs((field[:96], field[96:]), (oh[...], olo[...]), NT)
    for value, out, turned in zip(split(slab[:, TAIL:]), (ph, plo), (th, tlo)):
        placed = dot(value, place, NN)
        out[...] = placed.astype(BF16)
        turned[...] = placed.T.astype(BF16)
    for copy in copies:
        copy.wait()


def halo_kernel(odd, sxa, sxb, sya, syb, part, ph, plo, th, tlo, half, bxa, bxb, bya, byb):
    xa, xb, ya, yb = sxa[...], sxb[...], sya[...], syb[...]
    arrived = jnp.concatenate(
        [pick(odd[0], xb, xa), pick(odd[0], xa, xb), pick(odd[1], yb, ya), pick(odd[1], ya, yb)], axis=1
    )
    solved = part[...] + dot_pairs(split(arrived), (th[...], tlo[...]), NN)
    half[...] = solved
    back = dot_pairs(split(solved), (ph[...], plo[...]), NN)
    b = [back[:, k * LANES : (k + 1) * LANES] for k in range(4)]
    bxa[...] = pick(odd[0], b[1], b[0])
    bxb[...] = pick(odd[0], b[0], b[1])
    bya[...] = pick(odd[1], b[3], b[2])
    byb[...] = pick(odd[1], b[2], b[3])


def slab_term(field, slab):
    width = slab.shape[1]
    block = split(slab[...])
    solved = dot_pairs((field[:96, :width], field[96:, :width]), block, NT)
    return dot_pairs(split(solved), block, NN)


def head_kernel(field, *refs):
    slabs, out = refs[:-1], refs[-1]
    out[...] = slab_term(field, slabs[-1])
    for slab in slabs[:-1]:
        width = slab.shape[1]
        out[:, :width] = out[:, :width] + slab_term(field, slab)


def side_kernel(ids, ritz_hbm, search_hbm, early, hot, turned, same, rsh, rsl, rgh, rgl, ritz, search, sem):
    fetch_ritz = pltpu.make_async_copy(ritz_hbm, ritz, sem.at[0])
    fetch_search = pltpu.make_async_copy(search_hbm, search, sem.at[1])
    fetch_ritz.start()
    fetch_search.start()
    own = ritz.shape[1]
    numbers = ids[...].astype(F32)
    columns = numbers.T
    across = lax.broadcasted_iota(jnp.int32, (LANES, own), 1).astype(F32)
    down = lax.broadcasted_iota(jnp.int32, (own, LANES), 0).astype(F32)
    for k in range(4):
        lanes = slice(k * LANES, (k + 1) * LANES)
        column = columns[:, k : k + 1]
        turned[lanes] = jnp.where(column == across, 1.0, 0.0).astype(BF16)
        hot[:, lanes] = jnp.where(numbers[k : k + 1] == down, 1.0, 0.0).astype(BF16)
        for j in range(4):
            row = numbers[j : j + 1]
            agree = (column == row) & (row >= 0.0)
            same[lanes, j * LANES : (j + 1) * LANES] = jnp.where(agree, 1.0, 0.0).astype(BF16)
    fetch_ritz.wait()
    fetch_search.wait()
    r, s = split(ritz[...]), split(search[...])
    blank = jnp.zeros((32, own), F32)
    padded = jnp.concatenate([ritz[...], blank, search[...], blank], axis=0)
    sides = split(padded.T)
    rsh[...], rsl[...] = sides
    for side, out in zip(sides, (rgh, rgl)):
        out[...] = dot(turned[...], side, NN).astype(BF16)
    both = (jnp.concatenate([r[0], s[0]], axis=0), jnp.concatenate([r[1], s[1]], axis=0))
    cross = dot_pairs(both, (rsh[...], rsl[...]), NN)
    early[:192] = cross[:, :96]
    early[192:] = cross[96:, LANES : LANES + 96]


def local_kernel(head, last, half, oh, olo, hot, rsh, rsl, local, sent, base):
    add = dot_pairs(split(half[...]), (oh[...], olo[...]), NN)
    value = add + jnp.concatenate([head[...], jnp.zeros((96, add.shape[1] - TAIL + 256), F32)], axis=1)
    value = value + jnp.concatenate([last[...], jnp.zeros((96, add.shape[1] - TAIL), F32)], axis=1)
    local[...] = value
    pair = split(value)
    sent[...] = dot_exact(pair, hot[...], NN)
    base[:96] = dot_pairs(pair, pair, NT)
    cross = dot_pairs(pair, (rsh[...], rsl[...]), NN)
    base[96:192] = cross[:, :96]
    base[192:] = cross[:, LANES : LANES + 96]


def gram_kernel(odd, rxa, rxb, rya, ryb, same, sent, rgh, rgl, base, early, away, kept, back):
    back[...] = jnp.concatenate([rxa[...], rxb[...], rya[...], ryb[...]], axis=1)
    pair = split(back[...])
    mixed = sent[...] + 0.5 * dot_exact(pair, same[...], NN)
    square = dot_pairs(split(mixed), pair, NT)
    cross = dot_pairs(pair, (rgh[...], rgl[...]), NN)
    late = [
        base[:96] + square + square.T,
        base[96:192] + cross[:, :96],
        base[192:] + cross[:, LANES : LANES + 96],
    ]
    for k, value in enumerate(late):
        rows = slice(96 * k, 96 * (k + 1))
        first = early[rows]
        away[rows] = pick(odd[0], first, value)
        kept[rows] = pick(odd[0], value, first)


def update_kernel(back, turned, local, precond):
    precond[...] = local[...] + dot_exact(split(back[...]), turned[...], NN)


def final_kernel(scale, odd, mine, other, out):
    late = pick(odd[0], mine[...], other[...]) * scale
    early = pick(odd[0], other[...], mine[...]) * scale
    pp, pr, ps = (late[n * 96 : (n + 1) * 96] for n in range(3))
    rr, sr, ss = (early[n * 96 : (n + 1) * 96] for n in range(3))
    out[0:96, :] = jnp.concatenate([rr, pr.T, sr.T], axis=1)
    out[96:192, :] = jnp.concatenate([pr, pp, ps], axis=1)
    out[192:288, :] = jnp.concatenate([sr, ps.T, ss], axis=1)


def swap(block, axis, step):
    return lax.ppermute(block, axis, [(i, i ^ step) for i in range(lax.axis_size(axis))])


def swap_odd(block, axis):
    size = lax.axis_size(axis)
    route = [(i, i + 1) for i in range(1, size - 1, 2)]
    return lax.ppermute(block, axis, route + [(b, a) for a, b in route])


def body(residual, ritz_block, search_block, inverse_factor, send_rows, send_count):
    own = residual.shape[1]
    p, q = lax.axis_index("sx"), lax.axis_index("sy")
    odd = jnp.stack([p % 2, q % 2]).astype(jnp.int32)
    lane = jnp.arange(LANES)[None, :]
    msg = shaped(96, LANES)

    factor = in_hbm(inverse_factor)
    sxa, sxb, sya, syb, field, ids, slab = call(
        gather_kernel,
        (
            msg,
            msg,
            msg,
            msg,
            shaped(192, own, dtype=BF16),
            shaped(8, LANES, dtype=jnp.int32),
            shaped(320, 1600),
        ),
        [SMEM, HBM, HBM, HBM, HBM],
        [
            pltpu.SMEM((1, 1, 8), jnp.int32),
            pltpu.VMEM((1, 1, 8, LANES), jnp.int32),
            pltpu.VMEM((96, own), F32),
            pltpu.SemaphoreType.DMA((4,)),
        ],
        flops=2 * 192 * 1296 * 512,
        moved=2000000,
        name="gather",
    )(odd, in_hbm(send_count), in_hbm(send_rows), in_hbm(residual), factor)

    gxb, gxa = swap_odd(sxb, "sx"), swap(sxa, "sx", 1)

    placed, turned = shaped(320, 512, dtype=BF16), shaped(512, 320, dtype=BF16)
    wide = shaped(320, own, dtype=BF16)
    part, ph, plo, th, tlo, oh, olo, *slabs = call(
        tail_kernel,
        (shaped(96, 320), placed, placed, turned, turned, wide, wide)
        + tuple(shaped(256, 256 * (k + 1)) for k in range(5)),
        [VMEM, VMEM, HBM],
        [pltpu.SemaphoreType.DMA((5,))],
        flops=2 * 96 * 1296 * 320 * 3,
        moved=6000000,
        name="tail",
    )(field, slab, factor)
    gxa, gxb, part = lax.optimization_barrier((gxa, gxb, part))

    relay = jnp.where(lane >= EDGE, gxa + gxb, 0.0)
    gyb, gya = swap_odd(syb + relay, "sy"), swap(sya + relay, "sy", 1)

    head = call(
        head_kernel,
        shaped(96, 1024),
        [VMEM] * 5,
        flops=2 * 2 * 96 * 256 * 256 * 10 * 3,
        moved=3000000,
        name="head",
    )(field, *slabs[:4])
    gya, gyb, head = lax.optimization_barrier((gya, gyb, head))

    half, bxa, bxb, bya, byb = call(
        halo_kernel,
        (shaped(96, 320), msg, msg, msg, msg),
        [SMEM] + [VMEM] * 9,
        flops=2 * 2 * 96 * 320 * 512 * 3,
        moved=1000000,
        name="halo",
    )(odd, gxa, gxb, gya, gyb, part, ph, plo, th, tlo)

    ryb, rya = swap_odd(byb, "sy"), swap(bya, "sy", 1)

    last = call(
        head_kernel,
        shaped(96, TAIL),
        [VMEM] * 2,
        flops=2 * 2 * 96 * 256 * 256 * 5 * 3,
        moved=1500000,
        name="last",
    )(field, slabs[4])
    sides, sent_sides = shaped(own, 2 * LANES, dtype=BF16), shaped(512, 2 * LANES, dtype=BF16)
    early, hot, turned, same, rsh, rsl, rgh, rgl = call(
        side_kernel,
        (
            shaped(288, 96),
            shaped(own, 512, dtype=BF16),
            shaped(512, own, dtype=BF16),
            shaped(512, 512, dtype=BF16),
            sides,
            sides,
            sent_sides,
            sent_sides,
        ),
        [VMEM, HBM, HBM],
        [pltpu.VMEM((96, own), F32), pltpu.VMEM((96, own), F32), pltpu.SemaphoreType.DMA((2,))],
        flops=2 * 192 * 256 * 1296 * 3,
        moved=3000000,
        name="side",
    )(ids, in_hbm(ritz_block), in_hbm(search_block))
    rya, ryb, last, early = lax.optimization_barrier((rya, ryb, last, early))

    relay = jnp.where(lane >= EDGE, rya + ryb, 0.0)
    rxb, rxa = swap_odd(bxb + relay, "sx"), swap(bxa + relay, "sx", 1)

    local, sent, base = call(
        local_kernel,
        (shaped(96, own), shaped(96, 512), shaped(288, 96)),
        [VMEM] * 8,
        flops=2 * 96 * 1296 * 1100 * 3,
        moved=4000000,
        name="local",
    )(head, last, half, oh, olo, hot, rsh, rsl)

    away, kept, back = call(
        gram_kernel,
        (shaped(288, 96), shaped(288, 96), shaped(96, 512)),
        [SMEM] + [VMEM] * 10,
        flops=2 * 96 * 512 * 900 * 3,
        moved=2000000,
        name="gram",
    )(odd, rxa, rxb, rya, ryb, same, sent, rgh, rgl, base, early)

    precond = call(
        update_kernel,
        shaped(96, own),
        [VMEM] * 3,
        flops=2 * 192 * 1296 * 512,
        moved=3000000,
        name="update",
    )(back, turned, local)

    y = p // 2
    quarters = (kept + swap(away, "sx", 1)).reshape(4, 72, 96)

    def quarter(m):
        return lax.dynamic_index_in_dim(quarters, y ^ m, 0, keepdims=False)

    def summed(value, axis, steps):
        total = value
        for step in steps:
            total = total + swap(value, axis, step)
        return total

    total = quarter(0)
    for m in (1, 3, 2):
        total = total + swap(quarter(m), "sx", 2 * m)
    total = summed(total, "sy", (8, 24, 16))
    total = summed(total, "sy", (3, 2, 1))
    total = summed(total, "sy", (6,))
    mine = jnp.zeros((4, 72, 96), F32)
    for m in (0, 1, 3, 2):
        piece = swap(total, "sx", 2 * m) if m else total
        mine = lax.dynamic_update_index_in_dim(mine, piece, y ^ m, 0)
    mine = mine.reshape(288, 96)
    other = swap(mine, "sx", 1)

    vertex_total = own * lax.axis_size("sx") * lax.axis_size("sy")

    def finish(odd, *refs):
        final_kernel(1.0 / vertex_total, odd, *refs)

    gram = call(
        finish,
        shaped(288, 288),
        [SMEM] + [VMEM] * 2,
        flops=1000000,
        moved=700000,
        name="final",
    )(odd, mine, other)
    return precond, gram


def solution(mesh):
    placed = (
        P(None, ("sx", "sy")),
        P(None, ("sx", "sy")),
        P(None, ("sx", "sy")),
        P("sx", "sy", None, None),
        P("sx", "sy", None, None),
        P("sx", "sy", None),
    )
    return jax.shard_map(
        body, mesh=mesh, in_specs=placed, out_specs=(P(None, ("sx", "sy")), P()), check_vma=False
    )
```

```python
import jax
import jax.numpy as jnp
from jax import lax
from jax.experimental import pallas as pl
from jax.experimental.pallas import tpu as pltpu
from jax.sharding import PartitionSpec as P

EDGE = 72
LANES = 128
TAIL = 1280
F32 = jnp.float32
BF16 = jnp.bfloat16
VMEM = pl.BlockSpec(memory_space=pltpu.VMEM)
SMEM = pl.BlockSpec(memory_space=pltpu.SMEM)
HBM = pl.BlockSpec(memory_space=pl.ANY)
NN = (((1,), (0,)), ((), ()))
NT = (((1,), (1,)), ((), ()))


def split(value):
    high = value.astype(BF16)
    low = (value - high.astype(F32)).astype(BF16)
    return high, low


def dot(left, right, dims):
    return lax.dot_general(left, right, dims, preferred_element_type=F32)


def dot_pairs(left, right, dims):
    rows = left[0].shape[0]
    both = dot(jnp.concatenate(left, axis=0), right[0], dims)
    return both[:rows] + both[rows:] + dot(left[0], right[1], dims)


def dot_exact(left, right, dims):
    rows = left[0].shape[0]
    both = dot(jnp.concatenate(left, axis=0), right, dims)
    return both[:rows] + both[rows:]


def pick(odd, when_even, when_odd):
    return jnp.where(jnp.full(when_even.shape, odd, jnp.int32) == 0, when_even, when_odd)


def call(kernel, out, in_specs, scratch=(), flops=0, moved=0, name=None, out_specs=None, limit=20):
    return pl.pallas_call(
        kernel,
        out_shape=out,
        in_specs=in_specs,
        out_specs=jax.tree.map(lambda _: VMEM, out) if out_specs is None else out_specs,
        scratch_shapes=list(scratch),
        compiler_params=pltpu.CompilerParams(vmem_limit_bytes=limit * 1024 * 1024),
        cost_estimate=pl.CostEstimate(flops=flops, bytes_accessed=moved, transcendentals=0),
        name=name,
    )


def shaped(*shape, dtype=F32):
    return jax.ShapeDtypeStruct(shape, dtype)


def in_hbm(value):
    return pltpu.with_memory_space_constraint(value, pltpu.HBM)


def gather_kernel(
    odd, count_hbm, rows_hbm, res_hbm, factor, sxa, sxb, sya, syb, field, ids, slab, count, rows, res, sem
):
    fetch_count = pltpu.make_async_copy(count_hbm, count, sem.at[0])
    fetch_rows = pltpu.make_async_copy(rows_hbm, rows, sem.at[1])
    fetch_res = pltpu.make_async_copy(res_hbm, res, sem.at[2])
    fetch_count.start()
    fetch_rows.start()
    fetch_res.start()
    fetch_slab = pltpu.make_async_copy(factor.at[0, 0, pl.ds(TAIL, 320), :], slab, sem.at[3])
    fetch_slab.start()
    lane = lax.broadcasted_iota(jnp.int32, (1, LANES), 1)
    fetch_count.wait()
    fetch_rows.wait()
    table = rows[0, 0]

    def live(n):
        return count[0, 0, n]

    def edge(n):
        return jnp.where(lane < live(n), table[n : n + 1], -1)

    def corner(base, n, at):
        moved = pltpu.roll(table, at, 1)[n : n + 1]
        return jnp.where((lane >= at) & (lane < at + live(n)), moved, base)

    down = corner(corner(edge(0), 4, 72), 5, 80)
    up = corner(corner(edge(1), 6, 76), 7, 84)
    right, left = edge(2), edge(3)
    lists = [
        pick(odd[0], down, up),
        pick(odd[0], up, down),
        pick(odd[1], right, left),
        pick(odd[1], left, right),
    ]
    for k, values in enumerate(lists + lists):
        ids[k : k + 1] = values
    own = res.shape[1]
    row = lax.broadcasted_iota(jnp.int32, (own, LANES), 0)
    ones = [jnp.where(row == values, 1.0, 0.0).astype(BF16) for values in lists]
    onehot = jnp.concatenate(ones, axis=1)
    fetch_res.wait()
    high, low = split(res[...])
    field[:96] = high
    field[96:] = low
    packed = dot(field[...], onehot, NN)
    packed = packed[:96] + packed[96:]
    for k, out in enumerate((sxa, sxb, sya, syb)):
        out[...] = packed[:, k * LANES : (k + 1) * LANES]
    fetch_slab.wait()


def halo_place():
    col = lax.broadcasted_iota(jnp.int32, (320, 4 * LANES), 0) - 16
    spot = lax.broadcasted_iota(jnp.int32, (1, 4 * LANES), 1)
    lane = spot % LANES
    block = spot // LANES
    source = jnp.where(lane < EDGE, block * EDGE + lane, -99)
    for n, b, at in ((4, 2, 72), (6, 2, 76), (5, 3, 80), (7, 3, 84)):
        inside = (block == b) & (lane >= at) & (lane < at + 4)
        source = jnp.where(inside, 4 * EDGE + (n - 4) * 4 + lane - at, source)
    return jnp.where(col == source, 1.0, 0.0).astype(BF16)


def fetch(pairs, sem):
    copies = [pltpu.make_async_copy(source, dest, sem.at[k]) for k, (source, dest) in enumerate(pairs)]
    for copy in copies:
        copy.start()
    return copies


def own_slab(factor, k):
    return factor.at[0, 0, pl.ds(256 * k, 256), pl.ds(0, 256 * (k + 1))]


def tail_kernel(field, slab, factor, part, ph, plo, th, tlo, oh, olo, slab0, slab1, slab2, slab3, sem):
    slabs = (slab0, slab1, slab2, slab3)
    copies = fetch([(own_slab(factor, k), dest) for k, dest in enumerate(slabs)], sem)
    place = halo_place()
    own = field.shape[1]
    oh[...], olo[...] = split(slab[:, :own])
    part[...] = dot_pairs((field[:96], field[96:]), (oh[...], olo[...]), NT)
    for value, out, turned in zip(split(slab[:, TAIL:]), (ph, plo), (th, tlo)):
        placed = dot(value, place, NN)
        out[...] = placed.astype(BF16)
        turned[...] = placed.T.astype(BF16)
    for copy in copies:
        copy.wait()


def halo_kernel(odd, sxa, sxb, sya, syb, part, ph, plo, th, tlo, half, bxa, bxb, bya, byb):
    xa, xb, ya, yb = sxa[...], sxb[...], sya[...], syb[...]
    arrived = jnp.concatenate(
        [pick(odd[0], xb, xa), pick(odd[0], xa, xb), pick(odd[1], yb, ya), pick(odd[1], ya, yb)], axis=1
    )
    solved = part[...] + dot_pairs(split(arrived), (th[...], tlo[...]), NN)
    half[...] = solved
    back = dot_pairs(split(solved), (ph[...], plo[...]), NN)
    b = [back[:, k * LANES : (k + 1) * LANES] for k in range(4)]
    bxa[...] = pick(odd[0], b[1], b[0])
    bxb[...] = pick(odd[0], b[0], b[1])
    bya[...] = pick(odd[1], b[3], b[2])
    byb[...] = pick(odd[1], b[2], b[3])


def slab_term(field, slab):
    width = slab.shape[1]
    block = split(slab[...])
    solved = dot_pairs((field[:96, :width], field[96:, :width]), block, NT)
    return dot_pairs(split(solved), block, NN)


def head_kernel(field, slab0, slab1, slab2, slab3, factor, ritz_hbm, search_hbm, out, slab4, ritz, search, sem):
    copies = fetch([(own_slab(factor, 4), slab4), (ritz_hbm, ritz), (search_hbm, search)], sem)
    out[...] = slab_term(field, slab3)
    for slab in (slab2, slab1, slab0):
        width = slab.shape[1]
        out[:, :width] = out[:, :width] + slab_term(field, slab)
    for copy in copies:
        copy.wait()


def last_kernel(field, slab4, out):
    out[...] = slab_term(field, slab4)


def side_kernel(ids, ritz, search, early, turned, same, sides_h, sides_l, rgh, rgl):
    own = ritz.shape[1]
    numbers = ids[...].astype(F32)
    columns = numbers.T
    live = jnp.where(columns < 0.0, -2.0, columns)
    across = lax.broadcasted_iota(jnp.int32, (LANES, own), 1).astype(F32)
    for k in range(4):
        lanes = slice(k * LANES, (k + 1) * LANES)
        turned[lanes] = jnp.where(columns[:, k : k + 1] == across, 1.0, 0.0).astype(BF16)
        for j in range(4):
            agree = live[:, k : k + 1] == numbers[j : j + 1]
            same[lanes, j * LANES : (j + 1) * LANES] = jnp.where(agree, 1.0, 0.0).astype(BF16)
    blank = jnp.zeros((32, own), BF16)
    for r, s, out in zip(split(ritz[...]), split(search[...]), (sides_h, sides_l)):
        out[:96] = r
        out[96:128] = blank
        out[128:224] = s
        out[224:] = blank
    for side, out in zip((sides_h, sides_l), (rgh, rgl)):
        out[...] = dot(turned[...], side[...], NT).astype(BF16)
    pair = (sides_h[...], sides_l[...])
    cross = dot_pairs(pair, pair, NT)
    early[:96] = cross[:96, :96]
    early[96:192] = cross[128:224, :96]
    early[192:] = cross[128:224, LANES : LANES + 96]


def local_kernel(head, last, half, oh, olo, turned, sides_h, sides_l, local, sent, base):
    add = dot_pairs(split(half[...]), (oh[...], olo[...]), NN)
    value = add + jnp.concatenate([head[...], jnp.zeros((96, add.shape[1] - TAIL + 256), F32)], axis=1)
    value = value + jnp.concatenate([last[...], jnp.zeros((96, add.shape[1] - TAIL), F32)], axis=1)
    local[...] = value
    pair = split(value)
    sent[...] = dot_exact(pair, turned[...], NT)
    base[:96] = dot_pairs(pair, pair, NT)
    cross = dot_pairs(pair, (sides_h[...], sides_l[...]), NT)
    base[96:192] = cross[:, :96]
    base[192:] = cross[:, LANES : LANES + 96]


def gram_kernel(odd, rxa, rxb, rya, ryb, same, sent, rgh, rgl, base, early, away, kept, back):
    back[...] = jnp.concatenate([rxa[...], rxb[...], rya[...], ryb[...]], axis=1)
    pair = split(back[...])
    mixed = sent[...] + 0.5 * dot_exact(pair, same[...], NN)
    square = dot_pairs(split(mixed), pair, NT)
    cross = dot_pairs(pair, (rgh[...], rgl[...]), NN)
    late = [
        base[:96] + square + square.T,
        base[96:192] + cross[:, :96],
        base[192:] + cross[:, LANES : LANES + 96],
    ]
    for k, value in enumerate(late):
        rows = slice(96 * k, 96 * (k + 1))
        first = early[rows]
        away[rows] = pick(odd[0], first, value)
        kept[rows] = pick(odd[0], value, first)


def update_kernel(back, turned, local, precond):
    precond[...] = local[...] + dot_exact(split(back[...]), turned[...], NN)


def final_kernel(scale, odd, mine, other, out):
    late = pick(odd[0], mine[...], other[...]) * scale
    early = pick(odd[0], other[...], mine[...]) * scale
    pp, pr, ps = (late[n * 96 : (n + 1) * 96] for n in range(3))
    rr, sr, ss = (early[n * 96 : (n + 1) * 96] for n in range(3))
    out[0:96, :] = jnp.concatenate([rr, pr.T, sr.T], axis=1)
    out[96:192, :] = jnp.concatenate([pr, pp, ps], axis=1)
    out[192:288, :] = jnp.concatenate([sr, ps.T, ss], axis=1)


def swap(block, axis, step):
    return lax.ppermute(block, axis, [(i, i ^ step) for i in range(lax.axis_size(axis))])


def swap_odd(block, axis):
    size = lax.axis_size(axis)
    route = [(i, (i + 1) % size) for i in range(1, size, 2)]
    return lax.ppermute(block, axis, route + [(b, a) for a, b in route])


def body(residual, ritz_block, search_block, inverse_factor, send_rows, send_count):
    own = residual.shape[1]
    p, q = lax.axis_index("sx"), lax.axis_index("sy")
    odd = jnp.stack([p % 2, q % 2]).astype(jnp.int32)
    lane = jnp.arange(LANES)[None, :]
    msg = shaped(96, LANES)

    factor = in_hbm(inverse_factor)
    sxa, sxb, sya, syb, field, ids, slab = call(
        gather_kernel,
        (
            msg,
            msg,
            msg,
            msg,
            shaped(192, own, dtype=BF16),
            shaped(8, LANES, dtype=jnp.int32),
            shaped(320, 1600),
        ),
        [SMEM, HBM, HBM, HBM, HBM],
        [
            pltpu.SMEM((1, 1, 8), jnp.int32),
            pltpu.VMEM((1, 1, 8, LANES), jnp.int32),
            pltpu.VMEM((96, own), F32),
            pltpu.SemaphoreType.DMA((4,)),
        ],
        flops=2 * 192 * 1296 * 512,
        moved=2000000,
        name="gather",
    )(odd, in_hbm(send_count), in_hbm(send_rows), in_hbm(residual), factor)

    gxb, gxa = swap_odd(sxb, "sx"), swap(sxa, "sx", 1)

    placed, turned = shaped(320, 512, dtype=BF16), shaped(512, 320, dtype=BF16)
    wide = shaped(320, own, dtype=BF16)
    part, ph, plo, th, tlo, oh, olo, slab0, slab1, slab2, slab3 = call(
        tail_kernel,
        (shaped(96, 320), placed, placed, turned, turned, wide, wide)
        + tuple(shaped(256, 256 * (k + 1)) for k in range(4)),
        [VMEM, VMEM, HBM],
        [pltpu.SemaphoreType.DMA((4,))],
        flops=2 * 96 * 1296 * 320 * 3,
        moved=6000000,
        name="tail",
    )(field, slab, factor)
    gxa, gxb, part = lax.optimization_barrier((gxa, gxb, part))

    relay = jnp.where(lane >= EDGE, gxa + gxb, 0.0)
    gyb, gya = swap_odd(syb + relay, "sy"), swap(sya + relay, "sy", 1)

    head, slab4, ritz, search = call(
        head_kernel,
        (shaped(96, 1024), shaped(256, TAIL), shaped(96, own), shaped(96, own)),
        [VMEM] * 5 + [HBM] * 3,
        [pltpu.SemaphoreType.DMA((3,))],
        flops=2 * 2 * 96 * 256 * 256 * 10 * 3,
        moved=4000000,
        name="head",
    )(field, slab0, slab1, slab2, slab3, factor, in_hbm(ritz_block), in_hbm(search_block))
    gya, gyb, head = lax.optimization_barrier((gya, gyb, head))

    half, bxa, bxb, bya, byb = call(
        halo_kernel,
        (shaped(96, 320), msg, msg, msg, msg),
        [SMEM] + [VMEM] * 9,
        flops=2 * 2 * 96 * 320 * 512 * 3,
        moved=1000000,
        name="halo",
    )(odd, gxa, gxb, gya, gyb, part, ph, plo, th, tlo)

    ryb, rya = swap_odd(byb, "sy"), swap(bya, "sy", 1)

    last = call(
        last_kernel,
        shaped(96, TAIL),
        [VMEM] * 2,
        flops=2 * 2 * 96 * 256 * 256 * 5 * 3,
        moved=1500000,
        name="last",
    )(field, slab4)
    sides, sent_sides = shaped(2 * LANES, own, dtype=BF16), shaped(512, 2 * LANES, dtype=BF16)
    early, turned, same, sides_h, sides_l, rgh, rgl = call(
        side_kernel,
        (
            shaped(288, 96),
            shaped(512, own, dtype=BF16),
            shaped(512, 512, dtype=BF16),
            sides,
            sides,
            sent_sides,
            sent_sides,
        ),
        [VMEM] * 3,
        flops=2 * 192 * 256 * 1296 * 3,
        moved=3000000,
        name="side",
    )(ids, ritz, search)
    rya, ryb, last, early = lax.optimization_barrier((rya, ryb, last, early))

    relay = jnp.where(lane >= EDGE, rya + ryb, 0.0)
    rxb, rxa = swap_odd(bxb + relay, "sx"), swap(bxa + relay, "sx", 1)

    local, sent, base = call(
        local_kernel,
        (shaped(96, own), shaped(96, 512), shaped(288, 96)),
        [VMEM] * 8,
        flops=2 * 96 * 1296 * 1100 * 3,
        moved=4000000,
        name="local",
    )(head, last, half, oh, olo, turned, sides_h, sides_l)

    away, kept, back = call(
        gram_kernel,
        (shaped(288, 96), shaped(288, 96), shaped(96, 512)),
        [SMEM] + [VMEM] * 10,
        flops=2 * 96 * 512 * 900 * 3,
        moved=2000000,
        name="gram",
    )(odd, rxa, rxb, rya, ryb, same, sent, rgh, rgl, base, early)

    precond = call(
        update_kernel,
        shaped(96, own),
        [VMEM] * 3,
        flops=2 * 192 * 1296 * 512,
        moved=3000000,
        name="update",
    )(back, turned, local)

    y = p // 2
    quarters = (kept + swap(away, "sx", 1)).reshape(4, 72, 96)

    def quarter(m):
        return lax.dynamic_index_in_dim(quarters, y ^ m, 0, keepdims=False)

    def summed(value, axis, steps):
        total = value
        for step in steps:
            total = total + swap(value, axis, step)
        return total

    total = quarter(0)
    for m in (1, 3, 2):
        total = total + swap(quarter(m), "sx", 2 * m)
    total = summed(total, "sy", (8, 24, 16))
    total = summed(total, "sy", (3, 2, 1))
    total = summed(total, "sy", (6,))
    total, precond = lax.optimization_barrier((total, precond))
    mine = jnp.zeros((4, 72, 96), F32)
    for m in (0, 1, 3, 2):
        piece = swap(total, "sx", 2 * m) if m else total
        mine = lax.dynamic_update_index_in_dim(mine, piece, y ^ m, 0)
    mine = mine.reshape(288, 96)
    other = swap(mine, "sx", 1)

    vertex_total = own * lax.axis_size("sx") * lax.axis_size("sy")

    def finish(odd, *refs):
        final_kernel(1.0 / vertex_total, odd, *refs)

    gram = call(
        finish,
        shaped(288, 288),
        [SMEM] + [VMEM] * 2,
        flops=1000000,
        moved=700000,
        name="final",
    )(odd, mine, other)
    return precond, gram


def solution(mesh):
    placed = (
        P(None, ("sx", "sy")),
        P(None, ("sx", "sy")),
        P(None, ("sx", "sy")),
        P("sx", "sy", None, None),
        P("sx", "sy", None, None),
        P("sx", "sy", None),
    )
    return jax.shard_map(
        body, mesh=mesh, in_specs=placed, out_specs=(P(None, ("sx", "sy")), P()), check_vma=False
    )
```

```python
import jax
import jax.numpy as jnp
from jax import lax
from jax.experimental import pallas as pl
from jax.experimental.pallas import tpu as pltpu
from jax.sharding import PartitionSpec as P

EDGE = 72
LANES = 128
TAIL = 1280
F32 = jnp.float32
BF16 = jnp.bfloat16
VMEM = pl.BlockSpec(memory_space=pltpu.VMEM)
HBM = pl.BlockSpec(memory_space=pl.ANY)
NN = (((1,), (0,)), ((), ()))
NT = (((1,), (1,)), ((), ()))


def split(value):
    high = value.astype(BF16)
    low = (value - high.astype(F32)).astype(BF16)
    return high, low


def dot(left, right, dims):
    return lax.dot_general(left, right, dims, preferred_element_type=F32)


def dot_pairs(left, right, dims):
    rows = left[0].shape[0]
    both = dot(jnp.concatenate(left, axis=0), right[0], dims)
    return both[:rows] + both[rows:] + dot(left[0], right[1], dims)


def dot_exact(left, right, dims):
    rows = left[0].shape[0]
    both = dot(jnp.concatenate(left, axis=0), right, dims)
    return both[:rows] + both[rows:]


def pick(flag, when_even, when_odd):
    return jnp.where(flag[:, : when_even.shape[1]] == 0, when_even, when_odd)


def call(kernel, out, in_specs, scratch=(), flops=0, moved=0, name=None, out_specs=None, limit=20):
    return pl.pallas_call(
        kernel,
        out_shape=out,
        in_specs=in_specs,
        out_specs=jax.tree.map(lambda _: VMEM, out) if out_specs is None else out_specs,
        scratch_shapes=list(scratch),
        compiler_params=pltpu.CompilerParams(vmem_limit_bytes=limit * 1024 * 1024),
        cost_estimate=pl.CostEstimate(flops=flops, bytes_accessed=moved, transcendentals=0),
        name=name,
    )


def shaped(*shape, dtype=F32):
    return jax.ShapeDtypeStruct(shape, dtype)


def in_hbm(value):
    return pltpu.with_memory_space_constraint(value, pltpu.HBM)


def gather_kernel(
    odd, count_hbm, rows_hbm, res_hbm, factor, sxa, sxb, sya, syb, field, ids, slab, count, rows, res, sem
):
    fetch_count = pltpu.make_async_copy(count_hbm, count, sem.at[0])
    fetch_rows = pltpu.make_async_copy(rows_hbm, rows, sem.at[1])
    fetch_res = pltpu.make_async_copy(res_hbm, res, sem.at[2])
    fetch_count.start()
    fetch_rows.start()
    fetch_res.start()
    fetch_slab = pltpu.make_async_copy(factor.at[0, 0, pl.ds(TAIL, 320), :], slab, sem.at[3])
    fetch_slab.start()
    lane = lax.broadcasted_iota(jnp.int32, (1, LANES), 1)
    fetch_count.wait()
    fetch_rows.wait()
    table = rows[0, 0]

    def live(n):
        return count[0, 0, n]

    def edge(n):
        return jnp.where(lane < live(n), table[n : n + 1], -1)

    def corner(base, n, at):
        moved = pltpu.roll(table, at, 1)[n : n + 1]
        return jnp.where((lane >= at) & (lane < at + live(n)), moved, base)

    down = corner(corner(edge(0), 4, 72), 5, 80)
    up = corner(corner(edge(1), 6, 76), 7, 84)
    right, left = edge(2), edge(3)
    lists = [
        pick(odd[0:1], down, up),
        pick(odd[0:1], up, down),
        pick(odd[1:2], right, left),
        pick(odd[1:2], left, right),
    ]
    for k, values in enumerate(lists + lists):
        ids[k : k + 1] = values
    own = res.shape[1]
    row = lax.broadcasted_iota(jnp.int32, (own, LANES), 0)
    ones = [jnp.where(row == values, 1.0, 0.0).astype(BF16) for values in lists]
    onehot = jnp.concatenate(ones, axis=1)
    fetch_res.wait()
    high, low = split(res[...])
    field[:96] = high
    field[96:] = low
    packed = dot(field[...], onehot, NN)
    packed = packed[:96] + packed[96:]
    for k, out in enumerate((sxa, sxb, sya, syb)):
        out[...] = packed[:, k * LANES : (k + 1) * LANES]
    fetch_slab.wait()


def halo_place():
    col = lax.broadcasted_iota(jnp.int32, (320, 4 * LANES), 0) - 16
    spot = lax.broadcasted_iota(jnp.int32, (1, 4 * LANES), 1)
    lane = spot % LANES
    block = spot // LANES
    source = jnp.where(lane < EDGE, block * EDGE + lane, -99)
    for n, b, at in ((4, 2, 72), (6, 2, 76), (5, 3, 80), (7, 3, 84)):
        inside = (block == b) & (lane >= at) & (lane < at + 4)
        source = jnp.where(inside, 4 * EDGE + (n - 4) * 4 + lane - at, source)
    return jnp.where(col == source, 1.0, 0.0).astype(BF16)


def fetch(pairs, sem):
    copies = [pltpu.make_async_copy(source, dest, sem.at[k]) for k, (source, dest) in enumerate(pairs)]
    for copy in copies:
        copy.start()
    return copies


def own_slab(factor, k):
    return factor.at[0, 0, pl.ds(256 * k, 256), pl.ds(0, 256 * (k + 1))]


def tail_kernel(
    field, slab, factor, ritz_hbm, search_hbm, part, ph, plo, th, tlo, oh, olo, ritz, search, slab0, slab1, slab2, sem
):
    slabs = [(own_slab(factor, k), dest) for k, dest in enumerate((slab0, slab1, slab2))]
    copies = fetch([(ritz_hbm, ritz), (search_hbm, search)] + slabs, sem)
    place = halo_place()
    own = field.shape[1]
    oh[...], olo[...] = split(slab[:, :own])
    part[...] = dot_pairs((field[:96], field[96:]), (oh[...], olo[...]), NT)
    for value, out, turned in zip(split(slab[:, TAIL:]), (ph, plo), (th, tlo)):
        placed = dot(value, place, NN)
        out[...] = placed.astype(BF16)
        turned[...] = placed.T.astype(BF16)
    for copy in copies:
        copy.wait()


def halo_kernel(odd, sxa, sxb, sya, syb, part, ph, plo, th, tlo, given, half, bxa, bxb, bya, byb):
    xa, xb, ya, yb = sxa[...], sxb[...], sya[...], syb[...]
    arrived = jnp.concatenate(
        [pick(odd[0:1], xb, xa), pick(odd[0:1], xa, xb), pick(odd[1:2], yb, ya), pick(odd[1:2], ya, yb)], axis=1
    )
    solved = part[...] + dot_pairs(split(arrived), (th[...], tlo[...]), NN)
    half[...] = solved
    back = dot_pairs(split(solved), (ph[...], plo[...]), NN)
    b = [back[:, k * LANES : (k + 1) * LANES] for k in range(4)]
    bxa[...] = pick(odd[0:1], b[1], b[0])
    bxb[...] = pick(odd[0:1], b[0], b[1])
    bya[:96] = pick(odd[1:2], b[3], b[2])
    bya[96:] = given[...]
    byb[...] = pick(odd[1:2], b[2], b[3])


def slab_term(field, slab):
    width = slab.shape[1]
    block = split(slab[...])
    solved = dot_pairs((field[:96, :width], field[96:, :width]), block, NT)
    return dot_pairs(split(solved), block, NN)


def body_kernel(field, slab0, slab1, slab2, slab3, factor, out, slab4, sem):
    (copy,) = fetch([(own_slab(factor, 4), slab4)], sem)
    out[:, :1024] = slab_term(field, slab3)
    for slab in (slab2, slab1, slab0):
        width = slab.shape[1]
        out[:, :width] = out[:, :width] + slab_term(field, slab)
    copy.wait()
    term = slab_term(field, slab4)
    out[:, :1024] = out[:, :1024] + term[:, :1024]
    out[:, 1024:] = term[:, 1024:]


def distinct_tiles(square):
    tiles = [square[32 * i : 32 * i + 32, 32 * j : 32 * j + 32] for i in range(3) for j in range(i, 3)]
    return jnp.concatenate(tiles, axis=0)


def whole_square(tiles):
    t = [tiles[32 * k : 32 * k + 32] for k in range(6)]
    blank = jnp.zeros((32, 32), F32)
    upper = jnp.concatenate(
        [
            jnp.concatenate([t[0], t[1], t[2]], axis=1),
            jnp.concatenate([blank, t[3], t[4]], axis=1),
            jnp.concatenate([blank, blank, t[5]], axis=1),
        ],
        axis=0,
    )
    row = lax.broadcasted_iota(jnp.int32, (96, 96), 0) // 32
    col = lax.broadcasted_iota(jnp.int32, (96, 96), 1) // 32
    return jnp.where(row <= col, upper, upper.T)


def side_kernel(
    odd, ids, ritz, search, factor, held, given, turned, same, sides_h, sides_l, rgh, rgl, slab3, sem
):
    copies = fetch([(own_slab(factor, 3), slab3)], sem)
    own = ritz.shape[1]
    numbers = ids[...].astype(F32)
    columns = numbers.T
    live = jnp.where(columns < 0.0, -2.0, columns)
    across = lax.broadcasted_iota(jnp.int32, (LANES, own), 1).astype(F32)
    for k in range(4):
        lanes = slice(k * LANES, (k + 1) * LANES)
        turned[lanes] = jnp.where(columns[:, k : k + 1] == across, 1.0, 0.0).astype(BF16)
        for j in range(4):
            agree = live[:, k : k + 1] == numbers[j : j + 1]
            same[lanes, j * LANES : (j + 1) * LANES] = jnp.where(agree, 1.0, 0.0).astype(BF16)
    blank = jnp.zeros((32, own), BF16)
    for r, s, out in zip(split(ritz[...]), split(search[...]), (sides_h, sides_l)):
        out[:96] = r
        out[96:128] = blank
        out[128:224] = s
        out[224:] = blank
    for side, out in zip((sides_h, sides_l), (rgh, rgl)):
        out[...] = dot(turned[...], side[...], NT).astype(BF16)
    pair = (sides_h[...], sides_l[...])
    cross = dot_pairs(pair, pair, NT)
    rr, sr, ss = cross[:96, :96], cross[128:224, :96], cross[128:224, LANES : LANES + 96]
    rt, st = distinct_tiles(rr), distinct_tiles(ss)
    first = jnp.concatenate([sr, rt[:96]], axis=1)
    second = jnp.concatenate([rt[96:], st[:96], st[96:], jnp.zeros((96, 32), F32)], axis=1)
    held[...] = pick(odd[1:2], first, second)
    given[...] = pick(odd[1:2], second, first)
    for copy in copies:
        copy.wait()


def local_kernel(own_part, half, oh, olo, turned, sides_h, sides_l, local, sent, base):
    add = dot_pairs(split(half[...]), (oh[...], olo[...]), NN)
    value = add + jnp.concatenate([own_part[...], jnp.zeros((96, add.shape[1] - TAIL), F32)], axis=1)
    local[...] = value
    pair = split(value)
    sent[...] = dot_exact(pair, turned[...], NT)
    base[:96] = dot_pairs(pair, pair, NT)
    cross = dot_pairs(pair, (sides_h[...], sides_l[...]), NT)
    base[96:192] = cross[:, :96]
    base[192:] = cross[:, LANES : LANES + 96]


def gram_kernel(odd, rxa, rxb, rya, ryb, same, sent, rgh, rgl, base, held, away, kept, back):
    back[...] = jnp.concatenate([rxa[...], rxb[...], rya[:96], ryb[...]], axis=1)
    pair = split(back[...])
    mixed = sent[...] + 0.5 * dot_exact(pair, same[...], NN)
    square = dot_pairs(split(mixed), pair, NT)
    cross = dot_pairs(pair, (rgh[...], rgl[...]), NN)
    pp = base[:96] + square + square.T
    pr = base[96:192] + cross[:, :96]
    ps = base[192:] + cross[:, LANES : LANES + 96]
    tiles = distinct_tiles(pp)
    first = jnp.concatenate([pr, tiles[:96]], axis=1)
    second = jnp.concatenate([ps, tiles[96:]], axis=1)
    kept[:96] = pick(odd[0:1], first, second)
    away[:96] = pick(odd[0:1], second, first)
    early = held[...] + rya[96:]
    kept[96:] = pick(odd[0:1], early[:48], early[48:])
    away[96:] = pick(odd[0:1], early[48:], early[:48])


def update_kernel(back, turned, local, precond):
    precond[...] = local[...] + dot_exact(split(back[...]), turned[...], NN)


def final_kernel(scale, odd, mine, other, out):
    def by_core(rows):
        a, b = mine[rows], other[rows]
        return pick(odd[0:1], a, b) * scale, pick(odd[0:1], b, a) * scale

    late = by_core(slice(0, 96))
    near, far = by_core(slice(96, 144)), by_core(slice(144, 192))
    near, far = jnp.concatenate(near, axis=0), jnp.concatenate(far, axis=0)
    first, second = pick(odd[1:2], near, far), pick(odd[1:2], far, near)
    pr, ps = late[0][:, :96], late[1][:, :96]
    pp = whole_square(jnp.concatenate([late[0][:, 96:], late[1][:, 96:]], axis=0))
    sr = first[:, :96]
    rr = whole_square(jnp.concatenate([first[:, 96:], second[:, :32]], axis=0))
    ss = whole_square(jnp.concatenate([second[:, 32:64], second[:, 64:96]], axis=0))
    out[0:96, :] = jnp.concatenate([rr, pr.T, sr.T], axis=1)
    out[96:192, :] = jnp.concatenate([pr, pp, ps], axis=1)
    out[192:288, :] = jnp.concatenate([sr, ps.T, ss], axis=1)


def swap(block, axis, step):
    return lax.ppermute(block, axis, [(i, i ^ step) for i in range(lax.axis_size(axis))])


def swap_odd(block, axis):
    size = lax.axis_size(axis)
    route = [(i, (i + 1) % size) for i in range(1, size, 2)]
    return lax.ppermute(block, axis, route + [(b, a) for a, b in route])


def body(residual, ritz_block, search_block, inverse_factor, send_rows, send_count):
    own = residual.shape[1]
    p, q = lax.axis_index("sx"), lax.axis_index("sy")
    odd = jnp.where(jnp.arange(8)[:, None] == 0, p % 2, q % 2) + jnp.zeros((8, LANES), jnp.int32)
    lane = jnp.arange(LANES)[None, :]
    msg = shaped(96, LANES)

    factor = in_hbm(inverse_factor)
    sxa, sxb, sya, syb, field, ids, slab = call(
        gather_kernel,
        (
            msg,
            msg,
            msg,
            msg,
            shaped(192, own, dtype=BF16),
            shaped(8, LANES, dtype=jnp.int32),
            shaped(320, 1600),
        ),
        [VMEM, HBM, HBM, HBM, HBM],
        [
            pltpu.SMEM((1, 1, 8), jnp.int32),
            pltpu.VMEM((1, 1, 8, LANES), jnp.int32),
            pltpu.VMEM((96, own), F32),
            pltpu.SemaphoreType.DMA((4,)),
        ],
        flops=2 * 192 * 1296 * 512,
        moved=2000000,
        name="gather",
    )(odd, in_hbm(send_count), in_hbm(send_rows), in_hbm(residual), factor)

    gxb, gxa = swap_odd(sxb, "sx"), swap(sxa, "sx", 1)

    placed, turned = shaped(320, 512, dtype=BF16), shaped(512, 320, dtype=BF16)
    wide = shaped(320, own, dtype=BF16)
    part, ph, plo, th, tlo, oh, olo, ritz, search, slab0, slab1, slab2 = call(
        tail_kernel,
        (shaped(96, 320), placed, placed, turned, turned, wide, wide)
        + (shaped(96, own), shaped(96, own), shaped(256, 256), shaped(256, 512), shaped(256, 768)),
        [VMEM, VMEM, HBM, HBM, HBM],
        [pltpu.SemaphoreType.DMA((5,))],
        flops=2 * 96 * 1296 * 320 * 3,
        moved=6000000,
        name="tail",
    )(field, slab, factor, in_hbm(ritz_block), in_hbm(search_block))
    gxa, gxb, part = lax.optimization_barrier((gxa, gxb, part))

    relay = jnp.where(lane >= EDGE, gxa + gxb, 0.0)
    gyb, gya = swap_odd(syb + relay, "sy"), swap(sya + relay, "sy", 1)

    sides, sent_sides = shaped(2 * LANES, own, dtype=BF16), shaped(512, 2 * LANES, dtype=BF16)
    held, given, turned, same, sides_h, sides_l, rgh, rgl, slab3 = call(
        side_kernel,
        (
            msg,
            msg,
            shaped(512, own, dtype=BF16),
            shaped(512, 512, dtype=BF16),
            sides,
            sides,
            sent_sides,
            sent_sides,
            shaped(256, 1024),
        ),
        [VMEM] + [VMEM] * 3 + [HBM],
        [pltpu.SemaphoreType.DMA((1,))],
        flops=2 * 192 * 256 * 1296 * 3,
        moved=3000000,
        name="side",
    )(odd, ids, ritz, search, factor)

    half, bxa, bxb, bya, byb = call(
        halo_kernel,
        (shaped(96, 320), msg, msg, shaped(192, LANES), msg),
        [VMEM] + [VMEM] * 10,
        flops=2 * 2 * 96 * 320 * 512 * 3,
        moved=1000000,
        name="halo",
    )(odd, gxa, gxb, gya, gyb, part, ph, plo, th, tlo, given)

    ryb, rya = swap_odd(byb, "sy"), swap(bya, "sy", 1)

    own_part = call(
        body_kernel,
        shaped(96, TAIL),
        [VMEM] * 5 + [HBM],
        [pltpu.VMEM((256, TAIL), F32), pltpu.SemaphoreType.DMA((1,))],
        flops=2 * 2 * 96 * 256 * 256 * 15 * 3,
        moved=4000000,
        name="body",
    )(field, slab0, slab1, slab2, slab3, factor)
    rya, ryb, own_part = lax.optimization_barrier((rya, ryb, own_part))

    relay = jnp.where(lane >= EDGE, rya[:96] + ryb, 0.0)
    rxb, rxa = swap_odd(bxb + relay, "sx"), swap(bxa + relay, "sx", 1)

    local, sent, base = call(
        local_kernel,
        (shaped(96, own), shaped(96, 512), shaped(288, 96)),
        [VMEM] * 7,
        flops=2 * 96 * 1296 * 1100 * 3,
        moved=4000000,
        name="local",
    )(own_part, half, oh, olo, turned, sides_h, sides_l)

    away, kept, back = call(
        gram_kernel,
        (shaped(144, LANES), shaped(144, LANES), shaped(96, 512)),
        [VMEM] + [VMEM] * 10,
        flops=2 * 96 * 512 * 900 * 3,
        moved=2000000,
        name="gram",
    )(odd, rxa, rxb, rya, ryb, same, sent, rgh, rgl, base, held)

    precond = call(
        update_kernel,
        shaped(96, own),
        [VMEM] * 3,
        flops=2 * 192 * 1296 * 512,
        moved=3000000,
        name="update",
    )(back, turned, local)

    def summed(value, axis, steps):
        total = value
        for step in steps:
            total = total + swap(value, axis, step)
        return total

    total = kept + swap(away, "sx", 1)
    total = summed(total, "sx", (2, 6, 4))
    total = summed(total, "sy", (8, 24, 16))
    total = summed(total, "sy", (6,))
    total, precond = lax.optimization_barrier((total, precond))
    three, two, one = (swap(total, "sy", step) for step in (3, 2, 1))
    late = (total[:96] + one[:96]) + (two[:96] + three[:96])
    mine = jnp.concatenate([late, total[96:] + two[96:], one[96:] + three[96:]], axis=0)
    other = swap(mine, "sx", 1)

    vertex_total = own * lax.axis_size("sx") * lax.axis_size("sy")

    def finish(odd, *refs):
        final_kernel(1.0 / vertex_total, odd, *refs)

    gram = call(
        finish,
        shaped(288, 288),
        [VMEM] + [VMEM] * 2,
        flops=1000000,
        moved=700000,
        name="final",
    )(odd, mine, other)
    return precond, gram


def solution(mesh):
    placed = (
        P(None, ("sx", "sy")),
        P(None, ("sx", "sy")),
        P(None, ("sx", "sy")),
        P("sx", "sy", None, None),
        P("sx", "sy", None, None),
        P("sx", "sy", None),
    )
    return jax.shard_map(
        body, mesh=mesh, in_specs=placed, out_specs=(P(None, ("sx", "sy")), P()), check_vma=False
    )
```

```python
import jax
import jax.numpy as jnp
from jax import lax
from jax.experimental import pallas as pl
from jax.experimental.pallas import tpu as pltpu
from jax.sharding import PartitionSpec as P

EDGE = 72
LANES = 128
TAIL = 1280
F32 = jnp.float32
BF16 = jnp.bfloat16
VMEM = pl.BlockSpec(memory_space=pltpu.VMEM)
HBM = pl.BlockSpec(memory_space=pl.ANY)
NN = (((1,), (0,)), ((), ()))
NT = (((1,), (1,)), ((), ()))


def split(value):
    high = value.astype(BF16)
    low = (value - high.astype(F32)).astype(BF16)
    return high, low


def dot(left, right, dims):
    return lax.dot_general(left, right, dims, preferred_element_type=F32)


def dot_pairs(left, right, dims):
    rows = left[0].shape[0]
    both = dot(jnp.concatenate(left, axis=0), right[0], dims)
    return both[:rows] + both[rows:] + dot(left[0], right[1], dims)


def dot_exact(left, right, dims):
    rows = left[0].shape[0]
    both = dot(jnp.concatenate(left, axis=0), right, dims)
    return both[:rows] + both[rows:]


def pick(flag, when_even, when_odd):
    return jnp.where(flag[:, : when_even.shape[1]] == 0, when_even, when_odd)


def call(kernel, out, in_specs, scratch=(), flops=0, moved=0, name=None, out_specs=None, limit=20):
    return pl.pallas_call(
        kernel,
        out_shape=out,
        in_specs=in_specs,
        out_specs=jax.tree.map(lambda _: VMEM, out) if out_specs is None else out_specs,
        scratch_shapes=list(scratch),
        compiler_params=pltpu.CompilerParams(vmem_limit_bytes=limit * 1024 * 1024),
        cost_estimate=pl.CostEstimate(flops=flops, bytes_accessed=moved, transcendentals=0),
        name=name,
    )


def shaped(*shape, dtype=F32):
    return jax.ShapeDtypeStruct(shape, dtype)


def in_hbm(value):
    return pltpu.with_memory_space_constraint(value, pltpu.HBM)


def gather_kernel(
    odd, count_hbm, rows_hbm, res_hbm, factor, sxa, sxb, sya, syb, field, ids, slab, count, rows, res, sem
):
    fetch_count = pltpu.make_async_copy(count_hbm, count, sem.at[0])
    fetch_rows = pltpu.make_async_copy(rows_hbm, rows, sem.at[1])
    fetch_res = pltpu.make_async_copy(res_hbm, res, sem.at[2])
    fetch_count.start()
    fetch_rows.start()
    fetch_res.start()
    fetch_slab = pltpu.make_async_copy(factor.at[0, 0, pl.ds(TAIL, 320), :], slab, sem.at[3])
    fetch_slab.start()
    lane = lax.broadcasted_iota(jnp.int32, (1, LANES), 1)
    fetch_count.wait()
    fetch_rows.wait()
    table = rows[0, 0]

    def live(n):
        return count[0, 0, n]

    def edge(n):
        return jnp.where(lane < live(n), table[n : n + 1], -1)

    def corner(base, n, at):
        moved = pltpu.roll(table, at, 1)[n : n + 1]
        return jnp.where((lane >= at) & (lane < at + live(n)), moved, base)

    down = corner(corner(edge(0), 4, 72), 5, 80)
    up = corner(corner(edge(1), 6, 76), 7, 84)
    right, left = edge(2), edge(3)
    lists = [
        pick(odd[0:1], down, up),
        pick(odd[0:1], up, down),
        pick(odd[1:2], right, left),
        pick(odd[1:2], left, right),
    ]
    for k, values in enumerate(lists + lists):
        ids[k : k + 1] = values
    own = res.shape[1]
    row = lax.broadcasted_iota(jnp.int32, (own, LANES), 0)
    ones = [jnp.where(row == values, 1.0, 0.0).astype(BF16) for values in lists]
    onehot = jnp.concatenate(ones, axis=1)
    fetch_res.wait()
    high, low = split(res[...])
    field[:96] = high
    field[96:] = low
    packed = dot(field[...], onehot, NN)
    packed = packed[:96] + packed[96:]
    for k, out in enumerate((sxa, sxb, sya, syb)):
        out[...] = packed[:, k * LANES : (k + 1) * LANES]
    fetch_slab.wait()


def halo_place():
    col = lax.broadcasted_iota(jnp.int32, (320, 4 * LANES), 0) - 16
    spot = lax.broadcasted_iota(jnp.int32, (1, 4 * LANES), 1)
    lane = spot % LANES
    block = spot // LANES
    source = jnp.where(lane < EDGE, block * EDGE + lane, -99)
    for n, b, at in ((4, 2, 72), (6, 2, 76), (5, 3, 80), (7, 3, 84)):
        inside = (block == b) & (lane >= at) & (lane < at + 4)
        source = jnp.where(inside, 4 * EDGE + (n - 4) * 4 + lane - at, source)
    return jnp.where(col == source, 1.0, 0.0).astype(BF16)


def fetch(pairs, sem):
    copies = [pltpu.make_async_copy(source, dest, sem.at[k]) for k, (source, dest) in enumerate(pairs)]
    for copy in copies:
        copy.start()
    return copies


def own_slab(factor, k):
    return factor.at[0, 0, pl.ds(256 * k, 256), pl.ds(0, 256 * (k + 1))]


def tail_kernel(
    field, slab, factor, ritz_hbm, search_hbm, part, ph, plo, th, tlo, oh, olo, ritz, search, slab0, slab1, slab2, sem
):
    slabs = [(own_slab(factor, k), dest) for k, dest in enumerate((slab0, slab1, slab2))]
    copies = fetch([(ritz_hbm, ritz), (search_hbm, search)] + slabs, sem)
    place = halo_place()
    own = field.shape[1]
    oh[...], olo[...] = split(slab[:, :own])
    part[...] = dot_pairs((field[:96], field[96:]), (oh[...], olo[...]), NT)
    for value, out, turned in zip(split(slab[:, TAIL:]), (ph, plo), (th, tlo)):
        placed = dot(value, place, NN)
        out[...] = placed.astype(BF16)
        turned[...] = placed.T.astype(BF16)
    for copy in copies:
        copy.wait()


def halo_kernel(odd, sxa, sxb, sya, syb, part, ph, plo, th, tlo, given, half, bxa, bxb, bya, byb):
    xa, xb, ya, yb = sxa[...], sxb[...], sya[...], syb[...]
    arrived = jnp.concatenate(
        [pick(odd[0:1], xb, xa), pick(odd[0:1], xa, xb), pick(odd[1:2], yb, ya), pick(odd[1:2], ya, yb)], axis=1
    )
    solved = part[...] + dot_pairs(split(arrived), (th[...], tlo[...]), NN)
    half[...] = solved
    back = dot_pairs(split(solved), (ph[...], plo[...]), NN)
    b = [back[:, k * LANES : (k + 1) * LANES] for k in range(4)]
    bxa[...] = pick(odd[0:1], b[1], b[0])
    bxb[...] = pick(odd[0:1], b[0], b[1])
    bya[:96] = pick(odd[1:2], b[3], b[2])
    bya[96:] = given[...]
    byb[...] = pick(odd[1:2], b[2], b[3])


def slab_term(field, slab):
    width = slab.shape[1]
    block = split(slab[...])
    solved = dot_pairs((field[:96, :width], field[96:, :width]), block, NT)
    return dot_pairs(split(solved), block, NN)


def head_kernel(field, slab0, slab1, slab2, out):
    out[...] = slab_term(field, slab2)
    for slab in (slab1, slab0):
        width = slab.shape[1]
        out[:, :width] = out[:, :width] + slab_term(field, slab)


def last_kernel(field, slab3, head, factor, out, slab4, sem):
    (copy,) = fetch([(own_slab(factor, 4), slab4)], sem)
    out[:, :1024] = slab_term(field, slab3)
    out[:, :768] = out[:, :768] + head[...]
    copy.wait()
    term = slab_term(field, slab4)
    out[:, :1024] = out[:, :1024] + term[:, :1024]
    out[:, 1024:] = term[:, 1024:]


def distinct_tiles(square):
    tiles = [square[32 * i : 32 * i + 32, 32 * j : 32 * j + 32] for i in range(3) for j in range(i, 3)]
    return jnp.concatenate(tiles, axis=0)


def whole_square(tiles):
    t = [tiles[32 * k : 32 * k + 32] for k in range(6)]
    blank = jnp.zeros((32, 32), F32)
    upper = jnp.concatenate(
        [
            jnp.concatenate([t[0], t[1], t[2]], axis=1),
            jnp.concatenate([blank, t[3], t[4]], axis=1),
            jnp.concatenate([blank, blank, t[5]], axis=1),
        ],
        axis=0,
    )
    row = lax.broadcasted_iota(jnp.int32, (96, 96), 0) // 32
    col = lax.broadcasted_iota(jnp.int32, (96, 96), 1) // 32
    return jnp.where(row <= col, upper, upper.T)


def side_kernel(
    odd, ids, ritz, search, factor, held, given, turned, same, sides_h, sides_l, rgh, rgl, slab3, sem
):
    copies = fetch([(own_slab(factor, 3), slab3)], sem)
    own = ritz.shape[1]
    numbers = ids[...].astype(F32)
    columns = numbers.T
    live = jnp.where(columns < 0.0, -2.0, columns)
    across = lax.broadcasted_iota(jnp.int32, (LANES, own), 1).astype(F32)
    for k in range(4):
        lanes = slice(k * LANES, (k + 1) * LANES)
        turned[lanes] = jnp.where(columns[:, k : k + 1] == across, 1.0, 0.0).astype(BF16)
        for j in range(4):
            agree = live[:, k : k + 1] == numbers[j : j + 1]
            same[lanes, j * LANES : (j + 1) * LANES] = jnp.where(agree, 1.0, 0.0).astype(BF16)
    blank = jnp.zeros((32, own), BF16)
    for r, s, out in zip(split(ritz[...]), split(search[...]), (sides_h, sides_l)):
        out[:96] = r
        out[96:128] = blank
        out[128:224] = s
        out[224:] = blank
    for side, out in zip((sides_h, sides_l), (rgh, rgl)):
        out[...] = dot(turned[...], side[...], NT).astype(BF16)
    pair = (sides_h[...], sides_l[...])
    cross = dot_pairs(pair, pair, NT)
    rr, sr, ss = cross[:96, :96], cross[128:224, :96], cross[128:224, LANES : LANES + 96]
    rt, st = distinct_tiles(rr), distinct_tiles(ss)
    first = jnp.concatenate([sr, rt[:96]], axis=1)
    second = jnp.concatenate([rt[96:], st[:96], st[96:], jnp.zeros((96, 32), F32)], axis=1)
    held[...] = pick(odd[1:2], first, second)
    given[...] = pick(odd[1:2], second, first)
    for copy in copies:
        copy.wait()


def local_kernel(own_part, half, oh, olo, turned, sides_h, sides_l, local, sent, base):
    add = dot_pairs(split(half[...]), (oh[...], olo[...]), NN)
    value = add + jnp.concatenate([own_part[...], jnp.zeros((96, add.shape[1] - TAIL), F32)], axis=1)
    local[...] = value
    pair = split(value)
    sent[...] = dot_exact(pair, turned[...], NT)
    base[:96] = dot_pairs(pair, pair, NT)
    cross = dot_pairs(pair, (sides_h[...], sides_l[...]), NT)
    base[96:192] = cross[:, :96]
    base[192:] = cross[:, LANES : LANES + 96]


def gram_kernel(odd, rxa, rxb, rya, ryb, same, sent, rgh, rgl, base, held, away, kept, back):
    back[...] = jnp.concatenate([rxa[...], rxb[...], rya[:96], ryb[...]], axis=1)
    pair = split(back[...])
    mixed = sent[...] + 0.5 * dot_exact(pair, same[...], NN)
    square = dot_pairs(split(mixed), pair, NT)
    cross = dot_pairs(pair, (rgh[...], rgl[...]), NN)
    pp = base[:96] + square + square.T
    pr = base[96:192] + cross[:, :96]
    ps = base[192:] + cross[:, LANES : LANES + 96]
    tiles = distinct_tiles(pp)
    first = jnp.concatenate([pr, tiles[:96]], axis=1)
    second = jnp.concatenate([ps, tiles[96:]], axis=1)
    kept[:96] = pick(odd[0:1], first, second)
    away[:96] = pick(odd[0:1], second, first)
    early = held[...] + rya[96:]
    kept[96:] = pick(odd[0:1], early[:48], early[48:])
    away[96:] = pick(odd[0:1], early[48:], early[:48])


def update_kernel(back, turned, local, precond):
    precond[...] = local[...] + dot_exact(split(back[...]), turned[...], NN)


def final_kernel(scale, odd, mine, other, out):
    def by_core(rows):
        a, b = mine[rows], other[rows]
        return pick(odd[0:1], a, b) * scale, pick(odd[0:1], b, a) * scale

    late = by_core(slice(0, 96))
    near, far = by_core(slice(96, 144)), by_core(slice(144, 192))
    near, far = jnp.concatenate(near, axis=0), jnp.concatenate(far, axis=0)
    first, second = pick(odd[1:2], near, far), pick(odd[1:2], far, near)
    pr, ps = late[0][:, :96], late[1][:, :96]
    pp = whole_square(jnp.concatenate([late[0][:, 96:], late[1][:, 96:]], axis=0))
    sr = first[:, :96]
    rr = whole_square(jnp.concatenate([first[:, 96:], second[:, :32]], axis=0))
    ss = whole_square(jnp.concatenate([second[:, 32:64], second[:, 64:96]], axis=0))
    out[0:96, :] = jnp.concatenate([rr, pr.T, sr.T], axis=1)
    out[96:192, :] = jnp.concatenate([pr, pp, ps], axis=1)
    out[192:288, :] = jnp.concatenate([sr, ps.T, ss], axis=1)


def swap(block, axis, step):
    return lax.ppermute(block, axis, [(i, i ^ step) for i in range(lax.axis_size(axis))])


def swap_odd(block, axis):
    size = lax.axis_size(axis)
    route = [(i, (i + 1) % size) for i in range(1, size, 2)]
    return lax.ppermute(block, axis, route + [(b, a) for a, b in route])


def body(residual, ritz_block, search_block, inverse_factor, send_rows, send_count):
    own = residual.shape[1]
    p, q = lax.axis_index("sx"), lax.axis_index("sy")
    odd = jnp.where(jnp.arange(8)[:, None] == 0, p % 2, q % 2) + jnp.zeros((8, LANES), jnp.int32)
    lane = jnp.arange(LANES)[None, :]
    msg = shaped(96, LANES)

    factor = in_hbm(inverse_factor)
    sxa, sxb, sya, syb, field, ids, slab = call(
        gather_kernel,
        (
            msg,
            msg,
            msg,
            msg,
            shaped(192, own, dtype=BF16),
            shaped(8, LANES, dtype=jnp.int32),
            shaped(320, 1600),
        ),
        [VMEM, HBM, HBM, HBM, HBM],
        [
            pltpu.SMEM((1, 1, 8), jnp.int32),
            pltpu.VMEM((1, 1, 8, LANES), jnp.int32),
            pltpu.VMEM((96, own), F32),
            pltpu.SemaphoreType.DMA((4,)),
        ],
        flops=2 * 192 * 1296 * 512,
        moved=2000000,
        name="gather",
    )(odd, in_hbm(send_count), in_hbm(send_rows), in_hbm(residual), factor)

    gxb, gxa = swap_odd(sxb, "sx"), swap(sxa, "sx", 1)

    placed, turned = shaped(320, 512, dtype=BF16), shaped(512, 320, dtype=BF16)
    wide = shaped(320, own, dtype=BF16)
    part, ph, plo, th, tlo, oh, olo, ritz, search, slab0, slab1, slab2 = call(
        tail_kernel,
        (shaped(96, 320), placed, placed, turned, turned, wide, wide)
        + (shaped(96, own), shaped(96, own), shaped(256, 256), shaped(256, 512), shaped(256, 768)),
        [VMEM, VMEM, HBM, HBM, HBM],
        [pltpu.SemaphoreType.DMA((5,))],
        flops=2 * 96 * 1296 * 320 * 3,
        moved=6000000,
        name="tail",
    )(field, slab, factor, in_hbm(ritz_block), in_hbm(search_block))
    gxa, gxb, part = lax.optimization_barrier((gxa, gxb, part))

    relay = jnp.where(lane >= EDGE, gxa + gxb, 0.0)
    gyb, gya = swap_odd(syb + relay, "sy"), swap(sya + relay, "sy", 1)

    sides, sent_sides = shaped(2 * LANES, own, dtype=BF16), shaped(512, 2 * LANES, dtype=BF16)
    held, given, turned, same, sides_h, sides_l, rgh, rgl, slab3 = call(
        side_kernel,
        (
            msg,
            msg,
            shaped(512, own, dtype=BF16),
            shaped(512, 512, dtype=BF16),
            sides,
            sides,
            sent_sides,
            sent_sides,
            shaped(256, 1024),
        ),
        [VMEM] + [VMEM] * 3 + [HBM],
        [pltpu.SemaphoreType.DMA((1,))],
        flops=2 * 192 * 256 * 1296 * 3,
        moved=3000000,
        name="side",
    )(odd, ids, ritz, search, factor)

    head = call(
        head_kernel,
        shaped(96, 768),
        [VMEM] * 4,
        flops=2 * 2 * 96 * 256 * 256 * 6 * 3,
        moved=2500000,
        name="head",
    )(field, slab0, slab1, slab2)
    gya, gyb, head = lax.optimization_barrier((gya, gyb, head))

    half, bxa, bxb, bya, byb = call(
        halo_kernel,
        (shaped(96, 320), msg, msg, shaped(192, LANES), msg),
        [VMEM] + [VMEM] * 10,
        flops=2 * 2 * 96 * 320 * 512 * 3,
        moved=1000000,
        name="halo",
    )(odd, gxa, gxb, gya, gyb, part, ph, plo, th, tlo, given)

    ryb, rya = swap_odd(byb, "sy"), swap(bya, "sy", 1)

    own_part = call(
        last_kernel,
        shaped(96, TAIL),
        [VMEM] * 3 + [HBM],
        [pltpu.VMEM((256, TAIL), F32), pltpu.SemaphoreType.DMA((1,))],
        flops=2 * 2 * 96 * 256 * 256 * 9 * 3,
        moved=3000000,
        name="last",
    )(field, slab3, head, factor)
    rya, ryb, own_part = lax.optimization_barrier((rya, ryb, own_part))

    relay = jnp.where(lane >= EDGE, rya[:96] + ryb, 0.0)
    rxb, rxa = swap_odd(bxb + relay, "sx"), swap(bxa + relay, "sx", 1)

    local, sent, base = call(
        local_kernel,
        (shaped(96, own), shaped(96, 512), shaped(288, 96)),
        [VMEM] * 7,
        flops=2 * 96 * 1296 * 1100 * 3,
        moved=4000000,
        name="local",
    )(own_part, half, oh, olo, turned, sides_h, sides_l)

    away, kept, back = call(
        gram_kernel,
        (shaped(144, LANES), shaped(144, LANES), shaped(96, 512)),
        [VMEM] + [VMEM] * 10,
        flops=2 * 96 * 512 * 900 * 3,
        moved=2000000,
        name="gram",
    )(odd, rxa, rxb, rya, ryb, same, sent, rgh, rgl, base, held)

    precond = call(
        update_kernel,
        shaped(96, own),
        [VMEM] * 3,
        flops=2 * 192 * 1296 * 512,
        moved=3000000,
        name="update",
    )(back, turned, local)

    def summed(value, axis, steps):
        total = swap(value, axis, steps[0])
        for step in steps[1:]:
            total = total + swap(value, axis, step)
        return value + total

    total = kept + swap(away, "sx", 1)
    total = summed(total, "sx", (2, 6, 4))
    total = summed(total, "sy", (8, 24, 16))
    total = summed(total, "sy", (6,))
    total, precond = lax.optimization_barrier((total, precond))
    three, two, one = (swap(total, "sy", step) for step in (3, 2, 1))
    late = (total[:96] + one[:96]) + (two[:96] + three[:96])
    mine = jnp.concatenate([late, total[96:] + two[96:], one[96:] + three[96:]], axis=0)
    other = swap(mine, "sx", 1)

    vertex_total = own * lax.axis_size("sx") * lax.axis_size("sy")

    def finish(odd, *refs):
        final_kernel(1.0 / vertex_total, odd, *refs)

    gram = call(
        finish,
        shaped(288, 288),
        [VMEM] + [VMEM] * 2,
        flops=1000000,
        moved=700000,
        name="final",
    )(odd, mine, other)
    return precond, gram


def solution(mesh):
    placed = (
        P(None, ("sx", "sy")),
        P(None, ("sx", "sy")),
        P(None, ("sx", "sy")),
        P("sx", "sy", None, None),
        P("sx", "sy", None, None),
        P("sx", "sy", None),
    )
    return jax.shard_map(
        body, mesh=mesh, in_specs=placed, out_specs=(P(None, ("sx", "sy")), P()), check_vma=False
    )
```

```python
import jax
import jax.numpy as jnp
from jax import lax
from jax.experimental import pallas as pl
from jax.experimental.pallas import tpu as pltpu
from jax.sharding import PartitionSpec as P

EDGE = 72
LANES = 128
TAIL = 1280
F32 = jnp.float32
BF16 = jnp.bfloat16
VMEM = pl.BlockSpec(memory_space=pltpu.VMEM)
HBM = pl.BlockSpec(memory_space=pl.ANY)
NN = (((1,), (0,)), ((), ()))
NT = (((1,), (1,)), ((), ()))


def split(value):
    high = value.astype(BF16)
    low = (value - high.astype(F32)).astype(BF16)
    return high, low


def dot(left, right, dims):
    return lax.dot_general(left, right, dims, preferred_element_type=F32)


def dot_pairs(left, right, dims):
    rows = left[0].shape[0]
    both = dot(jnp.concatenate(left, axis=0), right[0], dims)
    return both[:rows] + both[rows:] + dot(left[0], right[1], dims)


def dot_exact(left, right, dims):
    rows = left[0].shape[0]
    both = dot(jnp.concatenate(left, axis=0), right, dims)
    return both[:rows] + both[rows:]


def pick(flag, when_even, when_odd):
    return jnp.where(flag[:, : when_even.shape[1]] == 0, when_even, when_odd)


def call(kernel, out, in_specs, scratch=(), flops=0, moved=0, name=None, out_specs=None, limit=20):
    return pl.pallas_call(
        kernel,
        out_shape=out,
        in_specs=in_specs,
        out_specs=jax.tree.map(lambda _: VMEM, out) if out_specs is None else out_specs,
        scratch_shapes=list(scratch),
        compiler_params=pltpu.CompilerParams(vmem_limit_bytes=limit * 1024 * 1024),
        cost_estimate=pl.CostEstimate(flops=flops, bytes_accessed=moved, transcendentals=0),
        name=name,
    )


def shaped(*shape, dtype=F32):
    return jax.ShapeDtypeStruct(shape, dtype)


def in_hbm(value):
    return pltpu.with_memory_space_constraint(value, pltpu.HBM)


def gather_kernel(
    odd, count_hbm, rows_hbm, res_hbm, factor, sxa, sxb, sya, syb, field, ids, slab, count, rows, res, sem
):
    fetch_count = pltpu.make_async_copy(count_hbm, count, sem.at[0])
    fetch_rows = pltpu.make_async_copy(rows_hbm, rows, sem.at[1])
    fetch_res = pltpu.make_async_copy(res_hbm, res, sem.at[2])
    fetch_count.start()
    fetch_rows.start()
    fetch_res.start()
    fetch_slab = pltpu.make_async_copy(factor.at[0, 0, pl.ds(TAIL, 320), :], slab, sem.at[3])
    fetch_slab.start()
    lane = lax.broadcasted_iota(jnp.int32, (1, LANES), 1)
    fetch_count.wait()
    fetch_rows.wait()
    table = rows[0, 0]

    def live(n):
        return count[0, 0, n]

    def edge(n):
        return jnp.where(lane < live(n), table[n : n + 1], -1)

    def corner(base, n, at):
        moved = pltpu.roll(table, at, 1)[n : n + 1]
        return jnp.where((lane >= at) & (lane < at + live(n)), moved, base)

    down = corner(corner(edge(0), 4, 72), 5, 80)
    up = corner(corner(edge(1), 6, 76), 7, 84)
    right, left = edge(2), edge(3)
    lists = [
        pick(odd[0:1], down, up),
        pick(odd[0:1], up, down),
        pick(odd[1:2], right, left),
        pick(odd[1:2], left, right),
    ]
    for k, values in enumerate(lists + lists):
        ids[k : k + 1] = values
    own = res.shape[1]
    row = lax.broadcasted_iota(jnp.int32, (own, LANES), 0)
    ones = [jnp.where(row == values, 1.0, 0.0).astype(BF16) for values in lists]
    onehot = jnp.concatenate(ones, axis=1)
    fetch_res.wait()
    high, low = split(res[...])
    field[:96] = high
    field[96:] = low
    packed = dot(field[...], onehot, NN)
    packed = packed[:96] + packed[96:]
    for k, out in enumerate((sxa, sxb, sya, syb)):
        out[...] = packed[:, k * LANES : (k + 1) * LANES]
    fetch_slab.wait()


def halo_place():
    col = lax.broadcasted_iota(jnp.int32, (320, 4 * LANES), 0) - 16
    spot = lax.broadcasted_iota(jnp.int32, (1, 4 * LANES), 1)
    lane = spot % LANES
    block = spot // LANES
    source = jnp.where(lane < EDGE, block * EDGE + lane, -99)
    for n, b, at in ((4, 2, 72), (6, 2, 76), (5, 3, 80), (7, 3, 84)):
        inside = (block == b) & (lane >= at) & (lane < at + 4)
        source = jnp.where(inside, 4 * EDGE + (n - 4) * 4 + lane - at, source)
    return jnp.where(col == source, 1.0, 0.0).astype(BF16)


def fetch(pairs, sem):
    copies = [pltpu.make_async_copy(source, dest, sem.at[k]) for k, (source, dest) in enumerate(pairs)]
    for copy in copies:
        copy.start()
    return copies


def own_slab(factor, k):
    return factor.at[0, 0, pl.ds(256 * k, 256), pl.ds(0, 256 * (k + 1))]


def tail_kernel(
    field, slab, factor, ritz_hbm, search_hbm, part, ph, plo, th, tlo, oh, olo, ritz, search, slab0, slab1, slab2, sem
):
    slabs = [(own_slab(factor, k), dest) for k, dest in enumerate((slab0, slab1, slab2))]
    copies = fetch([(ritz_hbm, ritz), (search_hbm, search)] + slabs, sem)
    place = halo_place()
    own = field.shape[1]
    oh[...], olo[...] = split(slab[:, :own])
    part[...] = dot_pairs((field[:96], field[96:]), (oh[...], olo[...]), NT)
    for value, out, turned in zip(split(slab[:, TAIL:]), (ph, plo), (th, tlo)):
        placed = dot(value, place, NN)
        out[...] = placed.astype(BF16)
        turned[...] = placed.T.astype(BF16)
    for copy in copies:
        copy.wait()


def halo_kernel(odd, sxa, sxb, sya, syb, part, ph, plo, th, tlo, given, half, bxa, bxb, bya, byb):
    xa, xb, ya, yb = sxa[...], sxb[...], sya[...], syb[...]
    arrived = jnp.concatenate(
        [pick(odd[0:1], xb, xa), pick(odd[0:1], xa, xb), pick(odd[1:2], yb, ya), pick(odd[1:2], ya, yb)], axis=1
    )
    solved = part[...] + dot_pairs(split(arrived), (th[...], tlo[...]), NN)
    half[...] = solved
    back = dot_pairs(split(solved), (ph[...], plo[...]), NN)
    b = [back[:, k * LANES : (k + 1) * LANES] for k in range(4)]
    bxa[...] = pick(odd[0:1], b[1], b[0])
    bxb[...] = pick(odd[0:1], b[0], b[1])
    bya[:96] = pick(odd[1:2], b[3], b[2])
    bya[96:] = given[...]
    byb[...] = pick(odd[1:2], b[2], b[3])


def slab_term(field, slab):
    width = slab.shape[1]
    block = split(slab[...])
    solved = dot_pairs((field[:96, :width], field[96:, :width]), block, NT)
    return dot_pairs(split(solved), block, NN)


def head_kernel(field, slab0, slab1, out):
    out[...] = slab_term(field, slab1)
    out[:, :256] = out[:, :256] + slab_term(field, slab0)


def last_kernel(field, slab2, slab3, head, factor, out, slab4, sem):
    (copy,) = fetch([(own_slab(factor, 4), slab4)], sem)
    out[:, :1024] = slab_term(field, slab3)
    out[:, :768] = out[:, :768] + slab_term(field, slab2)
    out[:, :512] = out[:, :512] + head[...]
    copy.wait()
    term = slab_term(field, slab4)
    out[:, :1024] = out[:, :1024] + term[:, :1024]
    out[:, 1024:] = term[:, 1024:]


def distinct_tiles(square):
    tiles = [square[32 * i : 32 * i + 32, 32 * j : 32 * j + 32] for i in range(3) for j in range(i, 3)]
    return jnp.concatenate(tiles, axis=0)


def whole_square(tiles):
    t = [tiles[32 * k : 32 * k + 32] for k in range(6)]
    blank = jnp.zeros((32, 32), F32)
    upper = jnp.concatenate(
        [
            jnp.concatenate([t[0], t[1], t[2]], axis=1),
            jnp.concatenate([blank, t[3], t[4]], axis=1),
            jnp.concatenate([blank, blank, t[5]], axis=1),
        ],
        axis=0,
    )
    row = lax.broadcasted_iota(jnp.int32, (96, 96), 0) // 32
    col = lax.broadcasted_iota(jnp.int32, (96, 96), 1) // 32
    return jnp.where(row <= col, upper, upper.T)


def side_kernel(
    odd, ids, ritz, search, factor, held, given, turned, same, sides_h, sides_l, rgh, rgl, slab3, sem
):
    copies = fetch([(own_slab(factor, 3), slab3)], sem)
    own = ritz.shape[1]
    numbers = ids[...].astype(F32)
    columns = numbers.T
    live = jnp.where(columns < 0.0, -2.0, columns)
    across = lax.broadcasted_iota(jnp.int32, (LANES, own), 1).astype(F32)
    for k in range(4):
        lanes = slice(k * LANES, (k + 1) * LANES)
        turned[lanes] = jnp.where(columns[:, k : k + 1] == across, 1.0, 0.0).astype(BF16)
        for j in range(4):
            agree = live[:, k : k + 1] == numbers[j : j + 1]
            same[lanes, j * LANES : (j + 1) * LANES] = jnp.where(agree, 1.0, 0.0).astype(BF16)
    blank = jnp.zeros((32, own), BF16)
    for r, s, out in zip(split(ritz[...]), split(search[...]), (sides_h, sides_l)):
        out[:96] = r
        out[96:128] = blank
        out[128:224] = s
        out[224:] = blank
    for side, out in zip((sides_h, sides_l), (rgh, rgl)):
        out[...] = dot(turned[...], side[...], NT).astype(BF16)
    pair = (sides_h[...], sides_l[...])
    cross = dot_pairs(pair, pair, NT)
    rr, sr, ss = cross[:96, :96], cross[128:224, :96], cross[128:224, LANES : LANES + 96]
    rt, st = distinct_tiles(rr), distinct_tiles(ss)
    first = jnp.concatenate([sr, rt[:96]], axis=1)
    second = jnp.concatenate([rt[96:], st[:96], st[96:], jnp.zeros((96, 32), F32)], axis=1)
    held[...] = pick(odd[1:2], first, second)
    given[...] = pick(odd[1:2], second, first)
    for copy in copies:
        copy.wait()


def local_kernel(own_part, half, oh, olo, turned, sides_h, sides_l, local, sent, base):
    add = dot_pairs(split(half[...]), (oh[...], olo[...]), NN)
    value = add + jnp.concatenate([own_part[...], jnp.zeros((96, add.shape[1] - TAIL), F32)], axis=1)
    local[...] = value
    pair = split(value)
    sent[...] = dot_exact(pair, turned[...], NT)
    base[:96] = dot_pairs(pair, pair, NT)
    cross = dot_pairs(pair, (sides_h[...], sides_l[...]), NT)
    base[96:192] = cross[:, :96]
    base[192:] = cross[:, LANES : LANES + 96]


def gram_kernel(odd, rxa, rxb, rya, ryb, same, sent, rgh, rgl, base, held, away, kept, back):
    back[...] = jnp.concatenate([rxa[...], rxb[...], rya[:96], ryb[...]], axis=1)
    pair = split(back[...])
    mixed = sent[...] + 0.5 * dot_exact(pair, same[...], NN)
    square = dot_pairs(split(mixed), pair, NT)
    cross = dot_pairs(pair, (rgh[...], rgl[...]), NN)
    pp = base[:96] + square + square.T
    pr = base[96:192] + cross[:, :96]
    ps = base[192:] + cross[:, LANES : LANES + 96]
    tiles = distinct_tiles(pp)
    first = jnp.concatenate([pr, tiles[:96]], axis=1)
    second = jnp.concatenate([ps, tiles[96:]], axis=1)
    kept[:96] = pick(odd[0:1], first, second)
    away[:96] = pick(odd[0:1], second, first)
    early = held[...] + rya[96:]
    kept[96:] = pick(odd[0:1], early[:48], early[48:])
    away[96:] = pick(odd[0:1], early[48:], early[:48])


def update_kernel(back, turned, local, precond):
    precond[...] = local[...] + dot_exact(split(back[...]), turned[...], NN)


def final_kernel(scale, odd, mine, other, gram, out, sem):
    def by_core(rows):
        a, b = mine[rows], other[rows]
        return pick(odd[0:1], a, b) * scale, pick(odd[0:1], b, a) * scale

    late = by_core(slice(0, 96))
    near, far = by_core(slice(96, 144)), by_core(slice(144, 192))
    near, far = jnp.concatenate(near, axis=0), jnp.concatenate(far, axis=0)
    first, second = pick(odd[1:2], near, far), pick(odd[1:2], far, near)
    pr, ps = late[0][:, :96], late[1][:, :96]
    pp = whole_square(jnp.concatenate([late[0][:, 96:], late[1][:, 96:]], axis=0))
    sr = first[:, :96]
    rr = whole_square(jnp.concatenate([first[:, 96:], second[:, :32]], axis=0))
    ss = whole_square(jnp.concatenate([second[:, 32:64], second[:, 64:96]], axis=0))
    copies = []
    bands = ([pr, pp, ps], [rr, pr.T, sr.T], [sr, ps.T, ss])
    for k, parts in zip((1, 0, 2), bands):
        rows = slice(96 * k, 96 * (k + 1))
        out[rows] = jnp.concatenate(parts, axis=1)
        copies.append(pltpu.make_async_copy(out.at[rows], gram.at[rows], sem.at[k]))
        copies[-1].start()
    for copy in copies:
        copy.wait()


def swap(block, axis, step):
    return lax.ppermute(block, axis, [(i, i ^ step) for i in range(lax.axis_size(axis))])


def swap_odd(block, axis):
    size = lax.axis_size(axis)
    route = [(i, (i + 1) % size) for i in range(1, size, 2)]
    return lax.ppermute(block, axis, route + [(b, a) for a, b in route])


def body(residual, ritz_block, search_block, inverse_factor, send_rows, send_count):
    own = residual.shape[1]
    p, q = lax.axis_index("sx"), lax.axis_index("sy")
    odd = jnp.where(jnp.arange(8)[:, None] == 0, p % 2, q % 2) + jnp.zeros((8, LANES), jnp.int32)
    lane = jnp.arange(LANES)[None, :]
    msg = shaped(96, LANES)

    factor = in_hbm(inverse_factor)
    sxa, sxb, sya, syb, field, ids, slab = call(
        gather_kernel,
        (
            msg,
            msg,
            msg,
            msg,
            shaped(192, own, dtype=BF16),
            shaped(8, LANES, dtype=jnp.int32),
            shaped(320, 1600),
        ),
        [VMEM, HBM, HBM, HBM, HBM],
        [
            pltpu.SMEM((1, 1, 8), jnp.int32),
            pltpu.VMEM((1, 1, 8, LANES), jnp.int32),
            pltpu.VMEM((96, own), F32),
            pltpu.SemaphoreType.DMA((4,)),
        ],
        flops=2 * 192 * 1296 * 512,
        moved=2000000,
        name="gather",
    )(odd, in_hbm(send_count), in_hbm(send_rows), in_hbm(residual), factor)

    gxb, gxa = swap_odd(sxb, "sx"), swap(sxa, "sx", 1)

    placed, turned = shaped(320, 512, dtype=BF16), shaped(512, 320, dtype=BF16)
    wide = shaped(320, own, dtype=BF16)
    part, ph, plo, th, tlo, oh, olo, ritz, search, slab0, slab1, slab2 = call(
        tail_kernel,
        (shaped(96, 320), placed, placed, turned, turned, wide, wide)
        + (shaped(96, own), shaped(96, own), shaped(256, 256), shaped(256, 512), shaped(256, 768)),
        [VMEM, VMEM, HBM, HBM, HBM],
        [pltpu.SemaphoreType.DMA((5,))],
        flops=2 * 96 * 1296 * 320 * 3,
        moved=6000000,
        name="tail",
    )(field, slab, factor, in_hbm(ritz_block), in_hbm(search_block))
    gxa, gxb, part = lax.optimization_barrier((gxa, gxb, part))

    relay = jnp.where(lane >= EDGE, gxa + gxb, 0.0)
    gyb, gya = swap_odd(syb + relay, "sy"), swap(sya + relay, "sy", 1)

    sides, sent_sides = shaped(2 * LANES, own, dtype=BF16), shaped(512, 2 * LANES, dtype=BF16)
    held, given, turned, same, sides_h, sides_l, rgh, rgl, slab3 = call(
        side_kernel,
        (
            msg,
            msg,
            shaped(512, own, dtype=BF16),
            shaped(512, 512, dtype=BF16),
            sides,
            sides,
            sent_sides,
            sent_sides,
            shaped(256, 1024),
        ),
        [VMEM] + [VMEM] * 3 + [HBM],
        [pltpu.SemaphoreType.DMA((1,))],
        flops=2 * 192 * 256 * 1296 * 3,
        moved=3000000,
        name="side",
    )(odd, ids, ritz, search, factor)

    head = call(
        head_kernel,
        shaped(96, 512),
        [VMEM] * 3,
        flops=2 * 2 * 96 * 256 * 256 * 3 * 3,
        moved=1200000,
        name="head",
    )(field, slab0, slab1)
    gya, gyb, head = lax.optimization_barrier((gya, gyb, head))

    half, bxa, bxb, bya, byb = call(
        halo_kernel,
        (shaped(96, 320), msg, msg, shaped(192, LANES), msg),
        [VMEM] + [VMEM] * 10,
        flops=2 * 2 * 96 * 320 * 512 * 3,
        moved=1000000,
        name="halo",
    )(odd, gxa, gxb, gya, gyb, part, ph, plo, th, tlo, given)

    ryb, rya = swap_odd(byb, "sy"), swap(bya, "sy", 1)

    own_part = call(
        last_kernel,
        shaped(96, TAIL),
        [VMEM] * 4 + [HBM],
        [pltpu.VMEM((256, TAIL), F32), pltpu.SemaphoreType.DMA((1,))],
        flops=2 * 2 * 96 * 256 * 256 * 12 * 3,
        moved=3000000,
        name="last",
    )(field, slab2, slab3, head, factor)
    rya, ryb, own_part = lax.optimization_barrier((rya, ryb, own_part))

    relay = jnp.where(lane >= EDGE, rya[:96] + ryb, 0.0)
    rxb, rxa = swap_odd(bxb + relay, "sx"), swap(bxa + relay, "sx", 1)

    local, sent, base = call(
        local_kernel,
        (shaped(96, own), shaped(96, 512), shaped(288, 96)),
        [VMEM] * 7,
        flops=2 * 96 * 1296 * 1100 * 3,
        moved=4000000,
        name="local",
    )(own_part, half, oh, olo, turned, sides_h, sides_l)

    away, kept, back = call(
        gram_kernel,
        (shaped(144, LANES), shaped(144, LANES), shaped(96, 512)),
        [VMEM] + [VMEM] * 10,
        flops=2 * 96 * 512 * 900 * 3,
        moved=2000000,
        name="gram",
    )(odd, rxa, rxb, rya, ryb, same, sent, rgh, rgl, base, held)

    precond = call(
        update_kernel,
        shaped(96, own),
        [VMEM] * 3,
        flops=2 * 192 * 1296 * 512,
        moved=3000000,
        name="update",
    )(back, turned, local)

    def summed(value, axis, steps):
        total = swap(value, axis, steps[0])
        for step in steps[1:]:
            total = total + swap(value, axis, step)
        return value + total

    def summed_apart(value, first):
        rows, cols = lax.axis_size("sx"), lax.axis_size("sy")

        def partner(r, c, step):
            return (r ^ (2 * step), c) if r % 2 == first else (r, c ^ (8 * step))

        def moved(step):
            route = []
            for r in range(rows):
                for c in range(cols):
                    to_row, to_col = partner(r, c, step)
                    route.append((r * cols + c, to_row * cols + to_col))
            return lax.ppermute(value, ("sx", "sy"), route)

        total = moved(1)
        for step in (3, 2):
            total = total + moved(step)
        return value + total

    total = kept + swap(away, "sx", 1)
    total = summed_apart(total, 0)
    total = summed_apart(total, 1)
    total = summed(total, "sy", (6,))
    total, precond = lax.optimization_barrier((total, precond))
    three, two, one = (swap(total, "sy", step) for step in (3, 2, 1))
    late = (total[:96] + one[:96]) + (two[:96] + three[:96])
    mine = jnp.concatenate([late, total[96:] + two[96:], one[96:] + three[96:]], axis=0)
    other = swap(mine, "sx", 1)

    vertex_total = own * lax.axis_size("sx") * lax.axis_size("sy")

    def finish(odd, *refs):
        final_kernel(1.0 / vertex_total, odd, *refs)

    gram = call(
        finish,
        shaped(288, 288),
        [VMEM] * 3,
        [pltpu.VMEM((288, 288), F32), pltpu.SemaphoreType.DMA((3,))],
        flops=1000000,
        moved=700000,
        name="final",
        out_specs=HBM,
    )(odd, mine, other)
    return precond, gram


def solution(mesh):
    placed = (
        P(None, ("sx", "sy")),
        P(None, ("sx", "sy")),
        P(None, ("sx", "sy")),
        P("sx", "sy", None, None),
        P("sx", "sy", None, None),
        P("sx", "sy", None),
    )
    return jax.shard_map(
        body, mesh=mesh, in_specs=placed, out_specs=(P(None, ("sx", "sy")), P()), check_vma=False
    )
```

```python
import jax
import jax.numpy as jnp
from jax import lax
from jax.experimental import pallas as pl
from jax.experimental.pallas import tpu as pltpu
from jax.sharding import PartitionSpec as P

EDGE = 72
LANES = 128
TAIL = 1280
F32 = jnp.float32
BF16 = jnp.bfloat16
VMEM = pl.BlockSpec(memory_space=pltpu.VMEM)
HBM = pl.BlockSpec(memory_space=pl.ANY)
NN = (((1,), (0,)), ((), ()))
NT = (((1,), (1,)), ((), ()))


def split(value):
    high = value.astype(BF16)
    low = (value - high.astype(F32)).astype(BF16)
    return high, low


def dot(left, right, dims):
    return lax.dot_general(left, right, dims, preferred_element_type=F32)


def dot_pairs(left, right, dims):
    rows = left[0].shape[0]
    both = dot(jnp.concatenate(left, axis=0), right[0], dims)
    return both[:rows] + both[rows:] + dot(left[0], right[1], dims)


def dot_exact(left, right, dims):
    rows = left[0].shape[0]
    both = dot(jnp.concatenate(left, axis=0), right, dims)
    return both[:rows] + both[rows:]


def pick(flag, when_even, when_odd):
    return jnp.where(flag[:, : when_even.shape[1]] == 0, when_even, when_odd)


def call(kernel, out, in_specs, scratch=(), flops=0, moved=0, name=None, out_specs=None, limit=20):
    return pl.pallas_call(
        kernel,
        out_shape=out,
        in_specs=in_specs,
        out_specs=jax.tree.map(lambda _: VMEM, out) if out_specs is None else out_specs,
        scratch_shapes=list(scratch),
        compiler_params=pltpu.CompilerParams(vmem_limit_bytes=limit * 1024 * 1024),
        cost_estimate=pl.CostEstimate(flops=flops, bytes_accessed=moved, transcendentals=0),
        name=name,
    )


def shaped(*shape, dtype=F32):
    return jax.ShapeDtypeStruct(shape, dtype)


def in_hbm(value):
    return pltpu.with_memory_space_constraint(value, pltpu.HBM)


def gather_kernel(
    odd, count_hbm, rows_hbm, res_hbm, factor, sxb, sxa, sya, syb, field, ids, slab, count, rows, res, sem
):
    fetch_count = pltpu.make_async_copy(count_hbm, count, sem.at[0])
    fetch_rows = pltpu.make_async_copy(rows_hbm, rows, sem.at[1])
    fetch_res = pltpu.make_async_copy(res_hbm, res, sem.at[2])
    fetch_count.start()
    fetch_rows.start()
    fetch_res.start()
    fetch_slab = pltpu.make_async_copy(factor.at[0, 0, pl.ds(TAIL, 320), :], slab, sem.at[3])
    fetch_slab.start()
    lane = lax.broadcasted_iota(jnp.int32, (1, LANES), 1)
    fetch_count.wait()
    fetch_rows.wait()
    table = rows[0, 0]

    def live(n):
        return count[0, 0, n]

    def edge(n):
        return jnp.where(lane < live(n), table[n : n + 1], -1)

    def corner(base, n, at):
        moved = pltpu.roll(table, at, 1)[n : n + 1]
        return jnp.where((lane >= at) & (lane < at + live(n)), moved, base)

    down = corner(corner(edge(0), 4, 72), 5, 80)
    up = corner(corner(edge(1), 6, 76), 7, 84)
    right, left = edge(2), edge(3)
    lists = [
        pick(odd[0:1], down, up),
        pick(odd[0:1], up, down),
        pick(odd[1:2], right, left),
        pick(odd[1:2], left, right),
    ]
    for k, values in enumerate(lists + lists):
        ids[k : k + 1] = values
    own = res.shape[1]
    row = lax.broadcasted_iota(jnp.int32, (own, LANES), 0)
    ones = [jnp.where(row == values, 1.0, 0.0).astype(BF16) for values in lists]
    onehot = jnp.concatenate(ones, axis=1)
    fetch_res.wait()
    high, low = split(res[...])
    field[:96] = high
    field[96:] = low
    packed = dot(field[...], onehot, NN)
    packed = packed[:96] + packed[96:]
    for k, out in enumerate((sxa, sxb, sya, syb)):
        out[...] = packed[:, k * LANES : (k + 1) * LANES]
    fetch_slab.wait()


def halo_place():
    col = lax.broadcasted_iota(jnp.int32, (320, 4 * LANES), 0) - 16
    spot = lax.broadcasted_iota(jnp.int32, (1, 4 * LANES), 1)
    lane = spot % LANES
    block = spot // LANES
    source = jnp.where(lane < EDGE, block * EDGE + lane, -99)
    for n, b, at in ((4, 2, 72), (6, 2, 76), (5, 3, 80), (7, 3, 84)):
        inside = (block == b) & (lane >= at) & (lane < at + 4)
        source = jnp.where(inside, 4 * EDGE + (n - 4) * 4 + lane - at, source)
    return jnp.where(col == source, 1.0, 0.0).astype(BF16)


def fetch(pairs, sem):
    copies = [pltpu.make_async_copy(source, dest, sem.at[k]) for k, (source, dest) in enumerate(pairs)]
    for copy in copies:
        copy.start()
    return copies


def own_slab(factor, k):
    return factor.at[0, 0, pl.ds(256 * k, 256), pl.ds(0, 256 * (k + 1))]


def tail_kernel(
    field, slab, factor, ritz_hbm, search_hbm, part, ph, plo, th, tlo, oh, olo, ritz, search, slab0, slab1, slab2, sem
):
    slabs = [(own_slab(factor, k), dest) for k, dest in enumerate((slab0, slab1, slab2))]
    copies = fetch([(ritz_hbm, ritz), (search_hbm, search)] + slabs, sem)
    place = halo_place()
    own = field.shape[1]
    oh[...], olo[...] = split(slab[:, :own])
    part[...] = dot_pairs((field[:96], field[96:]), (oh[...], olo[...]), NT)
    for value, out, turned in zip(split(slab[:, TAIL:]), (ph, plo), (th, tlo)):
        placed = dot(value, place, NN)
        out[...] = placed.astype(BF16)
        turned[...] = placed.T.astype(BF16)
    for copy in copies:
        copy.wait()


def halo_kernel(odd, sxa, sxb, sya, syb, part, ph, plo, th, tlo, given, half, bxa, bxb, bya, byb):
    xa, xb, ya, yb = sxa[...], sxb[...], sya[...], syb[...]
    arrived = jnp.concatenate(
        [pick(odd[0:1], xb, xa), pick(odd[0:1], xa, xb), pick(odd[1:2], yb, ya), pick(odd[1:2], ya, yb)], axis=1
    )
    solved = part[...] + dot_pairs(split(arrived), (th[...], tlo[...]), NN)
    half[...] = solved
    back = dot_pairs(split(solved), (ph[...], plo[...]), NN)
    b = [back[:, k * LANES : (k + 1) * LANES] for k in range(4)]
    bxa[...] = pick(odd[0:1], b[1], b[0])
    bxb[...] = pick(odd[0:1], b[0], b[1])
    bya[:96] = pick(odd[1:2], b[3], b[2])
    bya[96:] = given[...]
    byb[...] = pick(odd[1:2], b[2], b[3])


def slab_term(field, slab):
    width = slab.shape[1]
    block = split(slab[...])
    solved = dot_pairs((field[:96, :width], field[96:, :width]), block, NT)
    return dot_pairs(split(solved), block, NN)


def head_kernel(field, slab0, slab1, out):
    out[...] = slab_term(field, slab1)
    out[:, :256] = out[:, :256] + slab_term(field, slab0)


def last_kernel(field, slab2, slab3, head, factor, out, slab4, sem):
    (copy,) = fetch([(own_slab(factor, 4), slab4)], sem)
    out[:, :1024] = slab_term(field, slab3)
    out[:, :768] = out[:, :768] + slab_term(field, slab2)
    out[:, :512] = out[:, :512] + head[...]
    copy.wait()
    term = slab_term(field, slab4)
    out[:, :1024] = out[:, :1024] + term[:, :1024]
    out[:, 1024:] = term[:, 1024:]


def distinct_tiles(square):
    tiles = [square[32 * i : 32 * i + 32, 32 * j : 32 * j + 32] for i in range(3) for j in range(i, 3)]
    return jnp.concatenate(tiles, axis=0)


def whole_square(tiles):
    t = [tiles[32 * k : 32 * k + 32] for k in range(6)]
    blank = jnp.zeros((32, 32), F32)
    upper = jnp.concatenate(
        [
            jnp.concatenate([t[0], t[1], t[2]], axis=1),
            jnp.concatenate([blank, t[3], t[4]], axis=1),
            jnp.concatenate([blank, blank, t[5]], axis=1),
        ],
        axis=0,
    )
    row = lax.broadcasted_iota(jnp.int32, (96, 96), 0) // 32
    col = lax.broadcasted_iota(jnp.int32, (96, 96), 1) // 32
    return jnp.where(row <= col, upper, upper.T)


def side_kernel(
    odd, ids, ritz, search, factor, held, given, turned, same, sides_h, sides_l, rgh, rgl, slab3, sem
):
    copies = fetch([(own_slab(factor, 3), slab3)], sem)
    own = ritz.shape[1]
    numbers = ids[...].astype(F32)
    columns = numbers.T
    live = jnp.where(columns < 0.0, -2.0, columns)
    across = lax.broadcasted_iota(jnp.int32, (LANES, own), 1).astype(F32)
    for k in range(4):
        lanes = slice(k * LANES, (k + 1) * LANES)
        turned[lanes] = jnp.where(columns[:, k : k + 1] == across, 1.0, 0.0).astype(BF16)
        for j in range(4):
            agree = live[:, k : k + 1] == numbers[j : j + 1]
            same[lanes, j * LANES : (j + 1) * LANES] = jnp.where(agree, 1.0, 0.0).astype(BF16)
    blank = jnp.zeros((32, own), BF16)
    for r, s, out in zip(split(ritz[...]), split(search[...]), (sides_h, sides_l)):
        out[:96] = r
        out[96:128] = blank
        out[128:224] = s
        out[224:] = blank
    for side, out in zip((sides_h, sides_l), (rgh, rgl)):
        out[...] = dot(turned[...], side[...], NT).astype(BF16)
    pair = (sides_h[...], sides_l[...])
    cross = dot_pairs(pair, pair, NT)
    rr, sr, ss = cross[:96, :96], cross[128:224, :96], cross[128:224, LANES : LANES + 96]
    rt, st = distinct_tiles(rr), distinct_tiles(ss)
    first = jnp.concatenate([sr, rt[:96]], axis=1)
    second = jnp.concatenate([rt[96:], st[:96], st[96:], jnp.zeros((96, 32), F32)], axis=1)
    held[...] = pick(odd[1:2], first, second)
    given[...] = pick(odd[1:2], second, first)
    for copy in copies:
        copy.wait()


def local_kernel(own_part, half, oh, olo, turned, sides_h, sides_l, local, sent, base):
    add = dot_pairs(split(half[...]), (oh[...], olo[...]), NN)
    value = add + jnp.concatenate([own_part[...], jnp.zeros((96, add.shape[1] - TAIL), F32)], axis=1)
    local[...] = value
    pair = split(value)
    sent[...] = dot_exact(pair, turned[...], NT)
    base[:96] = dot_pairs(pair, pair, NT)
    cross = dot_pairs(pair, (sides_h[...], sides_l[...]), NT)
    base[96:192] = cross[:, :96]
    base[192:] = cross[:, LANES : LANES + 96]


def gram_kernel(odd, rxa, rxb, rya, ryb, same, sent, rgh, rgl, base, held, away, kept, back):
    back[...] = jnp.concatenate([rxa[...], rxb[...], rya[:96], ryb[...]], axis=1)
    pair = split(back[...])
    mixed = sent[...] + 0.5 * dot_exact(pair, same[...], NN)
    square = dot_pairs(split(mixed), pair, NT)
    cross = dot_pairs(pair, (rgh[...], rgl[...]), NN)
    pp = base[:96] + square + square.T
    pr = base[96:192] + cross[:, :96]
    ps = base[192:] + cross[:, LANES : LANES + 96]
    tiles = distinct_tiles(pp)
    first = jnp.concatenate([pr, tiles[:96]], axis=1)
    second = jnp.concatenate([ps, tiles[96:]], axis=1)
    kept[:96] = pick(odd[0:1], first, second)
    away[:96] = pick(odd[0:1], second, first)
    early = held[...] + rya[96:]
    kept[96:] = pick(odd[0:1], early[:48], early[48:])
    away[96:] = pick(odd[0:1], early[48:], early[:48])


def update_kernel(back, turned, local, precond):
    precond[...] = local[...] + dot_exact(split(back[...]), turned[...], NN)


def final_kernel(scale, odd, mine, other, gram, out, sem):
    def by_core(rows):
        a, b = mine[rows], other[rows]
        return pick(odd[0:1], a, b) * scale, pick(odd[0:1], b, a) * scale

    late = by_core(slice(0, 96))
    near, far = by_core(slice(96, 144)), by_core(slice(144, 192))
    near, far = jnp.concatenate(near, axis=0), jnp.concatenate(far, axis=0)
    first, second = pick(odd[1:2], near, far), pick(odd[1:2], far, near)
    pr, ps = late[0][:, :96], late[1][:, :96]
    pp = whole_square(jnp.concatenate([late[0][:, 96:], late[1][:, 96:]], axis=0))
    sr = first[:, :96]
    rr = whole_square(jnp.concatenate([first[:, 96:], second[:, :32]], axis=0))
    ss = whole_square(jnp.concatenate([second[:, 32:64], second[:, 64:96]], axis=0))
    copies = []
    bands = ([pr, pp, ps], [rr, pr.T, sr.T], [sr, ps.T, ss])
    for k, parts in zip((1, 0, 2), bands):
        rows = slice(96 * k, 96 * (k + 1))
        out[rows] = jnp.concatenate(parts, axis=1)
        copies.append(pltpu.make_async_copy(out.at[rows], gram.at[rows], sem.at[k]))
        copies[-1].start()
    for copy in copies:
        copy.wait()


def swap(block, axis, step):
    return lax.ppermute(block, axis, [(i, i ^ step) for i in range(lax.axis_size(axis))])


def swap_odd(block, axis):
    size = lax.axis_size(axis)
    route = [(i, (i + 1) % size) for i in range(1, size, 2)]
    return lax.ppermute(block, axis, route + [(b, a) for a, b in route])


def body(residual, ritz_block, search_block, inverse_factor, send_rows, send_count):
    own = residual.shape[1]
    p, q = lax.axis_index("sx"), lax.axis_index("sy")
    odd = jnp.where(jnp.arange(8)[:, None] == 0, p % 2, q % 2) + jnp.zeros((8, LANES), jnp.int32)
    lane = jnp.arange(LANES)[None, :]
    msg = shaped(96, LANES)

    factor = in_hbm(inverse_factor)
    sxb, sxa, sya, syb, field, ids, slab = call(
        gather_kernel,
        (
            msg,
            msg,
            msg,
            msg,
            shaped(192, own, dtype=BF16),
            shaped(8, LANES, dtype=jnp.int32),
            shaped(320, 1600),
        ),
        [VMEM, HBM, HBM, HBM, HBM],
        [
            pltpu.SMEM((1, 1, 8), jnp.int32),
            pltpu.VMEM((1, 1, 8, LANES), jnp.int32),
            pltpu.VMEM((96, own), F32),
            pltpu.SemaphoreType.DMA((4,)),
        ],
        flops=2 * 192 * 1296 * 512,
        moved=2000000,
        name="gather",
    )(odd, in_hbm(send_count), in_hbm(send_rows), in_hbm(residual), factor)

    gxb, gxa = swap_odd(sxb, "sx"), swap(sxa, "sx", 1)

    placed, turned = shaped(320, 512, dtype=BF16), shaped(512, 320, dtype=BF16)
    wide = shaped(320, own, dtype=BF16)
    part, ph, plo, th, tlo, oh, olo, ritz, search, slab0, slab1, slab2 = call(
        tail_kernel,
        (shaped(96, 320), placed, placed, turned, turned, wide, wide)
        + (shaped(96, own), shaped(96, own), shaped(256, 256), shaped(256, 512), shaped(256, 768)),
        [VMEM, VMEM, HBM, HBM, HBM],
        [pltpu.SemaphoreType.DMA((5,))],
        flops=2 * 96 * 1296 * 320 * 3,
        moved=6000000,
        name="tail",
    )(field, slab, factor, in_hbm(ritz_block), in_hbm(search_block))
    gxb, gxa, part = lax.optimization_barrier((gxb, gxa, part))

    relay = jnp.where(lane >= EDGE, gxb + gxa, 0.0)
    gyb, gya = swap_odd(syb + relay, "sy"), swap(sya + relay, "sy", 1)

    sides, sent_sides = shaped(2 * LANES, own, dtype=BF16), shaped(512, 2 * LANES, dtype=BF16)
    held, given, turned, same, sides_h, sides_l, rgh, rgl, slab3 = call(
        side_kernel,
        (
            msg,
            msg,
            shaped(512, own, dtype=BF16),
            shaped(512, 512, dtype=BF16),
            sides,
            sides,
            sent_sides,
            sent_sides,
            shaped(256, 1024),
        ),
        [VMEM] + [VMEM] * 3 + [HBM],
        [pltpu.SemaphoreType.DMA((1,))],
        flops=2 * 192 * 256 * 1296 * 3,
        moved=3000000,
        name="side",
    )(odd, ids, ritz, search, factor)

    head = call(
        head_kernel,
        shaped(96, 512),
        [VMEM] * 3,
        flops=2 * 2 * 96 * 256 * 256 * 3 * 3,
        moved=1200000,
        name="head",
    )(field, slab0, slab1)
    gya, gyb, head = lax.optimization_barrier((gya, gyb, head))

    half, bxa, bxb, bya, byb = call(
        halo_kernel,
        (shaped(96, 320), msg, msg, shaped(192, LANES), msg),
        [VMEM] + [VMEM] * 10,
        flops=2 * 2 * 96 * 320 * 512 * 3,
        moved=1000000,
        name="halo",
    )(odd, gxa, gxb, gya, gyb, part, ph, plo, th, tlo, given)

    ryb, rya = swap_odd(byb, "sy"), swap(bya, "sy", 1)

    own_part = call(
        last_kernel,
        shaped(96, TAIL),
        [VMEM] * 4 + [HBM],
        [pltpu.VMEM((256, TAIL), F32), pltpu.SemaphoreType.DMA((1,))],
        flops=2 * 2 * 96 * 256 * 256 * 12 * 3,
        moved=3000000,
        name="last",
    )(field, slab2, slab3, head, factor)
    rya, ryb, own_part = lax.optimization_barrier((rya, ryb, own_part))

    relay = jnp.where(lane >= EDGE, rya[:96] + ryb, 0.0)
    rxb, rxa = swap_odd(bxb + relay, "sx"), swap(bxa + relay, "sx", 1)

    local, sent, base = call(
        local_kernel,
        (shaped(96, own), shaped(96, 512), shaped(288, 96)),
        [VMEM] * 7,
        flops=2 * 96 * 1296 * 1100 * 3,
        moved=4000000,
        name="local",
    )(own_part, half, oh, olo, turned, sides_h, sides_l)

    away, kept, back = call(
        gram_kernel,
        (shaped(144, LANES), shaped(144, LANES), shaped(96, 512)),
        [VMEM] + [VMEM] * 10,
        flops=2 * 96 * 512 * 900 * 3,
        moved=2000000,
        name="gram",
    )(odd, rxa, rxb, rya, ryb, same, sent, rgh, rgl, base, held)

    precond = call(
        update_kernel,
        shaped(96, own),
        [VMEM] * 3,
        flops=2 * 192 * 1296 * 512,
        moved=3000000,
        name="update",
    )(back, turned, local)

    rows, cols = lax.axis_size("sx"), lax.axis_size("sy")

    def swap_apart(value, even_core, odd_core):
        route = []
        for r in range(rows):
            for c in range(cols):
                row_step, col_step = odd_core if r % 2 else even_core
                route.append((r * cols + c, (r ^ row_step) * cols + (c ^ col_step)))
        return lax.ppermute(value, ("sx", "sy"), route)

    def summed(value, even_cores, odd_cores):
        total = swap_apart(value, even_cores[0], odd_cores[0])
        for even_core, odd_core in zip(even_cores[1:], odd_cores[1:]):
            total = total + swap_apart(value, even_core, odd_core)
        return value + total

    along_y = [(2 * step, 0) for step in (1, 3, 2)]
    along_x = [(0, 8 * step) for step in (1, 3, 2)]
    total = kept + swap(away, "sx", 1)
    total = summed(total, along_y, along_x)
    total = summed(total, along_x, along_y)
    total = summed(total, [(0, 6)], [(0, 2)])
    total, precond = lax.optimization_barrier((total, precond))
    three = swap_apart(total, (0, 3), (0, 7))
    two = swap_apart(total, (0, 2), (0, 6))
    one = swap_apart(total, (0, 1), (0, 1))
    late = (total[:96] + one[:96]) + (two[:96] + three[:96])
    mine = jnp.concatenate([late, total[96:] + two[96:], one[96:] + three[96:]], axis=0)
    other = swap(mine, "sx", 1)

    vertex_total = own * lax.axis_size("sx") * lax.axis_size("sy")

    def finish(odd, *refs):
        final_kernel(1.0 / vertex_total, odd, *refs)

    gram = call(
        finish,
        shaped(288, 288),
        [VMEM] * 3,
        [pltpu.VMEM((288, 288), F32), pltpu.SemaphoreType.DMA((3,))],
        flops=1000000,
        moved=700000,
        name="final",
        out_specs=HBM,
    )(odd, mine, other)
    return precond, gram


def solution(mesh):
    placed = (
        P(None, ("sx", "sy")),
        P(None, ("sx", "sy")),
        P(None, ("sx", "sy")),
        P("sx", "sy", None, None),
        P("sx", "sy", None, None),
        P("sx", "sy", None),
    )
    return jax.shard_map(
        body, mesh=mesh, in_specs=placed, out_specs=(P(None, ("sx", "sy")), P()), check_vma=False
    )
```

```python
import jax
import jax.numpy as jnp
from jax import lax
from jax.experimental import pallas as pl
from jax.experimental.pallas import tpu as pltpu
from jax.sharding import PartitionSpec as P

EDGE = 72
LANES = 128
TAIL = 1280
F32 = jnp.float32
BF16 = jnp.bfloat16
VMEM = pl.BlockSpec(memory_space=pltpu.VMEM)
HBM = pl.BlockSpec(memory_space=pl.ANY)
NN = (((1,), (0,)), ((), ()))
NT = (((1,), (1,)), ((), ()))


def split(value):
    high = value.astype(BF16)
    low = (value - high.astype(F32)).astype(BF16)
    return high, low


def dot(left, right, dims):
    return lax.dot_general(left, right, dims, preferred_element_type=F32)


def dot_pairs(left, right, dims):
    rows = left[0].shape[0]
    both = dot(jnp.concatenate(left, axis=0), right[0], dims)
    return both[:rows] + both[rows:] + dot(left[0], right[1], dims)


def dot_exact(left, right, dims):
    rows = left[0].shape[0]
    both = dot(jnp.concatenate(left, axis=0), right, dims)
    return both[:rows] + both[rows:]


def pick(flag, when_even, when_odd):
    return jnp.where(flag[:, : when_even.shape[1]] == 0, when_even, when_odd)


def call(kernel, out, in_specs, scratch=(), flops=0, moved=0, name=None, out_specs=None, limit=20):
    return pl.pallas_call(
        kernel,
        out_shape=out,
        in_specs=in_specs,
        out_specs=jax.tree.map(lambda _: VMEM, out) if out_specs is None else out_specs,
        scratch_shapes=list(scratch),
        compiler_params=pltpu.CompilerParams(vmem_limit_bytes=limit * 1024 * 1024),
        cost_estimate=pl.CostEstimate(flops=flops, bytes_accessed=moved, transcendentals=0),
        name=name,
    )


def shaped(*shape, dtype=F32):
    return jax.ShapeDtypeStruct(shape, dtype)


def in_hbm(value):
    return pltpu.with_memory_space_constraint(value, pltpu.HBM)


def gather_kernel(
    odd, count_hbm, rows_hbm, res_hbm, factor, sxb, sxa, sya, syb, field, ids, slab, count, rows, res, sem
):
    fetch_count = pltpu.make_async_copy(count_hbm, count, sem.at[0])
    fetch_rows = pltpu.make_async_copy(rows_hbm, rows, sem.at[1])
    fetch_res = pltpu.make_async_copy(res_hbm, res, sem.at[2])
    fetch_count.start()
    fetch_rows.start()
    fetch_res.start()
    fetch_slab = pltpu.make_async_copy(factor.at[0, 0, pl.ds(TAIL, 320), :], slab, sem.at[3])
    fetch_slab.start()
    lane = lax.broadcasted_iota(jnp.int32, (1, LANES), 1)
    fetch_count.wait()
    fetch_rows.wait()
    table = rows[0, 0]

    def live(n):
        return count[0, 0, n]

    def edge(n):
        return jnp.where(lane < live(n), table[n : n + 1], -1)

    def corner(base, n, at):
        moved = pltpu.roll(table, at, 1)[n : n + 1]
        return jnp.where((lane >= at) & (lane < at + live(n)), moved, base)

    down = corner(corner(edge(0), 4, 72), 5, 80)
    up = corner(corner(edge(1), 6, 76), 7, 84)
    right, left = edge(2), edge(3)
    lists = [
        pick(odd[0:1], down, up),
        pick(odd[0:1], up, down),
        pick(odd[1:2], right, left),
        pick(odd[1:2], left, right),
    ]
    for k, values in enumerate(lists + lists):
        ids[k : k + 1] = values
    own = res.shape[1]
    row = lax.broadcasted_iota(jnp.int32, (own, LANES), 0)
    ones = [jnp.where(row == values, 1.0, 0.0).astype(BF16) for values in lists]
    onehot = jnp.concatenate(ones, axis=1)
    fetch_res.wait()
    high, low = split(res[...])
    field[:96] = high
    field[96:] = low
    packed = dot(field[...], onehot, NN)
    packed = packed[:96] + packed[96:]
    for k, out in enumerate((sxa, sxb, sya, syb)):
        out[...] = packed[:, k * LANES : (k + 1) * LANES]
    fetch_slab.wait()


def halo_place():
    col = lax.broadcasted_iota(jnp.int32, (320, 4 * LANES), 0) - 16
    spot = lax.broadcasted_iota(jnp.int32, (1, 4 * LANES), 1)
    lane = spot % LANES
    block = spot // LANES
    source = jnp.where(lane < EDGE, block * EDGE + lane, -99)
    for n, b, at in ((4, 2, 72), (6, 2, 76), (5, 3, 80), (7, 3, 84)):
        inside = (block == b) & (lane >= at) & (lane < at + 4)
        source = jnp.where(inside, 4 * EDGE + (n - 4) * 4 + lane - at, source)
    return jnp.where(col == source, 1.0, 0.0).astype(BF16)


def fetch(pairs, sem):
    copies = [pltpu.make_async_copy(source, dest, sem.at[k]) for k, (source, dest) in enumerate(pairs)]
    for copy in copies:
        copy.start()
    return copies


def own_slab(factor, k):
    return factor.at[0, 0, pl.ds(256 * k, 256), pl.ds(0, 256 * (k + 1))]


def tail_kernel(
    field, slab, factor, ritz_hbm, search_hbm, part, ph, plo, th, tlo, oh, olo, ritz, search, slab0, slab1, sem
):
    slabs = [(own_slab(factor, k), dest) for k, dest in enumerate((slab0, slab1))]
    copies = fetch([(ritz_hbm, ritz), (search_hbm, search)] + slabs, sem)
    place = halo_place()
    own = field.shape[1]
    oh[...], olo[...] = split(slab[:, :own])
    part[...] = dot_pairs((field[:96], field[96:]), (oh[...], olo[...]), NT)
    for value, out, turned in zip(split(slab[:, TAIL:]), (ph, plo), (th, tlo)):
        placed = dot(value, place, NN)
        out[...] = placed.astype(BF16)
        turned[...] = placed.T.astype(BF16)
    for copy in copies:
        copy.wait()


def halo_kernel(odd, sxa, sxb, sya, syb, part, ph, plo, th, tlo, given, half, bxa, bxb, bya, byb):
    xa, xb, ya, yb = sxa[...], sxb[...], sya[...], syb[...]
    arrived = jnp.concatenate(
        [pick(odd[0:1], xb, xa), pick(odd[0:1], xa, xb), pick(odd[1:2], yb, ya), pick(odd[1:2], ya, yb)], axis=1
    )
    solved = part[...] + dot_pairs(split(arrived), (th[...], tlo[...]), NN)
    half[...] = solved
    back = dot_pairs(split(solved), (ph[...], plo[...]), NN)
    b = [back[:, k * LANES : (k + 1) * LANES] for k in range(4)]
    bxa[...] = pick(odd[0:1], b[1], b[0])
    bxb[...] = pick(odd[0:1], b[0], b[1])
    bya[:96] = pick(odd[1:2], b[3], b[2])
    bya[96:] = given[...]
    byb[...] = pick(odd[1:2], b[2], b[3])


def slab_term(field, slab):
    width = slab.shape[1]
    block = split(slab[...])
    solved = dot_pairs((field[:96, :width], field[96:, :width]), block, NT)
    return dot_pairs(split(solved), block, NN)


def head_kernel(field, slab0, slab1, out):
    out[...] = slab_term(field, slab1)
    out[:, :256] = out[:, :256] + slab_term(field, slab0)


def last_kernel(field, slab3, head, factor, out, slab2, slab4, sem):
    copies = fetch([(own_slab(factor, 2), slab2), (own_slab(factor, 4), slab4)], sem)
    out[:, :1024] = slab_term(field, slab3)
    out[:, :512] = out[:, :512] + head[...]
    copies[0].wait()
    out[:, :768] = out[:, :768] + slab_term(field, slab2)
    copies[1].wait()
    term = slab_term(field, slab4)
    out[:, :1024] = out[:, :1024] + term[:, :1024]
    out[:, 1024:] = term[:, 1024:]


def distinct_tiles(square):
    tiles = [square[32 * i : 32 * i + 32, 32 * j : 32 * j + 32] for i in range(3) for j in range(i, 3)]
    return jnp.concatenate(tiles, axis=0)


def whole_square(tiles):
    t = [tiles[32 * k : 32 * k + 32] for k in range(6)]
    blank = jnp.zeros((32, 32), F32)
    upper = jnp.concatenate(
        [
            jnp.concatenate([t[0], t[1], t[2]], axis=1),
            jnp.concatenate([blank, t[3], t[4]], axis=1),
            jnp.concatenate([blank, blank, t[5]], axis=1),
        ],
        axis=0,
    )
    row = lax.broadcasted_iota(jnp.int32, (96, 96), 0) // 32
    col = lax.broadcasted_iota(jnp.int32, (96, 96), 1) // 32
    return jnp.where(row <= col, upper, upper.T)


def side_kernel(
    odd, ids, ritz, search, factor, held, given, turned, same, sides_h, sides_l, rgh, rgl, slab3, sem
):
    copies = fetch([(own_slab(factor, 3), slab3)], sem)
    own = ritz.shape[1]
    numbers = ids[...].astype(F32)
    columns = numbers.T
    live = jnp.where(columns < 0.0, -2.0, columns)
    across = lax.broadcasted_iota(jnp.int32, (LANES, own), 1).astype(F32)
    for k in range(4):
        lanes = slice(k * LANES, (k + 1) * LANES)
        turned[lanes] = jnp.where(columns[:, k : k + 1] == across, 1.0, 0.0).astype(BF16)
        for j in range(4):
            agree = live[:, k : k + 1] == numbers[j : j + 1]
            same[lanes, j * LANES : (j + 1) * LANES] = jnp.where(agree, 1.0, 0.0).astype(BF16)
    blank = jnp.zeros((32, own), BF16)
    for r, s, out in zip(split(ritz[...]), split(search[...]), (sides_h, sides_l)):
        out[:96] = r
        out[96:128] = blank
        out[128:224] = s
        out[224:] = blank
    for side, out in zip((sides_h, sides_l), (rgh, rgl)):
        out[...] = dot(turned[...], side[...], NT).astype(BF16)
    pair = (sides_h[...], sides_l[...])
    cross = dot_pairs(pair, pair, NT)
    rr, sr, ss = cross[:96, :96], cross[128:224, :96], cross[128:224, LANES : LANES + 96]
    rt, st = distinct_tiles(rr), distinct_tiles(ss)
    first = jnp.concatenate([sr, rt[:96]], axis=1)
    second = jnp.concatenate([rt[96:], st[:96], st[96:], jnp.zeros((96, 32), F32)], axis=1)
    held[...] = pick(odd[1:2], first, second)
    given[...] = pick(odd[1:2], second, first)
    for copy in copies:
        copy.wait()


def local_kernel(own_part, half, oh, olo, turned, sides_h, sides_l, local, sent, base):
    add = dot_pairs(split(half[...]), (oh[...], olo[...]), NN)
    value = add + jnp.concatenate([own_part[...], jnp.zeros((96, add.shape[1] - TAIL), F32)], axis=1)
    local[...] = value
    pair = split(value)
    sent[...] = dot_exact(pair, turned[...], NT)
    base[:96] = dot_pairs(pair, pair, NT)
    cross = dot_pairs(pair, (sides_h[...], sides_l[...]), NT)
    base[96:192] = cross[:, :96]
    base[192:] = cross[:, LANES : LANES + 96]


def gram_kernel(odd, rxa, rxb, rya, ryb, same, sent, rgh, rgl, base, held, away, kept, back):
    back[...] = jnp.concatenate([rxa[...], rxb[...], rya[:96], ryb[...]], axis=1)
    pair = split(back[...])
    mixed = sent[...] + 0.5 * dot_exact(pair, same[...], NN)
    square = dot_pairs(split(mixed), pair, NT)
    cross = dot_pairs(pair, (rgh[...], rgl[...]), NN)
    pp = base[:96] + square + square.T
    pr = base[96:192] + cross[:, :96]
    ps = base[192:] + cross[:, LANES : LANES + 96]
    tiles = distinct_tiles(pp)
    first = jnp.concatenate([pr, tiles[:96]], axis=1)
    second = jnp.concatenate([ps, tiles[96:]], axis=1)
    kept[:96] = pick(odd[0:1], first, second)
    away[:96] = pick(odd[0:1], second, first)
    early = held[...] + rya[96:]
    kept[96:] = pick(odd[0:1], early[:48], early[48:])
    away[96:] = pick(odd[0:1], early[48:], early[:48])


def update_kernel(back, turned, local, precond):
    precond[...] = local[...] + dot_exact(split(back[...]), turned[...], NN)


def final_kernel(scale, odd, mine, other, gram, out, sem):
    def by_core(rows):
        a, b = mine[rows], other[rows]
        return pick(odd[0:1], a, b) * scale, pick(odd[0:1], b, a) * scale

    late = by_core(slice(0, 96))
    near, far = by_core(slice(96, 144)), by_core(slice(144, 192))
    near, far = jnp.concatenate(near, axis=0), jnp.concatenate(far, axis=0)
    first, second = pick(odd[1:2], near, far), pick(odd[1:2], far, near)
    pr, ps = late[0][:, :96], late[1][:, :96]
    pp = whole_square(jnp.concatenate([late[0][:, 96:], late[1][:, 96:]], axis=0))
    sr = first[:, :96]
    rr = whole_square(jnp.concatenate([first[:, 96:], second[:, :32]], axis=0))
    ss = whole_square(jnp.concatenate([second[:, 32:64], second[:, 64:96]], axis=0))
    copies = []
    bands = ([pr, pp, ps], [rr, pr.T, sr.T], [sr, ps.T, ss])
    for k, parts in zip((1, 0, 2), bands):
        rows = slice(96 * k, 96 * (k + 1))
        out[rows] = jnp.concatenate(parts, axis=1)
        copies.append(pltpu.make_async_copy(out.at[rows], gram.at[rows], sem.at[k]))
        copies[-1].start()
    for copy in copies:
        copy.wait()


def swap(block, axis, step):
    return lax.ppermute(block, axis, [(i, i ^ step) for i in range(lax.axis_size(axis))])


def swap_odd(block, axis):
    size = lax.axis_size(axis)
    route = [(i, (i + 1) % size) for i in range(1, size, 2)]
    return lax.ppermute(block, axis, route + [(b, a) for a, b in route])


def body(residual, ritz_block, search_block, inverse_factor, send_rows, send_count):
    own = residual.shape[1]
    p, q = lax.axis_index("sx"), lax.axis_index("sy")
    odd = jnp.where(jnp.arange(8)[:, None] == 0, p % 2, q % 2) + jnp.zeros((8, LANES), jnp.int32)
    lane = jnp.arange(LANES)[None, :]
    msg = shaped(96, LANES)

    factor = in_hbm(inverse_factor)
    sxb, sxa, sya, syb, field, ids, slab = call(
        gather_kernel,
        (
            msg,
            msg,
            msg,
            msg,
            shaped(192, own, dtype=BF16),
            shaped(8, LANES, dtype=jnp.int32),
            shaped(320, 1600),
        ),
        [VMEM, HBM, HBM, HBM, HBM],
        [
            pltpu.SMEM((1, 1, 8), jnp.int32),
            pltpu.VMEM((1, 1, 8, LANES), jnp.int32),
            pltpu.VMEM((96, own), F32),
            pltpu.SemaphoreType.DMA((4,)),
        ],
        flops=2 * 192 * 1296 * 512,
        moved=2000000,
        name="gather",
    )(odd, in_hbm(send_count), in_hbm(send_rows), in_hbm(residual), factor)

    gxb, gxa = swap_odd(sxb, "sx"), swap(sxa, "sx", 1)

    placed, turned = shaped(320, 512, dtype=BF16), shaped(512, 320, dtype=BF16)
    wide = shaped(320, own, dtype=BF16)
    part, ph, plo, th, tlo, oh, olo, ritz, search, slab0, slab1 = call(
        tail_kernel,
        (shaped(96, 320), placed, placed, turned, turned, wide, wide)
        + (shaped(96, own), shaped(96, own), shaped(256, 256), shaped(256, 512)),
        [VMEM, VMEM, HBM, HBM, HBM],
        [pltpu.SemaphoreType.DMA((4,))],
        flops=2 * 96 * 1296 * 320 * 3,
        moved=6000000,
        name="tail",
    )(field, slab, factor, in_hbm(ritz_block), in_hbm(search_block))
    gxb, gxa, part = lax.optimization_barrier((gxb, gxa, part))

    relay = jnp.where(lane >= EDGE, gxb + gxa, 0.0)
    gyb, gya = swap_odd(syb + relay, "sy"), swap(sya + relay, "sy", 1)

    sides, sent_sides = shaped(2 * LANES, own, dtype=BF16), shaped(512, 2 * LANES, dtype=BF16)
    held, given, turned, same, sides_h, sides_l, rgh, rgl, slab3 = call(
        side_kernel,
        (
            msg,
            msg,
            shaped(512, own, dtype=BF16),
            shaped(512, 512, dtype=BF16),
            sides,
            sides,
            sent_sides,
            sent_sides,
            shaped(256, 1024),
        ),
        [VMEM] + [VMEM] * 3 + [HBM],
        [pltpu.SemaphoreType.DMA((1,))],
        flops=2 * 192 * 256 * 1296 * 3,
        moved=3000000,
        name="side",
    )(odd, ids, ritz, search, factor)

    head = call(
        head_kernel,
        shaped(96, 512),
        [VMEM] * 3,
        flops=2 * 2 * 96 * 256 * 256 * 3 * 3,
        moved=1200000,
        name="head",
    )(field, slab0, slab1)
    gya, gyb, head = lax.optimization_barrier((gya, gyb, head))

    half, bxa, bxb, bya, byb = call(
        halo_kernel,
        (shaped(96, 320), msg, msg, shaped(192, LANES), msg),
        [VMEM] + [VMEM] * 10,
        flops=2 * 2 * 96 * 320 * 512 * 3,
        moved=1000000,
        name="halo",
    )(odd, gxa, gxb, gya, gyb, part, ph, plo, th, tlo, given)

    ryb, rya = swap_odd(byb, "sy"), swap(bya, "sy", 1)

    own_part = call(
        last_kernel,
        shaped(96, TAIL),
        [VMEM] * 3 + [HBM],
        [pltpu.VMEM((256, 768), F32), pltpu.VMEM((256, TAIL), F32), pltpu.SemaphoreType.DMA((2,))],
        flops=2 * 2 * 96 * 256 * 256 * 12 * 3,
        moved=3000000,
        name="last",
    )(field, slab3, head, factor)
    rya, ryb, own_part = lax.optimization_barrier((rya, ryb, own_part))

    relay = jnp.where(lane >= EDGE, rya[:96] + ryb, 0.0)
    rxb, rxa = swap_odd(bxb + relay, "sx"), swap(bxa + relay, "sx", 1)

    local, sent, base = call(
        local_kernel,
        (shaped(96, own), shaped(96, 512), shaped(288, 96)),
        [VMEM] * 7,
        flops=2 * 96 * 1296 * 1100 * 3,
        moved=4000000,
        name="local",
    )(own_part, half, oh, olo, turned, sides_h, sides_l)

    away, kept, back = call(
        gram_kernel,
        (shaped(144, LANES), shaped(144, LANES), shaped(96, 512)),
        [VMEM] + [VMEM] * 10,
        flops=2 * 96 * 512 * 900 * 3,
        moved=2000000,
        name="gram",
    )(odd, rxa, rxb, rya, ryb, same, sent, rgh, rgl, base, held)

    precond = call(
        update_kernel,
        shaped(96, own),
        [VMEM] * 3,
        flops=2 * 192 * 1296 * 512,
        moved=3000000,
        name="update",
    )(back, turned, local)

    rows, cols = lax.axis_size("sx"), lax.axis_size("sy")

    def swap_apart(value, even_core, odd_core):
        route = []
        for r in range(rows):
            for c in range(cols):
                row_step, col_step = odd_core if r % 2 else even_core
                route.append((r * cols + c, (r ^ row_step) * cols + (c ^ col_step)))
        return lax.ppermute(value, ("sx", "sy"), route)

    def summed(value, even_cores, odd_cores):
        total = swap_apart(value, even_cores[0], odd_cores[0])
        for even_core, odd_core in zip(even_cores[1:], odd_cores[1:]):
            total = total + swap_apart(value, even_core, odd_core)
        return value + total

    along_y = [(2 * step, 0) for step in (1, 3, 2)]
    along_x = [(0, 8 * step) for step in (1, 3, 2)]
    total = kept + swap(away, "sx", 1)
    total = summed(total, along_y, along_x)
    total = summed(total, along_x, along_y)
    total = summed(total, [(0, 6)], [(0, 2)])
    total, precond = lax.optimization_barrier((total, precond))
    three = swap_apart(total, (0, 3), (0, 7))
    two = swap_apart(total, (0, 2), (0, 6))
    one = swap_apart(total, (0, 1), (0, 1))
    three, two, one = lax.optimization_barrier((three, two, one))
    late = (total[:96] + one[:96]) + (two[:96] + three[:96])
    mine = jnp.concatenate([late, total[96:] + two[96:], one[96:] + three[96:]], axis=0)
    other = swap(mine, "sx", 1)

    vertex_total = own * lax.axis_size("sx") * lax.axis_size("sy")

    def finish(odd, *refs):
        final_kernel(1.0 / vertex_total, odd, *refs)

    gram = call(
        finish,
        shaped(288, 288),
        [VMEM] * 3,
        [pltpu.VMEM((288, 288), F32), pltpu.SemaphoreType.DMA((3,))],
        flops=1000000,
        moved=700000,
        name="final",
        out_specs=HBM,
    )(odd, mine, other)
    return precond, gram


def solution(mesh):
    placed = (
        P(None, ("sx", "sy")),
        P(None, ("sx", "sy")),
        P(None, ("sx", "sy")),
        P("sx", "sy", None, None),
        P("sx", "sy", None, None),
        P("sx", "sy", None),
    )
    return jax.shard_map(
        body, mesh=mesh, in_specs=placed, out_specs=(P(None, ("sx", "sy")), P()), check_vma=False
    )
```

```python
import jax
import jax.numpy as jnp
from jax import lax
from jax.experimental import pallas as pl
from jax.experimental.pallas import tpu as pltpu
from jax.sharding import PartitionSpec as P

EDGE = 72
LANES = 128
TAIL = 1280
F32 = jnp.float32
BF16 = jnp.bfloat16
VMEM = pl.BlockSpec(memory_space=pltpu.VMEM)
HBM = pl.BlockSpec(memory_space=pl.ANY)
NN = (((1,), (0,)), ((), ()))
NT = (((1,), (1,)), ((), ()))


def split(value):
    high = value.astype(BF16)
    low = (value - high.astype(F32)).astype(BF16)
    return high, low


def dot(left, right, dims):
    return lax.dot_general(left, right, dims, preferred_element_type=F32)


def dot_pairs(left, right, dims):
    rows = left[0].shape[0]
    both = dot(jnp.concatenate(left, axis=0), right[0], dims)
    return both[:rows] + both[rows:] + dot(left[0], right[1], dims)


def dot_exact(left, right, dims):
    rows = left[0].shape[0]
    both = dot(jnp.concatenate(left, axis=0), right, dims)
    return both[:rows] + both[rows:]


def pick(flag, when_even, when_odd):
    return jnp.where(flag[:, : when_even.shape[1]] == 0, when_even, when_odd)


def call(kernel, out, in_specs, scratch=(), flops=0, moved=0, name=None, out_specs=None, limit=20):
    return pl.pallas_call(
        kernel,
        out_shape=out,
        in_specs=in_specs,
        out_specs=jax.tree.map(lambda _: VMEM, out) if out_specs is None else out_specs,
        scratch_shapes=list(scratch),
        compiler_params=pltpu.CompilerParams(vmem_limit_bytes=limit * 1024 * 1024),
        cost_estimate=pl.CostEstimate(flops=flops, bytes_accessed=moved, transcendentals=0),
        name=name,
    )


def shaped(*shape, dtype=F32):
    return jax.ShapeDtypeStruct(shape, dtype)


def in_hbm(value):
    return pltpu.with_memory_space_constraint(value, pltpu.HBM)


def gather_kernel(
    odd, count_hbm, rows_hbm, res_hbm, factor, sxb, sxa, sya, syb, field, ids, slab, count, rows, res, sem
):
    fetch_count = pltpu.make_async_copy(count_hbm, count, sem.at[0])
    fetch_rows = pltpu.make_async_copy(rows_hbm, rows, sem.at[1])
    fetch_res = pltpu.make_async_copy(res_hbm, res, sem.at[2])
    fetch_count.start()
    fetch_rows.start()
    fetch_res.start()
    fetch_slab = pltpu.make_async_copy(factor.at[0, 0, pl.ds(TAIL, 320), :], slab, sem.at[3])
    fetch_slab.start()
    lane = lax.broadcasted_iota(jnp.int32, (1, LANES), 1)
    fetch_count.wait()
    fetch_rows.wait()
    table = rows[0, 0]

    def live(n):
        return count[0, 0, n]

    def edge(n):
        return jnp.where(lane < live(n), table[n : n + 1], -1)

    def corner(base, n, at):
        moved = pltpu.roll(table, at, 1)[n : n + 1]
        return jnp.where((lane >= at) & (lane < at + live(n)), moved, base)

    down = corner(corner(edge(0), 4, 72), 5, 80)
    up = corner(corner(edge(1), 6, 76), 7, 84)
    right, left = edge(2), edge(3)
    lists = [
        pick(odd[0:1], down, up),
        pick(odd[0:1], up, down),
        pick(odd[1:2], right, left),
        pick(odd[1:2], left, right),
    ]
    for k, values in enumerate(lists + lists):
        ids[k : k + 1] = values
    own = res.shape[1]
    row = lax.broadcasted_iota(jnp.int32, (own, LANES), 0)
    ones = [jnp.where(row == values, 1.0, 0.0).astype(BF16) for values in lists]
    onehot = jnp.concatenate(ones, axis=1)
    fetch_res.wait()
    high, low = split(res[...])
    field[:96] = high
    field[96:] = low
    packed = dot(field[...], onehot, NN)
    packed = packed[:96] + packed[96:]
    for k, out in enumerate((sxa, sxb, sya, syb)):
        out[...] = packed[:, k * LANES : (k + 1) * LANES]
    fetch_slab.wait()


def halo_place():
    col = lax.broadcasted_iota(jnp.int32, (320, 4 * LANES), 0) - 16
    spot = lax.broadcasted_iota(jnp.int32, (1, 4 * LANES), 1)
    lane = spot % LANES
    block = spot // LANES
    source = jnp.where(lane < EDGE, block * EDGE + lane, -99)
    for n, b, at in ((4, 2, 72), (6, 2, 76), (5, 3, 80), (7, 3, 84)):
        inside = (block == b) & (lane >= at) & (lane < at + 4)
        source = jnp.where(inside, 4 * EDGE + (n - 4) * 4 + lane - at, source)
    return jnp.where(col == source, 1.0, 0.0).astype(BF16)


def fetch(pairs, sem):
    copies = [pltpu.make_async_copy(source, dest, sem.at[k]) for k, (source, dest) in enumerate(pairs)]
    for copy in copies:
        copy.start()
    return copies


def own_slab(factor, k):
    return factor.at[0, 0, pl.ds(256 * k, 256), pl.ds(0, 256 * (k + 1))]


def tail_kernel(
    field, slab, factor, ritz_hbm, search_hbm, part, ph, plo, th, tlo, oh, olo, ritz, search, slab0, slab1, sem
):
    slabs = [(own_slab(factor, k), dest) for k, dest in enumerate((slab0, slab1))]
    copies = fetch([(ritz_hbm, ritz), (search_hbm, search)] + slabs, sem)
    place = halo_place()
    own = field.shape[1]
    oh[...], olo[...] = split(slab[:, :own])
    part[...] = dot_pairs((field[:96], field[96:]), (oh[...], olo[...]), NT)
    for value, out, turned in zip(split(slab[:, TAIL:]), (ph, plo), (th, tlo)):
        placed = dot(value, place, NN)
        out[...] = placed.astype(BF16)
        turned[...] = placed.T.astype(BF16)
    for copy in copies:
        copy.wait()


def halo_kernel(odd, sxa, sxb, sya, syb, part, ph, plo, th, tlo, given, half, bxa, bxb, bya, byb):
    xa, xb, ya, yb = sxa[...], sxb[...], sya[...], syb[...]
    arrived = jnp.concatenate(
        [pick(odd[0:1], xb, xa), pick(odd[0:1], xa, xb), pick(odd[1:2], yb, ya), pick(odd[1:2], ya, yb)], axis=1
    )
    solved = part[...] + dot_pairs(split(arrived), (th[...], tlo[...]), NN)
    half[...] = solved
    back = dot_pairs(split(solved), (ph[...], plo[...]), NN)
    b = [back[:, k * LANES : (k + 1) * LANES] for k in range(4)]
    bxa[...] = pick(odd[0:1], b[1], b[0])
    bxb[...] = pick(odd[0:1], b[0], b[1])
    bya[:96] = pick(odd[1:2], b[3], b[2])
    bya[96:] = given[...]
    byb[...] = pick(odd[1:2], b[2], b[3])


def slab_term(field, slab):
    width = slab.shape[1]
    block = split(slab[...])
    solved = dot_pairs((field[:96, :width], field[96:, :width]), block, NT)
    return dot_pairs(split(solved), block, NN)


def head_kernel(field, slab0, slab1, out):
    out[...] = slab_term(field, slab1)
    out[:, :256] = out[:, :256] + slab_term(field, slab0)


def last_kernel(field, slab3, head, factor, out, slab2, slab4, sem):
    copies = fetch([(own_slab(factor, 2), slab2), (own_slab(factor, 4), slab4)], sem)
    out[:, :1024] = slab_term(field, slab3)
    out[:, :512] = out[:, :512] + head[...]
    copies[0].wait()
    out[:, :768] = out[:, :768] + slab_term(field, slab2)
    copies[1].wait()
    term = slab_term(field, slab4)
    out[:, :1024] = out[:, :1024] + term[:, :1024]
    out[:, 1024:] = term[:, 1024:]


def distinct_tiles(square):
    tiles = [square[32 * i : 32 * i + 32, 32 * j : 32 * j + 32] for i in range(3) for j in range(i, 3)]
    return jnp.concatenate(tiles, axis=0)


def whole_square(tiles):
    t = [tiles[32 * k : 32 * k + 32] for k in range(6)]
    blank = jnp.zeros((32, 32), F32)
    upper = jnp.concatenate(
        [
            jnp.concatenate([t[0], t[1], t[2]], axis=1),
            jnp.concatenate([blank, t[3], t[4]], axis=1),
            jnp.concatenate([blank, blank, t[5]], axis=1),
        ],
        axis=0,
    )
    row = lax.broadcasted_iota(jnp.int32, (96, 96), 0) // 32
    col = lax.broadcasted_iota(jnp.int32, (96, 96), 1) // 32
    return jnp.where(row <= col, upper, upper.T)


def side_kernel(
    odd, ids, ritz, search, factor, held, given, turned, same, sides_h, sides_l, rgh, rgl, slab3, sem
):
    copies = fetch([(own_slab(factor, 3), slab3)], sem)
    own = ritz.shape[1]
    numbers = ids[...].astype(F32)
    columns = numbers.T
    live = jnp.where(columns < 0.0, -2.0, columns)
    across = lax.broadcasted_iota(jnp.int32, (LANES, own), 1).astype(F32)
    for k in range(4):
        lanes = slice(k * LANES, (k + 1) * LANES)
        turned[lanes] = jnp.where(columns[:, k : k + 1] == across, 1.0, 0.0).astype(BF16)
        for j in range(4):
            agree = live[:, k : k + 1] == numbers[j : j + 1]
            same[lanes, j * LANES : (j + 1) * LANES] = jnp.where(agree, 1.0, 0.0).astype(BF16)
    blank = jnp.zeros((32, own), BF16)
    for r, s, out in zip(split(ritz[...]), split(search[...]), (sides_h, sides_l)):
        out[:96] = r
        out[96:128] = blank
        out[128:224] = s
        out[224:] = blank
    for side, out in zip((sides_h, sides_l), (rgh, rgl)):
        out[...] = dot(turned[...], side[...], NT).astype(BF16)
    pair = (sides_h[...], sides_l[...])
    cross = dot_pairs(pair, pair, NT)
    rr, sr, ss = cross[:96, :96], cross[128:224, :96], cross[128:224, LANES : LANES + 96]
    rt, st = distinct_tiles(rr), distinct_tiles(ss)
    first = jnp.concatenate([sr, rt[:96]], axis=1)
    second = jnp.concatenate([rt[96:], st[:96], st[96:], jnp.zeros((96, 32), F32)], axis=1)
    held[...] = pick(odd[1:2], first, second)
    given[...] = pick(odd[1:2], second, first)
    for copy in copies:
        copy.wait()


def local_kernel(own_part, half, oh, olo, turned, sides_h, sides_l, local, sent, base):
    add = dot_pairs(split(half[...]), (oh[...], olo[...]), NN)
    value = add + jnp.concatenate([own_part[...], jnp.zeros((96, add.shape[1] - TAIL), F32)], axis=1)
    local[...] = value
    pair = split(value)
    sent[...] = dot_exact(pair, turned[...], NT)
    base[:96] = dot_pairs(pair, pair, NT)
    cross = dot_pairs(pair, (sides_h[...], sides_l[...]), NT)
    base[96:192] = cross[:, :96]
    base[192:] = cross[:, LANES : LANES + 96]


def gram_kernel(odd, rxa, rxb, rya, ryb, same, sent, rgh, rgl, base, held, away, kept, back):
    back[...] = jnp.concatenate([rxa[...], rxb[...], rya[:96], ryb[...]], axis=1)
    pair = split(back[...])
    mixed = sent[...] + 0.5 * dot_exact(pair, same[...], NN)
    square = dot_pairs(split(mixed), pair, NT)
    cross = dot_pairs(pair, (rgh[...], rgl[...]), NN)
    pp = base[:96] + square + square.T
    pr = base[96:192] + cross[:, :96]
    ps = base[192:] + cross[:, LANES : LANES + 96]
    tiles = distinct_tiles(pp)
    first = jnp.concatenate([pr, tiles[:96]], axis=1)
    second = jnp.concatenate([ps, tiles[96:]], axis=1)
    kept[:96] = pick(odd[0:1], first, second)
    away[:96] = pick(odd[0:1], second, first)
    early = held[...] + rya[96:]
    kept[96:] = pick(odd[0:1], early[:48], early[48:])
    away[96:] = pick(odd[0:1], early[48:], early[:48])


def update_kernel(back, turned, local, precond):
    precond[...] = local[...] + dot_exact(split(back[...]), turned[...], NN)


def final_kernel(scale, odd, mine, other, gram, out, sem):
    def by_core(rows):
        a, b = mine[rows], other[rows]
        return pick(odd[0:1], a, b) * scale, pick(odd[0:1], b, a) * scale

    late = by_core(slice(0, 96))
    near, far = by_core(slice(96, 144)), by_core(slice(144, 192))
    near, far = jnp.concatenate(near, axis=0), jnp.concatenate(far, axis=0)
    first, second = pick(odd[1:2], near, far), pick(odd[1:2], far, near)
    pr, ps = late[0][:, :96], late[1][:, :96]
    pp = whole_square(jnp.concatenate([late[0][:, 96:], late[1][:, 96:]], axis=0))
    sr = first[:, :96]
    rr = whole_square(jnp.concatenate([first[:, 96:], second[:, :32]], axis=0))
    ss = whole_square(jnp.concatenate([second[:, 32:64], second[:, 64:96]], axis=0))
    copies = []
    bands = ([pr, pp, ps], [rr, pr.T, sr.T], [sr, ps.T, ss])
    for k, parts in zip((1, 0, 2), bands):
        rows = slice(96 * k, 96 * (k + 1))
        out[rows] = jnp.concatenate(parts, axis=1)
        copies.append(pltpu.make_async_copy(out.at[rows], gram.at[rows], sem.at[k]))
        copies[-1].start()
    for copy in copies:
        copy.wait()


def swap(block, axis, step):
    return lax.ppermute(block, axis, [(i, i ^ step) for i in range(lax.axis_size(axis))])


def swap_odd(block, axis):
    size = lax.axis_size(axis)
    route = [(i, (i + 1) % size) for i in range(1, size, 2)]
    return lax.ppermute(block, axis, route + [(b, a) for a, b in route])


def body(residual, ritz_block, search_block, inverse_factor, send_rows, send_count):
    own = residual.shape[1]
    p, q = lax.axis_index("sx"), lax.axis_index("sy")
    odd = jnp.where(jnp.arange(8)[:, None] == 0, p % 2, q % 2) + jnp.zeros((8, LANES), jnp.int32)
    lane = jnp.arange(LANES)[None, :]
    msg = shaped(96, LANES)

    factor = in_hbm(inverse_factor)
    sxb, sxa, sya, syb, field, ids, slab = call(
        gather_kernel,
        (
            msg,
            msg,
            msg,
            msg,
            shaped(192, own, dtype=BF16),
            shaped(8, LANES, dtype=jnp.int32),
            shaped(320, 1600),
        ),
        [VMEM, HBM, HBM, HBM, HBM],
        [
            pltpu.SMEM((1, 1, 8), jnp.int32),
            pltpu.VMEM((1, 1, 8, LANES), jnp.int32),
            pltpu.VMEM((96, own), F32),
            pltpu.SemaphoreType.DMA((4,)),
        ],
        flops=2 * 192 * 1296 * 512,
        moved=2000000,
        name="gather",
    )(odd, in_hbm(send_count), in_hbm(send_rows), in_hbm(residual), factor)

    gxb, gxa = swap_odd(sxb, "sx"), swap(sxa, "sx", 1)

    placed, turned = shaped(320, 512, dtype=BF16), shaped(512, 320, dtype=BF16)
    wide = shaped(320, own, dtype=BF16)
    part, ph, plo, th, tlo, oh, olo, ritz, search, slab0, slab1 = call(
        tail_kernel,
        (shaped(96, 320), placed, placed, turned, turned, wide, wide)
        + (shaped(96, own), shaped(96, own), shaped(256, 256), shaped(256, 512)),
        [VMEM, VMEM, HBM, HBM, HBM],
        [pltpu.SemaphoreType.DMA((4,))],
        flops=2 * 96 * 1296 * 320 * 3,
        moved=6000000,
        name="tail",
    )(field, slab, factor, in_hbm(ritz_block), in_hbm(search_block))
    gxb, gxa, part = lax.optimization_barrier((gxb, gxa, part))

    relay = jnp.where(lane >= EDGE, gxb + gxa, 0.0)
    gyb, gya = swap_odd(syb + relay, "sy"), swap(sya + relay, "sy", 1)

    sides, sent_sides = shaped(2 * LANES, own, dtype=BF16), shaped(512, 2 * LANES, dtype=BF16)
    held, given, turned, same, sides_h, sides_l, rgh, rgl, slab3 = call(
        side_kernel,
        (
            msg,
            msg,
            shaped(512, own, dtype=BF16),
            shaped(512, 512, dtype=BF16),
            sides,
            sides,
            sent_sides,
            sent_sides,
            shaped(256, 1024),
        ),
        [VMEM] + [VMEM] * 3 + [HBM],
        [pltpu.SemaphoreType.DMA((1,))],
        flops=2 * 192 * 256 * 1296 * 3,
        moved=3000000,
        name="side",
    )(odd, ids, ritz, search, factor)

    head = call(
        head_kernel,
        shaped(96, 512),
        [VMEM] * 3,
        flops=2 * 2 * 96 * 256 * 256 * 3 * 3,
        moved=1200000,
        name="head",
    )(field, slab0, slab1)
    gya, gyb, head = lax.optimization_barrier((gya, gyb, head))

    half, bxa, bxb, bya, byb = call(
        halo_kernel,
        (shaped(96, 320), msg, msg, shaped(192, LANES), msg),
        [VMEM] + [VMEM] * 10,
        flops=2 * 2 * 96 * 320 * 512 * 3,
        moved=1000000,
        name="halo",
    )(odd, gxa, gxb, gya, gyb, part, ph, plo, th, tlo, given)

    ryb, rya = swap_odd(byb, "sy"), swap(bya, "sy", 1)

    own_part = call(
        last_kernel,
        shaped(96, TAIL),
        [VMEM] * 3 + [HBM],
        [pltpu.VMEM((256, 768), F32), pltpu.VMEM((256, TAIL), F32), pltpu.SemaphoreType.DMA((2,))],
        flops=2 * 2 * 96 * 256 * 256 * 12 * 3,
        moved=3000000,
        name="last",
    )(field, slab3, head, factor)
    rya, ryb, own_part = lax.optimization_barrier((rya, ryb, own_part))

    relay = jnp.where(lane >= EDGE, rya[:96] + ryb, 0.0)
    rxb, rxa = swap_odd(bxb + relay, "sx"), swap(bxa + relay, "sx", 1)

    local, sent, base = call(
        local_kernel,
        (shaped(96, own), shaped(96, 512), shaped(288, 96)),
        [VMEM] * 7,
        flops=2 * 96 * 1296 * 1100 * 3,
        moved=4000000,
        name="local",
    )(own_part, half, oh, olo, turned, sides_h, sides_l)

    away, kept, back = call(
        gram_kernel,
        (shaped(144, LANES), shaped(144, LANES), shaped(96, 512)),
        [VMEM] + [VMEM] * 10,
        flops=2 * 96 * 512 * 900 * 3,
        moved=2000000,
        name="gram",
    )(odd, rxa, rxb, rya, ryb, same, sent, rgh, rgl, base, held)

    precond = call(
        update_kernel,
        shaped(96, own),
        [VMEM] * 3,
        flops=2 * 192 * 1296 * 512,
        moved=3000000,
        name="update",
    )(back, turned, local)

    rows, cols = lax.axis_size("sx"), lax.axis_size("sy")

    def swap_apart(value, even_core, odd_core):
        route = []
        for r in range(rows):
            for c in range(cols):
                row_step, col_step = odd_core if r % 2 else even_core
                route.append((r * cols + c, (r ^ row_step) * cols + (c ^ col_step)))
        return lax.ppermute(value, ("sx", "sy"), route)

    def summed(value, even_cores, odd_cores):
        total = swap_apart(value, even_cores[0], odd_cores[0])
        for even_core, odd_core in zip(even_cores[1:], odd_cores[1:]):
            total = total + swap_apart(value, even_core, odd_core)
        return value + total

    along_y = [(2 * step, 0) for step in (1, 3, 2)]
    along_x = [(0, 8 * step) for step in (1, 3, 2)]
    total = kept + swap(away, "sx", 1)
    total = summed(total, along_y, along_x)
    total = summed(total, along_x, along_y)
    total = summed(total, [(0, 6)], [(0, 2)])
    total, precond = lax.optimization_barrier((total, precond))
    three = swap_apart(total, (0, 3), (0, 7))
    two = swap_apart(total, (0, 2), (0, 6))
    one = swap_apart(total, (0, 1), (0, 1))
    late = (total[:96] + one[:96]) + (two[:96] + three[:96])
    mine = jnp.concatenate([late, total[96:] + two[96:], one[96:] + three[96:]], axis=0)
    other = swap(mine, "sx", 1)

    vertex_total = own * lax.axis_size("sx") * lax.axis_size("sy")

    def finish(odd, *refs):
        final_kernel(1.0 / vertex_total, odd, *refs)

    gram = call(
        finish,
        shaped(288, 288),
        [VMEM] * 3,
        [pltpu.VMEM((288, 288), F32), pltpu.SemaphoreType.DMA((3,))],
        flops=1000000,
        moved=700000,
        name="final",
        out_specs=HBM,
    )(odd, mine, other)
    return precond, gram


def solution(mesh):
    placed = (
        P(None, ("sx", "sy")),
        P(None, ("sx", "sy")),
        P(None, ("sx", "sy")),
        P("sx", "sy", None, None),
        P("sx", "sy", None, None),
        P("sx", "sy", None),
    )
    return jax.shard_map(
        body, mesh=mesh, in_specs=placed, out_specs=(P(None, ("sx", "sy")), P()), check_vma=False
    )
```

```python
import jax
import jax.numpy as jnp
from jax import lax
from jax.experimental import pallas as pl
from jax.experimental.pallas import tpu as pltpu
from jax.sharding import PartitionSpec as P

EDGE = 72
LANES = 128
TAIL = 1280
F32 = jnp.float32
BF16 = jnp.bfloat16
VMEM = pl.BlockSpec(memory_space=pltpu.VMEM)
HBM = pl.BlockSpec(memory_space=pl.ANY)
NN = (((1,), (0,)), ((), ()))
NT = (((1,), (1,)), ((), ()))


def split(value):
    high = value.astype(BF16)
    low = (value - high.astype(F32)).astype(BF16)
    return high, low


def dot(left, right, dims):
    return lax.dot_general(left, right, dims, preferred_element_type=F32)


def dot_pairs(left, right, dims):
    rows = left[0].shape[0]
    both = dot(jnp.concatenate(left, axis=0), right[0], dims)
    return both[:rows] + both[rows:] + dot(left[0], right[1], dims)


def dot_exact(left, right, dims):
    rows = left[0].shape[0]
    both = dot(jnp.concatenate(left, axis=0), right, dims)
    return both[:rows] + both[rows:]


def pick(flag, when_even, when_odd):
    return jnp.where(flag[:, : when_even.shape[1]] == 0, when_even, when_odd)


def call(kernel, out, in_specs, scratch=(), flops=0, moved=0, name=None, out_specs=None, limit=20):
    return pl.pallas_call(
        kernel,
        out_shape=out,
        in_specs=in_specs,
        out_specs=jax.tree.map(lambda _: VMEM, out) if out_specs is None else out_specs,
        scratch_shapes=list(scratch),
        compiler_params=pltpu.CompilerParams(vmem_limit_bytes=limit * 1024 * 1024),
        cost_estimate=pl.CostEstimate(flops=flops, bytes_accessed=moved, transcendentals=0),
        name=name,
    )


def shaped(*shape, dtype=F32):
    return jax.ShapeDtypeStruct(shape, dtype)


def in_hbm(value):
    return pltpu.with_memory_space_constraint(value, pltpu.HBM)


def gather_kernel(
    odd, count_hbm, rows_hbm, res_hbm, factor, sxb, sxa, sya, syb, field, ids, slab, count, rows, res, sem
):
    fetch_count = pltpu.make_async_copy(count_hbm, count, sem.at[0])
    fetch_rows = pltpu.make_async_copy(rows_hbm, rows, sem.at[1])
    fetch_res = pltpu.make_async_copy(res_hbm, res, sem.at[2])
    fetch_count.start()
    fetch_rows.start()
    fetch_res.start()
    fetch_slab = pltpu.make_async_copy(factor.at[0, 0, pl.ds(TAIL, 320), :], slab, sem.at[3])
    fetch_slab.start()
    lane = lax.broadcasted_iota(jnp.int32, (1, LANES), 1)
    fetch_count.wait()
    fetch_rows.wait()
    table = rows[0, 0]

    def live(n):
        return count[0, 0, n]

    def edge(n):
        return jnp.where(lane < live(n), table[n : n + 1], -1)

    def corner(base, n, at):
        moved = pltpu.roll(table, at, 1)[n : n + 1]
        return jnp.where((lane >= at) & (lane < at + live(n)), moved, base)

    down = corner(corner(edge(0), 4, 72), 5, 80)
    up = corner(corner(edge(1), 6, 76), 7, 84)
    right, left = edge(2), edge(3)
    lists = [
        pick(odd[0:1], down, up),
        pick(odd[0:1], up, down),
        pick(odd[1:2], right, left),
        pick(odd[1:2], left, right),
    ]
    for k, values in enumerate(lists + lists):
        ids[k : k + 1] = values
    own = res.shape[1]
    row = lax.broadcasted_iota(jnp.int32, (own, LANES), 0)
    ones = [jnp.where(row == values, 1.0, 0.0).astype(BF16) for values in lists]
    onehot = jnp.concatenate(ones, axis=1)
    fetch_res.wait()
    high, low = split(res[...])
    field[:96] = high
    field[96:] = low
    packed = dot(field[...], onehot, NN)
    packed = packed[:96] + packed[96:]
    for k, out in enumerate((sxa, sxb, sya, syb)):
        out[...] = packed[:, k * LANES : (k + 1) * LANES]
    fetch_slab.wait()


def halo_place():
    col = lax.broadcasted_iota(jnp.int32, (320, 4 * LANES), 0) - 16
    spot = lax.broadcasted_iota(jnp.int32, (1, 4 * LANES), 1)
    lane = spot % LANES
    block = spot // LANES
    source = jnp.where(lane < EDGE, block * EDGE + lane, -99)
    for n, b, at in ((4, 2, 72), (6, 2, 76), (5, 3, 80), (7, 3, 84)):
        inside = (block == b) & (lane >= at) & (lane < at + 4)
        source = jnp.where(inside, 4 * EDGE + (n - 4) * 4 + lane - at, source)
    return jnp.where(col == source, 1.0, 0.0).astype(BF16)


def fetch(pairs, sem):
    copies = [pltpu.make_async_copy(source, dest, sem.at[k]) for k, (source, dest) in enumerate(pairs)]
    for copy in copies:
        copy.start()
    return copies


def own_slab(factor, k):
    return factor.at[0, 0, pl.ds(256 * k, 256), pl.ds(0, 256 * (k + 1))]


def tail_kernel(
    field, slab, factor, ritz_hbm, search_hbm, part, ph, plo, th, tlo, oh, olo, ritz, search, slab0, slab1, sem
):
    slabs = [(own_slab(factor, k), dest) for k, dest in enumerate((slab0, slab1))]
    copies = fetch([(ritz_hbm, ritz), (search_hbm, search)] + slabs, sem)
    place = halo_place()
    own = field.shape[1]
    oh[...], olo[...] = split(slab[:, :own])
    part[...] = dot_pairs((field[:96], field[96:]), (oh[...], olo[...]), NT)
    for value, out, turned in zip(split(slab[:, TAIL:]), (ph, plo), (th, tlo)):
        placed = dot(value, place, NN)
        out[...] = placed.astype(BF16)
        turned[...] = placed.T.astype(BF16)
    for copy in copies:
        copy.wait()


def halo_kernel(odd, sxa, sxb, sya, syb, part, ph, plo, th, tlo, given, half, bxa, bxb, bya, byb):
    xa, xb, ya, yb = sxa[...], sxb[...], sya[...], syb[...]
    arrived = jnp.concatenate(
        [pick(odd[0:1], xb, xa), pick(odd[0:1], xa, xb), pick(odd[1:2], yb, ya), pick(odd[1:2], ya, yb)], axis=1
    )
    solved = part[...] + dot_pairs(split(arrived), (th[...], tlo[...]), NN)
    half[...] = solved
    back = dot_pairs(split(solved), (ph[...], plo[...]), NN)
    b = [back[:, k * LANES : (k + 1) * LANES] for k in range(4)]
    bxa[...] = pick(odd[0:1], b[1], b[0])
    bxb[...] = pick(odd[0:1], b[0], b[1])
    bya[:96] = pick(odd[1:2], b[3], b[2])
    bya[96:] = given[...]
    byb[...] = pick(odd[1:2], b[2], b[3])


def slab_term(field, slab):
    width = slab.shape[1]
    block = split(slab[...])
    solved = dot_pairs((field[:96, :width], field[96:, :width]), block, NT)
    return dot_pairs(split(solved), block, NN)


def head_kernel(field, slab0, slab1, out):
    out[...] = slab_term(field, slab1)
    out[:, :256] = out[:, :256] + slab_term(field, slab0)


def last_kernel(field, slab3, head, factor, out, slab2, slab4, sem):
    copies = fetch([(own_slab(factor, 2), slab2), (own_slab(factor, 4), slab4)], sem)
    out[:, :1024] = slab_term(field, slab3)
    out[:, :512] = out[:, :512] + head[...]
    copies[0].wait()
    out[:, :768] = out[:, :768] + slab_term(field, slab2)
    copies[1].wait()
    term = slab_term(field, slab4)
    out[:, :1024] = out[:, :1024] + term[:, :1024]
    out[:, 1024:] = term[:, 1024:]


def distinct_tiles(square):
    tiles = [square[32 * i : 32 * i + 32, 32 * j : 32 * j + 32] for i in range(3) for j in range(i, 3)]
    return jnp.concatenate(tiles, axis=0)


def whole_square(tiles):
    t = [tiles[32 * k : 32 * k + 32] for k in range(6)]
    blank = jnp.zeros((32, 32), F32)
    upper = jnp.concatenate(
        [
            jnp.concatenate([t[0], t[1], t[2]], axis=1),
            jnp.concatenate([blank, t[3], t[4]], axis=1),
            jnp.concatenate([blank, blank, t[5]], axis=1),
        ],
        axis=0,
    )
    row = lax.broadcasted_iota(jnp.int32, (96, 96), 0) // 32
    col = lax.broadcasted_iota(jnp.int32, (96, 96), 1) // 32
    return jnp.where(row <= col, upper, upper.T)


def side_kernel(
    odd, ids, ritz, search, factor, held, given, turned, same, sides_h, sides_l, rgh, rgl, slab3, sem
):
    copies = fetch([(own_slab(factor, 3), slab3)], sem)
    own = ritz.shape[1]
    numbers = ids[...].astype(F32)
    columns = numbers.T
    live = jnp.where(columns < 0.0, -2.0, columns)
    across = lax.broadcasted_iota(jnp.int32, (LANES, own), 1).astype(F32)
    for k in range(4):
        lanes = slice(k * LANES, (k + 1) * LANES)
        turned[lanes] = jnp.where(columns[:, k : k + 1] == across, 1.0, 0.0).astype(BF16)
        for j in range(4):
            agree = live[:, k : k + 1] == numbers[j : j + 1]
            same[lanes, j * LANES : (j + 1) * LANES] = jnp.where(agree, 1.0, 0.0).astype(BF16)
    blank = jnp.zeros((32, own), BF16)
    for r, s, out in zip(split(ritz[...]), split(search[...]), (sides_h, sides_l)):
        out[:96] = r
        out[96:128] = blank
        out[128:224] = s
        out[224:] = blank
    for side, out in zip((sides_h, sides_l), (rgh, rgl)):
        out[...] = dot(turned[...], side[...], NT).astype(BF16)
    pair = (sides_h[...], sides_l[...])
    cross = dot_pairs(pair, pair, NT)
    rr, sr, ss = cross[:96, :96], cross[128:224, :96], cross[128:224, LANES : LANES + 96]
    rt, st = distinct_tiles(rr), distinct_tiles(ss)
    first = jnp.concatenate([sr, rt[:96]], axis=1)
    second = jnp.concatenate([rt[96:], st[:96], st[96:], jnp.zeros((96, 32), F32)], axis=1)
    held[...] = pick(odd[1:2], first, second)
    given[...] = pick(odd[1:2], second, first)
    for copy in copies:
        copy.wait()


def local_kernel(own_part, half, oh, olo, turned, sides_h, sides_l, local, sent, base):
    add = dot_pairs(split(half[...]), (oh[...], olo[...]), NN)
    value = add + jnp.concatenate([own_part[...], jnp.zeros((96, add.shape[1] - TAIL), F32)], axis=1)
    local[...] = value
    pair = split(value)
    sent[...] = dot_exact(pair, turned[...], NT)
    base[:96] = dot_pairs(pair, pair, NT)
    cross = dot_pairs(pair, (sides_h[...], sides_l[...]), NT)
    base[96:192] = cross[:, :96]
    base[192:] = cross[:, LANES : LANES + 96]


def gram_kernel(odd, rxa, rxb, rya, ryb, same, sent, rgh, rgl, base, held, away, kept, back):
    back[...] = jnp.concatenate([rxa[...], rxb[...], rya[:96], ryb[...]], axis=1)
    pair = split(back[...])
    mixed = sent[...] + 0.5 * dot_exact(pair, same[...], NN)
    square = dot_pairs(split(mixed), pair, NT)
    cross = dot_pairs(pair, (rgh[...], rgl[...]), NN)
    pp = base[:96] + square + square.T
    pr = base[96:192] + cross[:, :96]
    ps = base[192:] + cross[:, LANES : LANES + 96]
    tiles = distinct_tiles(pp)
    first = jnp.concatenate([pr, tiles[:96]], axis=1)
    second = jnp.concatenate([ps, tiles[96:]], axis=1)
    kept[:96] = pick(odd[0:1], first, second)
    away[:96] = pick(odd[0:1], second, first)
    early = held[...] + rya[96:]
    kept[96:] = pick(odd[0:1], early[:48], early[48:])
    away[96:] = pick(odd[0:1], early[48:], early[:48])


def update_kernel(back, turned, local, precond):
    precond[...] = local[...] + dot_exact(split(back[...]), turned[...], NN)


def final_kernel(scale, odd, mine, other, gram, out, sem):
    def by_core(rows):
        a, b = mine[rows], other[rows]
        return pick(odd[0:1], a, b) * scale, pick(odd[0:1], b, a) * scale

    late = by_core(slice(0, 96))
    near, far = by_core(slice(96, 144)), by_core(slice(144, 192))
    near, far = jnp.concatenate(near, axis=0), jnp.concatenate(far, axis=0)
    first, second = pick(odd[1:2], near, far), pick(odd[1:2], far, near)
    pr, ps = late[0][:, :96], late[1][:, :96]
    pp = whole_square(jnp.concatenate([late[0][:, 96:], late[1][:, 96:]], axis=0))
    sr = first[:, :96]
    rr = whole_square(jnp.concatenate([first[:, 96:], second[:, :32]], axis=0))
    ss = whole_square(jnp.concatenate([second[:, 32:64], second[:, 64:96]], axis=0))
    copies = []
    bands = ([pr, pp, ps], [rr, pr.T, sr.T], [sr, ps.T, ss])
    for k, parts in zip((1, 0, 2), bands):
        rows = slice(96 * k, 96 * (k + 1))
        out[rows] = jnp.concatenate(parts, axis=1)
        copies.append(pltpu.make_async_copy(out.at[rows], gram.at[rows], sem.at[k]))
        copies[-1].start()
    for copy in copies:
        copy.wait()


def swap(block, axis, step):
    return lax.ppermute(block, axis, [(i, i ^ step) for i in range(lax.axis_size(axis))])


def swap_odd(block, axis):
    size = lax.axis_size(axis)
    route = [(i, (i + 1) % size) for i in range(1, size, 2)]
    return lax.ppermute(block, axis, route + [(b, a) for a, b in route])


def body(residual, ritz_block, search_block, inverse_factor, send_rows, send_count):
    own = residual.shape[1]
    p, q = lax.axis_index("sx"), lax.axis_index("sy")
    odd = jnp.where(jnp.arange(8)[:, None] == 0, p % 2, q % 2) + jnp.zeros((8, LANES), jnp.int32)
    lane = jnp.arange(LANES)[None, :]
    msg = shaped(96, LANES)

    factor = in_hbm(inverse_factor)
    sxb, sxa, sya, syb, field, ids, slab = call(
        gather_kernel,
        (
            msg,
            msg,
            msg,
            msg,
            shaped(192, own, dtype=BF16),
            shaped(8, LANES, dtype=jnp.int32),
            shaped(320, 1600),
        ),
        [VMEM, HBM, HBM, HBM, HBM],
        [
            pltpu.SMEM((1, 1, 8), jnp.int32),
            pltpu.VMEM((1, 1, 8, LANES), jnp.int32),
            pltpu.VMEM((96, own), F32),
            pltpu.SemaphoreType.DMA((4,)),
        ],
        flops=2 * 192 * 1296 * 512,
        moved=2000000,
        name="gather",
    )(odd, in_hbm(send_count), in_hbm(send_rows), in_hbm(residual), factor)

    gxb, gxa = swap_odd(sxb, "sx"), swap(sxa, "sx", 1)

    placed, turned = shaped(320, 512, dtype=BF16), shaped(512, 320, dtype=BF16)
    wide = shaped(320, own, dtype=BF16)
    part, ph, plo, th, tlo, oh, olo, ritz, search, slab0, slab1 = call(
        tail_kernel,
        (shaped(96, 320), placed, placed, turned, turned, wide, wide)
        + (shaped(96, own), shaped(96, own), shaped(256, 256), shaped(256, 512)),
        [VMEM, VMEM, HBM, HBM, HBM],
        [pltpu.SemaphoreType.DMA((4,))],
        flops=2 * 96 * 1296 * 320 * 3,
        moved=6000000,
        name="tail",
    )(field, slab, factor, in_hbm(ritz_block), in_hbm(search_block))
    gxb, gxa, part = lax.optimization_barrier((gxb, gxa, part))

    relay = jnp.where(lane >= EDGE, gxb + gxa, 0.0)
    gyb, gya = swap_odd(syb + relay, "sy"), swap(sya + relay, "sy", 1)

    sides, sent_sides = shaped(2 * LANES, own, dtype=BF16), shaped(512, 2 * LANES, dtype=BF16)
    held, given, turned, same, sides_h, sides_l, rgh, rgl, slab3 = call(
        side_kernel,
        (
            msg,
            msg,
            shaped(512, own, dtype=BF16),
            shaped(512, 512, dtype=BF16),
            sides,
            sides,
            sent_sides,
            sent_sides,
            shaped(256, 1024),
        ),
        [VMEM] + [VMEM] * 3 + [HBM],
        [pltpu.SemaphoreType.DMA((1,))],
        flops=2 * 192 * 256 * 1296 * 3,
        moved=3000000,
        name="side",
    )(odd, ids, ritz, search, factor)

    head = call(
        head_kernel,
        shaped(96, 512),
        [VMEM] * 3,
        flops=2 * 2 * 96 * 256 * 256 * 3 * 3,
        moved=1200000,
        name="head",
    )(field, slab0, slab1)
    gya, gyb, head = lax.optimization_barrier((gya, gyb, head))

    half, bxa, bxb, bya, byb = call(
        halo_kernel,
        (shaped(96, 320), msg, msg, shaped(192, LANES), msg),
        [VMEM] + [VMEM] * 10,
        flops=2 * 2 * 96 * 320 * 512 * 3,
        moved=1000000,
        name="halo",
    )(odd, gxa, gxb, gya, gyb, part, ph, plo, th, tlo, given)

    ryb, rya = swap_odd(byb, "sy"), swap(bya, "sy", 1)

    own_part = call(
        last_kernel,
        shaped(96, TAIL),
        [VMEM] * 3 + [HBM],
        [pltpu.VMEM((256, 768), F32), pltpu.VMEM((256, TAIL), F32), pltpu.SemaphoreType.DMA((2,))],
        flops=2 * 2 * 96 * 256 * 256 * 12 * 3,
        moved=3000000,
        name="last",
    )(field, slab3, head, factor)
    ryb, rya, own_part = lax.optimization_barrier((ryb, rya, own_part))

    relay = jnp.where(lane >= EDGE, rya[:96] + ryb, 0.0)
    rxb, rxa = swap_odd(bxb + relay, "sx"), swap(bxa + relay, "sx", 1)

    local, sent, base = call(
        local_kernel,
        (shaped(96, own), shaped(96, 512), shaped(288, 96)),
        [VMEM] * 7,
        flops=2 * 96 * 1296 * 1100 * 3,
        moved=4000000,
        name="local",
    )(own_part, half, oh, olo, turned, sides_h, sides_l)

    away, kept, back = call(
        gram_kernel,
        (shaped(144, LANES), shaped(144, LANES), shaped(96, 512)),
        [VMEM] + [VMEM] * 10,
        flops=2 * 96 * 512 * 900 * 3,
        moved=2000000,
        name="gram",
    )(odd, rxa, rxb, rya, ryb, same, sent, rgh, rgl, base, held)

    precond = call(
        update_kernel,
        shaped(96, own),
        [VMEM] * 3,
        flops=2 * 192 * 1296 * 512,
        moved=3000000,
        name="update",
    )(back, turned, local)

    rows, cols = lax.axis_size("sx"), lax.axis_size("sy")

    def swap_apart(value, even_core, odd_core):
        route = []
        for r in range(rows):
            for c in range(cols):
                row_step, col_step = odd_core if r % 2 else even_core
                route.append((r * cols + c, (r ^ row_step) * cols + (c ^ col_step)))
        return lax.ppermute(value, ("sx", "sy"), route)

    def summed(value, even_cores, odd_cores):
        total = swap_apart(value, even_cores[0], odd_cores[0])
        for even_core, odd_core in zip(even_cores[1:], odd_cores[1:]):
            total = total + swap_apart(value, even_core, odd_core)
        return value + total

    along_y = [(2 * step, 0) for step in (1, 3, 2)]
    along_x = [(0, 8 * step) for step in (1, 3, 2)]
    total = kept + swap(away, "sx", 1)
    total = summed(total, along_y, along_x)
    total = summed(total, along_x, along_y)
    total = summed(total, [(0, 6)], [(0, 2)])
    total, precond = lax.optimization_barrier((total, precond))
    three = swap_apart(total, (0, 3), (0, 7))
    two = swap_apart(total, (0, 2), (0, 6))
    one = swap_apart(total, (0, 1), (0, 1))
    late = (total[:96] + one[:96]) + (two[:96] + three[:96])
    mine = jnp.concatenate([late, total[96:] + two[96:], one[96:] + three[96:]], axis=0)
    other = swap(mine, "sx", 1)

    vertex_total = own * lax.axis_size("sx") * lax.axis_size("sy")

    def finish(odd, *refs):
        final_kernel(1.0 / vertex_total, odd, *refs)

    gram = call(
        finish,
        shaped(288, 288),
        [VMEM] * 3,
        [pltpu.VMEM((288, 288), F32), pltpu.SemaphoreType.DMA((3,))],
        flops=1000000,
        moved=700000,
        name="final",
        out_specs=HBM,
    )(odd, mine, other)
    return precond, gram


def solution(mesh):
    placed = (
        P(None, ("sx", "sy")),
        P(None, ("sx", "sy")),
        P(None, ("sx", "sy")),
        P("sx", "sy", None, None),
        P("sx", "sy", None, None),
        P("sx", "sy", None),
    )
    return jax.shard_map(
        body, mesh=mesh, in_specs=placed, out_specs=(P(None, ("sx", "sy")), P()), check_vma=False
    )
```
